128 devices in a mesh: gx: 8 (over z, core), gy: 16 (over y, x).
Axes of the slice: x: 4, y: 4, z: 4, core: 2. Of those that a mesh axis runs over, the one named last changes fastest.
Arguments:
- cotangent: float32 [6, 256, 256, 128], P(None, 'gx', 'gy'), may hold values from -3000 to 3000
- diffusion: float32 [256, 256, 128], P('gx', 'gy'), may hold values from 50 to 2000
- phase: int32 [256, 256, 128], P('gx', 'gy'), may hold values 0 or 1
- courant: float32 [3, 256, 256, 128], P(None, 'gx', 'gy'), may hold values from 0.02 to 0.3
- upwind: int32 [3, 256, 256, 128], P(None, 'gx', 'gy'), may hold values 0 or 1
Outputs:
- grad: float32 [6, 256, 256, 128], P(None, 'gx', 'gy')
The draws below stay inside these ranges and needn't reach their ends.
All inputs are finite; a program needn't handle non-finite values. No bound on the sum of `phase` or of `upwind` on one device may be relied on, other than what follows from the above.
Results may differ from the reference program's by a relative error of at most 0.00019.
Values sent between devices are 32-bit elements; how exact they have to be, the bound alone decides.
A program may use at most 128 MiB of HBM per device.

```python
import math
import jax
import jax.numpy as jnp
from jax import lax

COMPS = 6
NX = 256
NY = 256
NZ = 128


def draw_cotangent(key, part):
    key = jax.random.fold_in(key, 11)
    shape = (COMPS, NX, NY, NZ)
    return jax.random.truncated_normal(key, -6.0, 6.0, shape, jnp.float32) * 500.0


def place_ends(values, own_key, least, high):
    place = [jax.random.randint(jax.random.fold_in(own_key, axis), (), 0, length) for axis, length in enumerate(values.shape)]
    main_axis = values.shape.index(max(values.shape))
    next_to = place[:main_axis] + [(place[main_axis] + 1) % values.shape[main_axis]] + place[main_axis + 1:]
    return values.at[tuple(place)].set(least).at[tuple(next_to)].set(high)


def levels(key, shape, shards, smallest, largest):
    def one(dim, blocks):
        steps = jax.random.uniform(jax.random.fold_in(jax.random.fold_in(key, 6), dim), (blocks,), jnp.float32, smallest / len(shards), largest / len(shards))
        return jnp.repeat(jnp.exp(steps), shape[dim] // blocks).reshape((-1,) + (1,) * (len(shape) - dim - 1))

    gain = one(*shards[0])
    for cut in shards[1:]:
        gain = gain * one(*cut)
    return gain


def setup_inputs(seed: int = 0) -> dict:
    arg_keys = jax.random.split(jax.random.key(seed), 6)
    cotangent = draw_cotangent(jax.random.fold_in(arg_keys[5], 71), 0)
    diffusion = jnp.clip(jnp.exp(math.log(2000.0) - 3.6888795 * jax.random.uniform(arg_keys[1], (NX, NY, NZ), jnp.float32) ** levels(arg_keys[1], (NX, NY, NZ), ((0, 8), (1, 16)), -0.2, 0.2)), 50.0, 2000.0)
    phase = place_ends((jax.random.randint(arg_keys[2], (NX, NY, NZ), 0, 4) < 1).astype(jnp.int32), jax.random.fold_in(arg_keys[2], 1), 0, 1)
    courant = jnp.clip(jnp.exp(math.log(0.3) - 2.7080503 * jax.random.uniform(arg_keys[3], (3, NX, NY, NZ), jnp.float32) ** levels(arg_keys[3], (3, NX, NY, NZ), ((1, 8), (2, 16)), -0.2, 0.2)), 0.02, 0.3)
    upwind = place_ends((jax.random.randint(arg_keys[4], (3, NX, NY, NZ), 0, 2) < 1).astype(jnp.int32), jax.random.fold_in(arg_keys[4], 1), 0, 1)
    return {"cotangent": cotangent, "diffusion": diffusion, "phase": phase, "courant": courant, "upwind": upwind}


def tridiag_solve(diag, rhs):
    def forward(carry, entry):
        carry_c, carry_d = carry
        diag_row, rhs_row = entry
        denom = diag_row + carry_c
        new_c = -1.0 / denom
        new_d = (rhs_row + carry_d) / denom[None]
        return (new_c, new_d), (new_c, new_d)

    start = (jnp.zeros(diag.shape[1:], diag.dtype), jnp.zeros(rhs.shape[1:], rhs.dtype))
    ending, sweeps = lax.scan(forward, start, (diag, rhs))

    def backward(later, entry):
        sweep_c, sweep_d = entry
        current = sweep_d - sweep_c[None] * later
        return current, current

    ending, solved = lax.scan(backward, jnp.zeros(rhs.shape[1:], rhs.dtype), sweeps, reverse=True)
    return solved


def line_solve(field, coeff, axis):
    moved = jnp.moveaxis(field, axis + 1, 0)
    scales = jnp.moveaxis(coeff, axis, 0)
    solved = tridiag_solve(2.0 + 1.0 / scales, moved)
    return jnp.moveaxis(solved / scales[:, None], 0, axis + 1)


def next_along(array, dim):
    extent = array.shape[dim]
    zero_face = jnp.zeros_like(lax.slice_in_dim(array, 0, 1, axis=dim))
    return jnp.concatenate([lax.slice_in_dim(array, 1, extent, axis=dim), zero_face], axis=dim)


def prev_along(array, dim):
    extent = array.shape[dim]
    zero_face = jnp.zeros_like(lax.slice_in_dim(array, 0, 1, axis=dim))
    return jnp.concatenate([zero_face, lax.slice_in_dim(array, 0, extent - 1, axis=dim)], axis=dim)


def adjoint_advect(field, courant, upwind):
    result = field
    for direction in range(3):
        flux = courant[direction][None] * field
        ahead = upwind[direction].astype(field.dtype)[None] * flux
        behind = flux - ahead
        result = result - ahead + behind + next_along(ahead, direction + 1) - prev_along(behind, direction + 1)
    return result


def reference(cotangent, diffusion, phase, courant, upwind):
    coeff = diffusion * (1.0 + 3.0 * phase.astype(diffusion.dtype))
    along_z = line_solve(cotangent, coeff, 2)
    along_y = line_solve(along_z, coeff, 1)
    along_x = line_solve(along_y, coeff, 0)
    return adjoint_advect(along_x, courant, upwind)
```

```python
import functools

import jax
import jax.numpy as jnp
from jax import lax
from jax.experimental import pallas as pl
from jax.experimental.pallas import tpu as pltpu
from jax.sharding import PartitionSpec as P

MESH = pl.DeviceIdType.MESH
C, X, Y, Z = 6, 32, 16, 128
NI, NJ = 8, 16
LINES = X * Y
PAD = 24
PLANES = X + 2
PITCH = PLANES * PAD + 8
HALF = C * 2
PACK = 2 * HALF
f32 = jnp.float32


def split(values):
    high = values.astype(jnp.bfloat16)
    low = (values - high.astype(f32)).astype(jnp.bfloat16)
    return jnp.concatenate([high, low], axis=1)


def body(
    cot_h, dif_h, pha_h, cou_h, upw_h, out_h,
    cot, dif, pha, cou, upw, ec,
    zt, zw, zo, zb, tri,
    yb, ya, yw, yo, yr, yf, ay, ayh,
    xe, xb, xa, xw, xo, xr,
    csy, csx, rcy, rcx, ky, kx, gl,
    sty, tty, oty, rty, stx, ttx, otx, rtx, ext,
    fsy, fry, fsx, frx,
    c0, ax, bx, ayp, byp, azn, bzp, fb,
    in_sem, out_sem,
    s_cy, r_cy, s_cx, r_cx, s_fy, r_fy, s_fx, r_fx,
    s_ty, r_ty, s_oy, r_oy, s_tx, r_tx, s_ox, r_ox, s_ex, r_ex,
):
    i = lax.axis_index("gx")
    j = lax.axis_index("gy")
    inext, iprev = lax.rem(i + 1, NI), lax.rem(i + NI - 1, NI)
    jnext, jprev = lax.rem(j + 1, NJ), lax.rem(j + NJ - 1, NJ)

    loads = [
        pltpu.make_async_copy(dif_h, dif, in_sem.at[0]),
        pltpu.make_async_copy(pha_h, pha, in_sem.at[1]),
        pltpu.make_async_copy(cot_h, cot, in_sem.at[2]),
        pltpu.make_async_copy(cou_h, cou, in_sem.at[3]),
        pltpu.make_async_copy(upw_h, upw, in_sem.at[4]),
    ]
    for load in loads:
        load.start()

    barrier = pltpu.get_barrier_semaphore()

    def greet_y(d, _):
        pl.semaphore_signal(barrier, inc=1, device_id=(i, lax.rem(j + d, NJ)), device_id_type=MESH)
        return 0

    def greet_x(d, _):
        pl.semaphore_signal(barrier, inc=1, device_id=(lax.rem(i + d, NI), j), device_id_type=MESH)
        return 0

    lax.fori_loop(1, NJ, greet_y, 0)
    lax.fori_loop(1, NI, greet_x, 0)

    @pl.when(i != 0)
    def _():
        pl.semaphore_signal(barrier, inc=1, device_id=(0, jnext), device_id_type=MESH)

    @pl.when(i != NI - 1)
    def _():
        pl.semaphore_signal(barrier, inc=1, device_id=(NI - 1, jprev), device_id_type=MESH)

    loads[0].wait()
    loads[1].wait()
    ec[...] = 1.0 / (dif[...] * (1.0 + 3.0 * pha[...].astype(f32)))

    for q in range(X // 8):
        xs = pl.ds(q * 8, 8)
        cells = [ec[pl.ds(q * 8 * Y + y, 8, stride=Y), :] for y in range(Y)]
        theta = jnp.ones((8, Z), f32)
        delta = jnp.ones((8, Z), f32)
        for y in range(Y):
            yb[y, xs, :] = theta
            delta = delta + cells[y] * theta
            theta = theta + delta
        rn = 1.0 / theta
        yr[xs, :] = rn
        phi = jnp.ones((8, Z), f32)
        delta = jnp.ones((8, Z), f32)
        after = jnp.ones((8, Z), f32)
        at = (q % 2) * 8 * 8 + q // 2
        for y in range(Y - 1, -1, -1):
            a = phi * rn
            b = yb[y, xs, :] * rn
            ya[y, xs, :] = a
            yb[y, xs, :] = b
            yw[y, xs, :] = 1.0 / (b * after)
            yo[y, xs, :] = b * cells[y]
            if y == Y - 1:
                csy[pl.ds(at + 4, 8, stride=8), :] = b
            if y == 0:
                csy[pl.ds(at, 8, stride=8), :] = a
            after = b
            delta = delta + cells[y] * phi
            phi = phi + delta
        csy[pl.ds(at + 2, 8, stride=8), :] = rn

    def x_factor(lo):
        rows = pl.ds(lo, 16)
        one = jnp.ones((16, Z), f32)

        def up(x, carry):
            theta, delta = carry
            xb[x, rows, :] = theta
            delta = delta + xe[x, rows, :] * theta
            return theta + delta, delta

        theta, _ = lax.fori_loop(0, X, up, (one, one), unroll=8)
        rn = 1.0 / theta
        xr[rows, :] = rn

        def down(step, carry):
            x = X - 1 - step
            phi, delta, after, _ = carry
            cell = xe[x, rows, :]
            a = phi * rn
            b = xb[x, rows, :] * rn
            xa[x, rows, :] = a
            xb[x, rows, :] = b
            xw[x, rows, :] = 1.0 / (b * after)
            xo[x, rows, :] = b * cell
            delta = delta + cell * phi
            return phi + delta, delta, b, a

        _, _, _, first = lax.fori_loop(0, X, down, (one, one, one, one), unroll=8)
        return first, rn

    for x in range(X):
        xe[x, 0:Y, :] = ec[x * Y : (x + 1) * Y, :]
    first, rn = x_factor(0)
    last = xb[X - 1, 0:Y, :]
    for r in range(2):
        csx[pl.ds(r, 8, stride=8), :] = first[r * 8 : r * 8 + 8]
        csx[pl.ds(2 + r, 8, stride=8), :] = rn[r * 8 : r * 8 + 8]
        csx[pl.ds(4 + r, 8, stride=8), :] = last[r * 8 : r * 8 + 8]

    loads[3].wait()
    loads[4].wait()
    fsy[0, 0] = ec[pl.ds(0, X, stride=Y), :]
    fsy[1, 0] = ec[pl.ds(Y - 1, X, stride=Y), :]
    fsy[0, 1] = upw[1, pl.ds(0, X, stride=Y), :].astype(f32) * cou[1, pl.ds(0, X, stride=Y), :]
    fsy[1, 1] = (1.0 - upw[1, pl.ds(Y - 1, X, stride=Y), :].astype(f32)) * cou[1, pl.ds(Y - 1, X, stride=Y), :]
    fsx[0] = upw[0, 0:Y, :].astype(f32) * cou[0, 0:Y, :] * ec[0:Y, :]
    fsx[1] = (1.0 - upw[0, LINES - Y : LINES, :].astype(f32)) * cou[0, LINES - Y : LINES, :] * ec[LINES - Y : LINES, :]

    outer = (i == 0) | (i == NI - 1)
    pl.semaphore_wait(barrier, NI + NJ - 2 + jnp.where(outer, NI - 1, 0))

    def exchange(src, dst, send, recv, rows, k, axis):
        here = j if axis == "gy" else i
        return pltpu.make_async_remote_copy(
            src_ref=src.at[pl.ds(pl.multiple_of(k * rows, 8), rows), :],
            dst_ref=dst.at[pl.ds(pl.multiple_of(here * rows, 8), rows), :],
            send_sem=send.at[k],
            recv_sem=recv.at[here],
            device_id={axis: k},
            device_id_type=MESH,
        )

    def arrival(src, dst, send, recv, rows, k, axis):
        return pltpu.make_async_remote_copy(
            src_ref=src.at[pl.ds(pl.multiple_of(k * rows, 8), rows), :],
            dst_ref=dst.at[pl.ds(pl.multiple_of(k * rows, 8), rows), :],
            send_sem=send.at[k],
            recv_sem=recv.at[k],
            device_id={axis: k},
            device_id_type=MESH,
        )

    def count_of(axis):
        return NJ if axis == "gy" else NI

    def send_all(src, dst, send, recv, rows, axis):
        n = count_of(axis)
        here = j if axis == "gy" else i
        mine = pl.ds(pl.multiple_of(here * rows, 8), rows)

        def step(d, _):
            exchange(src, dst, send, recv, rows, lax.rem(here + d, n), axis).start()
            return 0

        lax.fori_loop(1, n, step, 0)
        dst[mine, :] = src[mine, :]

    def recv_all(src, dst, send, recv, rows, axis):
        n = count_of(axis)
        here = j if axis == "gy" else i

        def step(d, _):
            arrival(src, dst, send, recv, rows, lax.rem(here + d, n), axis).wait_recv()
            return 0

        lax.fori_loop(1, n, step, 0)

    def sent_all(src, dst, send, recv, rows, axis):
        n = count_of(axis)
        here = j if axis == "gy" else i

        def step(d, _):
            arrival(src, dst, send, recv, rows, lax.rem(here + d, n), axis).wait_send()
            return 0

        lax.fori_loop(1, n, step, 0)

    coup_y = (csy, rcy, s_cy, r_cy, 8, "gy")
    coup_x = (csx, rcx, s_cx, r_cx, 8, "gx")
    tot_y = (sty, tty, s_ty, r_ty, PACK, "gy")
    ret_y = (oty, rty, s_oy, r_oy, PACK, "gy")
    tot_x = (stx, ttx, s_tx, r_tx, PACK, "gx")
    ret_x = (otx, rtx, s_ox, r_ox, PACK, "gx")

    def face(src, dst, send, recv, slot, axis, to):
        return pltpu.make_async_remote_copy(
            src_ref=src.at[slot], dst_ref=dst.at[slot], send_sem=send.at[slot], recv_sem=recv.at[slot],
            device_id={axis: to}, device_id_type=MESH,
        )

    faces = [
        face(fsy, fry, s_fy, r_fy, 0, "gy", jprev),
        face(fsy, fry, s_fy, r_fy, 1, "gy", jnext),
        face(fsx, frx, s_fx, r_fx, 0, "gx", iprev),
        face(fsx, frx, s_fx, r_fx, 1, "gx", inext),
    ]
    send_all(*coup_y)
    send_all(*coup_x)
    for f in faces:
        f.start()

    lane = lax.broadcasted_iota(jnp.int32, (64, Z), 1)

    def z_factor(block, _):
        rows = pl.ds(pl.multiple_of(block * 64, 64), 64)
        e = ec[rows, :]
        p11, p12, p21, p22 = 1.0 + e, jnp.ones_like(e), e, jnp.ones_like(e)
        step = 1
        while step < Z:
            keep = lane < step
            q11 = jnp.where(keep, 1.0, pltpu.roll(p11, step, 1))
            q12 = jnp.where(keep, 0.0, pltpu.roll(p12, step, 1))
            q21 = jnp.where(keep, 0.0, pltpu.roll(p21, step, 1))
            q22 = jnp.where(keep, 1.0, pltpu.roll(p22, step, 1))
            p11, p12, p21, p22 = (
                p11 * q11 + p12 * q21,
                p11 * q12 + p12 * q22,
                p21 * q11 + p22 * q21,
                p21 * q12 + p22 * q22,
            )
            step *= 2
        theta = p11 + p12
        before = jnp.where(lane < 1, 1.0, pltpu.roll(theta, 1, 1))
        zt[rows, :] = before
        zw[rows, :] = 1.0 / (theta * before)
        zo[rows, :] = before * e
        return 0

    lax.fori_loop(0, LINES // 64, z_factor, 0)

    row = lax.rem(lax.broadcasted_iota(jnp.int32, (2 * Z, Z), 0), Z)
    col = lax.broadcasted_iota(jnp.int32, (2 * Z, Z), 1)
    tri[0] = (row <= col).astype(f32).astype(jnp.bfloat16)
    tri[1] = (row >= col).astype(f32).astype(jnp.bfloat16)

    loads[2].wait()

    def z_and_y(q):
        rows = pl.ds(q * 8 * Y, 8 * Y)
        scale, weight, finish = zt[rows, :], zw[rows, :], zo[rows, :]
        sums = [
            jnp.dot(split(cot[c, rows, :] * scale), tri[0], preferred_element_type=f32) for c in range(C)
        ]
        for c in range(C):
            whole = jnp.dot(split(sums[c] * weight), tri[1], preferred_element_type=f32)
            zb[c, rows, :] = whole * finish
        xs = pl.ds(q * 8, 8)
        heads = [jnp.zeros((8, Z), f32) for _ in range(C)]
        tails = [jnp.zeros((8, Z), f32) for _ in range(C)]
        for y in range(Y):
            a, b = ya[y, xs, :], yb[y, xs, :]
            for c in range(C):
                value = zb[c, pl.ds(q * 8 * Y + y, 8, stride=Y), :]
                heads[c] = heads[c] + a * value
                tails[c] = tails[c] + b * value
                yf[c, y, xs, :] = tails[c]
        at = (q % 2) * 8 * PACK + (q // 2) * C
        for c in range(C):
            sty[pl.ds(at + c, 8, stride=PACK), :] = heads[c]
            sty[pl.ds(at + HALF + c, 8, stride=PACK), :] = tails[c]

    def wave(w):
        def step(d, _):
            k = lax.rem(j + d, 8) + 8 * w

            @pl.when(k != j)
            def _():
                exchange(*tot_y[:5], k, "gy").start()

            return 0

        lax.fori_loop(0, 8, step, 0)

    z_and_y(0)
    z_and_y(2)
    wave(0)
    z_and_y(1)
    z_and_y(3)
    wave(1)
    mine_y = pl.ds(pl.multiple_of(j * PACK, 8), PACK)
    tty[mine_y, :] = sty[mine_y, :]

    def reduce_factor(count, couplings, factors):
        def pair(base, t):
            return jnp.concatenate(
                [
                    jnp.broadcast_to(couplings[pl.ds(base + 2 * t, 1), :], (C, Z)),
                    jnp.broadcast_to(couplings[pl.ds(base + 2 * t + 1, 1), :], (C, Z)),
                ],
                axis=0,
            )

        edge = jnp.zeros((HALF, Z), f32)
        for m in range(count):
            a1, b1, bn = pair(m * 8, 0), pair(m * 8, 1), pair(m * 8, 2)
            alpha = 1.0 / (1.0 - a1 * edge)
            alpha_a = a1 * alpha
            forward = b1 * alpha
            back = b1 * edge
            factors[0, m, 0:HALF, :] = alpha
            factors[1, m, 0:HALF, :] = alpha_a
            factors[2, m, 0:HALF, :] = forward
            factors[3, m, 0:HALF, :] = edge
            factors[4, m, 0:HALF, :] = back * alpha
            factors[5, m, 0:HALF, :] = b1 + back * alpha_a
            edge = bn + back * forward

    def reduce_solve(count, totals, factors, results):
        gain = jnp.zeros((HALF, Z), f32)
        for m in range(count):
            head = totals[m * PACK : m * PACK + HALF, :]
            tail = totals[m * PACK + HALF : m * PACK + PACK, :]
            gl[0, m, 0:HALF, :] = gain
            gl[1, m, 0:HALF, :] = factors[0, m, 0:HALF, :] * head + factors[1, m, 0:HALF, :] * gain
            gain = tail + factors[4, m, 0:HALF, :] * head + factors[5, m, 0:HALF, :] * gain
        later = jnp.zeros((HALF, Z), f32)
        for m in range(count - 1, -1, -1):
            results[m * PACK + HALF : m * PACK + PACK, :] = later
            later = gl[1, m, 0:HALF, :] + factors[2, m, 0:HALF, :] * later
            results[m * PACK : m * PACK + HALF, :] = gl[0, m, 0:HALF, :] + factors[3, m, 0:HALF, :] * later

    recv_all(*coup_y)
    reduce_factor(NJ, rcy, ky)

    recv_all(*tot_y)
    reduce_solve(NJ, tty, ky, oty)
    send_all(*ret_y)

    recv_all(*coup_x)
    reduce_factor(NI, rcx, kx)
    for f in faces:
        f.wait_recv()

    for x in range(X):
        xe[x, 16:24, :] = jnp.broadcast_to(fry[1, 0, x : x + 1, :], (8, Z))
        xe[x, 24:32, :] = jnp.broadcast_to(fry[0, 0, x : x + 1, :], (8, Z))
    x_factor(16)

    low_ok = jnp.where(j > 0, 1.0, 0.0).astype(f32)
    high_ok = jnp.where(j < NJ - 1, 1.0, 0.0).astype(f32)
    lane16 = lax.broadcasted_iota(jnp.int32, (Y, Z), 1)

    def coefficients(x, _):
        rows = pl.ds(pl.multiple_of(x * Y, Y), Y)
        shifted = pl.ds(pl.multiple_of(x * Y + Y, Y), Y)
        padded = pl.ds(pl.multiple_of(x * PAD + 8, 8), Y)
        flux = [cou[d, rows, :] for d in range(3)]
        ahead = [upw[d, rows, :].astype(f32) * flux[d] for d in range(3)]
        behind = [flux[d] - ahead[d] for d in range(3)]
        c0[rows, :] = 1.0 + (behind[0] - ahead[0]) + (behind[1] - ahead[1]) + (behind[2] - ahead[2])
        ax[shifted, :] = ahead[0]
        bx[shifted, :] = behind[0]
        ayp[padded, :] = ahead[1]
        byp[padded, :] = behind[1]
        azn[rows, :] = jnp.where(lane16 < Z - 1, pltpu.roll(ahead[2], Z - 1, 1), 0.0)
        bzp[rows, :] = jnp.where(lane16 > 0, pltpu.roll(behind[2], 1, 1), 0.0)
        return 0

    lax.fori_loop(0, X, coefficients, 0, unroll=2)
    bx[0:Y, :] = frx[1]
    ax[(X + 1) * Y : (X + 2) * Y, :] = frx[0]
    byp[pl.ds(7, X, stride=PAD), :] = fry[1, 1] * low_ok
    ayp[pl.ds(PAD, X, stride=PAD), :] = fry[0, 1] * high_ok
    ayh[...] = jnp.zeros_like(ayh)

    recv_all(*ret_y)

    for q in (0, 2, 1, 3):
        xs = pl.ds(q * 8, 8)
        at = (q % 2) * 8 * PACK + (q // 2) * C
        below, above, live = [], [], []
        for c in range(C):
            left = rty[pl.ds(at + c, 8, stride=PACK), :]
            right = rty[pl.ds(at + HALF + c, 8, stride=PACK), :]
            ayh[pl.ds(q * 8 * 16 + c, 8, stride=16), :] = left * fry[1, 0, xs, :]
            ayh[pl.ds(q * 8 * 16 + 8 + c, 8, stride=16), :] = right * fry[0, 0, xs, :]
            below.append(left * yr[xs, :])
            live.append(right)
        for y in range(Y - 1, -1, -1):
            weight, finish = yw[y, xs, :], yo[y, xs, :]
            for c in range(C):
                live[c] = live[c] + weight * (yf[c, y, xs, :] + below[c])
                ay[c, pl.ds(q * 8 * Y + y, 8, stride=Y), :] = live[c] * finish

    def x_totals(x, carry):
        heads, tails, halo = carry
        rows = pl.ds(pl.multiple_of(x * Y, Y), Y)
        a, b = xa[x, 0:Y, :], xb[x, 0:Y, :]
        new_heads, new_tails = [], []
        for c in range(C):
            value = ay[c, rows, :]
            new_heads.append(heads[c] + a * value)
            tail = tails[c] + b * value
            new_tails.append(tail)
            ay[c, rows, :] = tail
        halo = halo + xb[x, 16:32, :] * ayh[rows, :]
        ayh[rows, :] = halo
        return tuple(new_heads), tuple(new_tails), halo

    none = jnp.zeros((Y, Z), f32)
    heads, tails, _ = lax.fori_loop(0, X, x_totals, ((none,) * C, (none,) * C, none), unroll=2)
    for c in range(C):
        for r in range(2):
            stx[pl.ds(r * C + c, 8, stride=PACK), :] = heads[c][r * 8 : r * 8 + 8]
            stx[pl.ds(HALF + r * C + c, 8, stride=PACK), :] = tails[c][r * 8 : r * 8 + 8]
    send_all(*tot_x)
    sent_all(*coup_y)
    sent_all(*coup_x)
    sent_all(*tot_y)
    sent_all(*ret_y)
    for f in faces:
        f.wait_send()
    recv_all(*tot_x)
    reduce_solve(NI, ttx, kx, otx)
    send_all(*ret_x)

    def extra(m, slot, to):
        return pltpu.make_async_remote_copy(
            src_ref=otx.at[pl.ds(pl.multiple_of(m * PACK, 8), PACK), :],
            dst_ref=ext.at[slot, pl.ds(0, PACK), :],
            send_sem=s_ex.at[slot, m],
            recv_sem=r_ex.at[slot],
            device_id=(m, to),
            device_id_type=MESH,
        )

    @pl.when(i == 0)
    def _():
        for m in range(NI):
            extra(m, 1, jprev).start()

    @pl.when(i == NI - 1)
    def _():
        for m in range(NI):
            extra(m, 0, jnext).start()

    recv_all(*ret_x)
    extra(0, 0, jnext).wait_recv()
    extra(0, 1, jprev).wait_recv()

    lefts, rights = [], []
    for c in range(C):
        left = jnp.concatenate([rtx[pl.ds(r * C + c, 8, stride=PACK), :] for r in range(2)], axis=0)
        right = jnp.concatenate([rtx[pl.ds(HALF + r * C + c, 8, stride=PACK), :] for r in range(2)], axis=0)
        fb[pl.ds(c * PITCH + 8, Y), :] = left
        fb[pl.ds(c * PITCH + (X + 1) * PAD + 8, Y), :] = right
        lefts.append(left * xr[0:Y, :])
        rights.append(right)
    left_halo = jnp.concatenate([ext[0, 6:14, :], ext[1, 0:8, :]], axis=0) * xr[16:32, :]
    right_halo = jnp.concatenate([ext[0, 18:26, :], ext[1, 12:20, :]], axis=0)

    def x_finish(step, carry):
        x = X - 1 - step
        live, halo = carry
        rows = pl.ds(pl.multiple_of(x * Y, Y), Y)
        weight, finish = xw[x, 0:Y, :], xo[x, 0:Y, :]
        out = []
        for c in range(C):
            value = live[c] + weight * (ay[c, rows, :] + lefts[c])
            fb[pl.ds(pl.multiple_of(c * PITCH + (x + 1) * PAD + 8, 8), Y), :] = value * finish
            out.append(value)
        halo = halo + xw[x, 16:32, :] * (ayh[rows, :] + left_halo)
        edge = halo * xo[x, 16:32, :]
        fb[pl.ds((x + 1) * PAD + 7, 8, stride=PITCH), :] = edge[0:8]
        fb[pl.ds((x + 2) * PAD, 8, stride=PITCH), :] = edge[8:16]
        return tuple(out), halo

    lax.fori_loop(0, X, x_finish, (tuple(rights), right_halo), unroll=2)

    def advect(x, _):
        rows = pl.ds(pl.multiple_of(x * Y, Y), Y)
        middle = c0[rows, :]
        from_x, to_x = bx[rows, :], ax[pl.ds(pl.multiple_of((x + 2) * Y, Y), Y), :]
        from_y, to_y = byp[pl.ds(x * PAD + 7, Y), :], ayp[pl.ds(x * PAD + 9, Y), :]
        from_z, to_z = bzp[rows, :], azn[rows, :]
        for c in range(C):
            at = c * PITCH + (x + 1) * PAD + 8
            value = fb[pl.ds(pl.multiple_of(at, 8), Y), :]
            result = middle * value
            result += to_x * fb[pl.ds(pl.multiple_of(at + PAD, 8), Y), :]
            result -= from_x * fb[pl.ds(pl.multiple_of(at - PAD, 8), Y), :]
            result += to_y * fb[pl.ds(at + 1, Y), :]
            result -= from_y * fb[pl.ds(at - 1, Y), :]
            result += to_z * pltpu.roll(value, Z - 1, 1)
            result -= from_z * pltpu.roll(value, 1, 1)
            cot[c, rows, :] = result
        return 0

    stores = []
    for part in range(4):
        lax.fori_loop(part * 8, part * 8 + 8, advect, 0, unroll=2)
        rows = pl.ds(part * 8 * Y, 8 * Y)
        store = pltpu.make_async_copy(cot.at[:, rows, :], out_h.at[:, rows, :], out_sem.at[part])
        store.start()
        stores.append(store)

    sent_all(*tot_x)
    sent_all(*ret_x)

    @pl.when(i == 0)
    def _():
        for m in range(NI):
            extra(m, 1, jprev).wait_send()

    @pl.when(i == NI - 1)
    def _():
        for m in range(NI):
            extra(m, 0, jnext).wait_send()

    for store in stores:
        store.wait()


def on_device(cotangent, diffusion, phase, courant, upwind):
    def vm(*shape, dtype=f32):
        return pltpu.VMEM(shape, dtype)

    dma = pltpu.SemaphoreType.DMA
    scratch = [
        vm(C, LINES, Z), vm(LINES, Z), vm(LINES, Z, dtype=jnp.int32), vm(3, LINES, Z), vm(3, LINES, Z, dtype=jnp.int32),
        vm(LINES, Z),
        vm(LINES, Z), vm(LINES, Z), vm(LINES, Z), vm(C, LINES, Z), vm(2, 2 * Z, Z, dtype=jnp.bfloat16),
        vm(Y, X, Z), vm(Y, X, Z), vm(Y, X, Z), vm(Y, X, Z), vm(X, Z), vm(C, Y, X, Z), vm(C, LINES, Z), vm(X * 16, Z),
        vm(X, 32, Z), vm(X, 32, Z), vm(X, 32, Z), vm(X, 32, Z), vm(X, 32, Z), vm(32, Z),
        vm(NJ * 8, Z), vm(NI * 8, Z), vm(NJ * 8, Z), vm(NI * 8, Z), vm(6, NJ, 16, Z), vm(6, NI, 16, Z), vm(2, NJ, 16, Z),
        vm(NJ * PACK, Z), vm(NJ * PACK, Z), vm(NJ * PACK, Z), vm(NJ * PACK, Z),
        vm(NI * PACK, Z), vm(NI * PACK, Z), vm(NI * PACK, Z), vm(NI * PACK, Z), vm(2, 32, Z),
        vm(2, 2, X, Z), vm(2, 2, X, Z), vm(2, Y, Z), vm(2, Y, Z),
        vm(LINES, Z), vm(LINES + 2 * Y, Z), vm(LINES + 2 * Y, Z), vm(X * PAD + 8, Z), vm(X * PAD + 8, Z), vm(LINES, Z), vm(LINES, Z),
        vm(8 * PITCH, Z),
        dma((5,)), dma((4,)),
        dma((NJ,)), dma((NJ,)), dma((NI,)), dma((NI,)), dma((2,)), dma((2,)), dma((2,)), dma((2,)),
        dma((NJ,)), dma((NJ,)), dma((NJ,)), dma((NJ,)), dma((NI,)), dma((NI,)), dma((NI,)), dma((NI,)),
        dma((2, NI)), dma((2,)),
    ]
    out = pl.pallas_call(
        body,
        out_shape=jax.ShapeDtypeStruct((C, LINES, Z), f32),
        in_specs=[pl.BlockSpec(memory_space=pl.ANY)] * 5,
        out_specs=pl.BlockSpec(memory_space=pl.ANY),
        scratch_shapes=scratch,
        compiler_params=pltpu.CompilerParams(
            collective_id=0, has_side_effects=True, vmem_limit_bytes=48 * 1024 * 1024
        ),
    )(
        cotangent.reshape(C, LINES, Z),
        diffusion.reshape(LINES, Z),
        phase.reshape(LINES, Z),
        courant.reshape(3, LINES, Z),
        upwind.reshape(3, LINES, Z),
    )
    return out.reshape(C, X, Y, Z)


def solution(mesh):
    placed = (
        P(None, "gx", "gy", None),
        P("gx", "gy", None),
        P("gx", "gy", None),
        P(None, "gx", "gy", None),
        P(None, "gx", "gy", None),
    )
    return jax.shard_map(
        on_device, mesh=mesh, in_specs=placed, out_specs=P(None, "gx", "gy", None), check_vma=False
    )
```

```python
import functools

import jax
import jax.numpy as jnp
from jax import lax
from jax.experimental import pallas as pl
from jax.experimental.pallas import tpu as pltpu
from jax.sharding import PartitionSpec as P

MESH = pl.DeviceIdType.MESH
C, X, Y, Z = 6, 32, 16, 128
NI, NJ = 8, 16
LINES = X * Y
PAD = 24
PLANES = X + 2
PITCH = PLANES * PAD + 8
HALF = C * 2
PACK = 2 * HALF
f32 = jnp.float32


def split(values):
    high = values.astype(jnp.bfloat16)
    low = (values - high.astype(f32)).astype(jnp.bfloat16)
    return jnp.concatenate([high, low], axis=1)


def body(
    cot_h, dif_h, pha_h, cou_h, upw_h, out,
    cot, dif, pha, cou, upw, ec,
    et, zt, zw, zo, zb, tri,
    yb, ya, yw, yo, yr, yf, ay, ayh,
    xe, xb, xa, xw, xo, xr,
    csy, csx, rcy, rcx, ky, kx, gl,
    sty, tty, oty, rty, stx, ttx, otx, rtx, ext,
    fsy, fry, fsx, frx,
    c0, ax, bx, ayp, byp, azn, bzp, fb,
    in_sem,
    s_cy, r_cy, s_cx, r_cx, s_fy, r_fy, s_fx, r_fx,
    s_ty, r_ty, s_oy, r_oy, s_tx, r_tx, s_ox, r_ox, s_ex, r_ex,
):
    i = lax.axis_index("gx")
    j = lax.axis_index("gy")
    inext, iprev = lax.rem(i + 1, NI), lax.rem(i + NI - 1, NI)
    jnext, jprev = lax.rem(j + 1, NJ), lax.rem(j + NJ - 1, NJ)

    loads = [
        pltpu.make_async_copy(dif_h, dif, in_sem.at[0]),
        pltpu.make_async_copy(pha_h, pha, in_sem.at[1]),
        pltpu.make_async_copy(cot_h, cot, in_sem.at[2]),
        pltpu.make_async_copy(cou_h, cou, in_sem.at[3]),
        pltpu.make_async_copy(upw_h, upw, in_sem.at[4]),
    ]
    for load in loads:
        load.start()

    barrier = pltpu.get_barrier_semaphore()

    def greet_y(d, _):
        pl.semaphore_signal(barrier, inc=1, device_id=(i, lax.rem(j + d, NJ)), device_id_type=MESH)
        return 0

    def greet_x(d, _):
        pl.semaphore_signal(barrier, inc=1, device_id=(lax.rem(i + d, NI), j), device_id_type=MESH)
        return 0

    lax.fori_loop(1, NJ, greet_y, 0)
    lax.fori_loop(1, NI, greet_x, 0)

    @pl.when(i != 0)
    def _():
        pl.semaphore_signal(barrier, inc=1, device_id=(0, jnext), device_id_type=MESH)

    @pl.when(i != NI - 1)
    def _():
        pl.semaphore_signal(barrier, inc=1, device_id=(NI - 1, jprev), device_id_type=MESH)

    loads[0].wait()
    loads[1].wait()
    ec[...] = 1.0 / (dif[...] * (1.0 + 3.0 * pha[...].astype(f32)))

    for q in range(X // 8):
        xs = pl.ds(q * 8, 8)
        cells = [ec[pl.ds(q * 8 * Y + y, 8, stride=Y), :] for y in range(Y)]
        theta = jnp.ones((8, Z), f32)
        delta = jnp.ones((8, Z), f32)
        for y in range(Y):
            yb[y, xs, :] = theta
            delta = delta + cells[y] * theta
            theta = theta + delta
        rn = 1.0 / theta
        yr[xs, :] = rn
        phi = jnp.ones((8, Z), f32)
        delta = jnp.ones((8, Z), f32)
        after = jnp.ones((8, Z), f32)
        at = (q % 2) * 8 * 8 + q // 2
        for y in range(Y - 1, -1, -1):
            a = phi * rn
            b = yb[y, xs, :] * rn
            ya[y, xs, :] = a
            yb[y, xs, :] = b
            yw[y, xs, :] = 1.0 / (b * after)
            yo[y, xs, :] = b * cells[y]
            if y == Y - 1:
                csy[pl.ds(at + 4, 8, stride=8), :] = b
            if y == 0:
                csy[pl.ds(at, 8, stride=8), :] = a
            after = b
            delta = delta + cells[y] * phi
            phi = phi + delta
        csy[pl.ds(at + 2, 8, stride=8), :] = rn

    def x_factor(lo):
        rows = pl.ds(lo, 16)
        one = jnp.ones((16, Z), f32)

        def up(x, carry):
            theta, delta = carry
            xb[x, rows, :] = theta
            delta = delta + xe[x, rows, :] * theta
            return theta + delta, delta

        theta, _ = lax.fori_loop(0, X, up, (one, one), unroll=8)
        rn = 1.0 / theta
        xr[rows, :] = rn

        def down(step, carry):
            x = X - 1 - step
            phi, delta, after, _ = carry
            cell = xe[x, rows, :]
            a = phi * rn
            b = xb[x, rows, :] * rn
            xa[x, rows, :] = a
            xb[x, rows, :] = b
            xw[x, rows, :] = 1.0 / (b * after)
            xo[x, rows, :] = b * cell
            delta = delta + cell * phi
            return phi + delta, delta, b, a

        _, _, _, first = lax.fori_loop(0, X, down, (one, one, one, one), unroll=8)
        return first, rn

    for x in range(X):
        xe[x, 0:Y, :] = ec[x * Y : (x + 1) * Y, :]
    first, rn = x_factor(0)
    last = xb[X - 1, 0:Y, :]
    for r in range(2):
        csx[pl.ds(r, 8, stride=8), :] = first[r * 8 : r * 8 + 8]
        csx[pl.ds(2 + r, 8, stride=8), :] = rn[r * 8 : r * 8 + 8]
        csx[pl.ds(4 + r, 8, stride=8), :] = last[r * 8 : r * 8 + 8]

    loads[3].wait()
    loads[4].wait()
    fsy[0, 0] = ec[pl.ds(0, X, stride=Y), :]
    fsy[1, 0] = ec[pl.ds(Y - 1, X, stride=Y), :]
    fsy[0, 1] = upw[1, pl.ds(0, X, stride=Y), :].astype(f32) * cou[1, pl.ds(0, X, stride=Y), :]
    fsy[1, 1] = (1.0 - upw[1, pl.ds(Y - 1, X, stride=Y), :].astype(f32)) * cou[1, pl.ds(Y - 1, X, stride=Y), :]
    fsx[0] = upw[0, 0:Y, :].astype(f32) * cou[0, 0:Y, :] * ec[0:Y, :]
    fsx[1] = (1.0 - upw[0, LINES - Y : LINES, :].astype(f32)) * cou[0, LINES - Y : LINES, :] * ec[LINES - Y : LINES, :]

    outer = (i == 0) | (i == NI - 1)
    pl.semaphore_wait(barrier, NI + NJ - 2 + jnp.where(outer, NI - 1, 0))

    def exchange(src, dst, send, recv, rows, k, axis):
        here = j if axis == "gy" else i
        return pltpu.make_async_remote_copy(
            src_ref=src.at[pl.ds(pl.multiple_of(k * rows, 8), rows), :],
            dst_ref=dst.at[pl.ds(pl.multiple_of(here * rows, 8), rows), :],
            send_sem=send.at[k],
            recv_sem=recv.at[here],
            device_id={axis: k},
            device_id_type=MESH,
        )

    def arrival(src, dst, send, recv, rows, k, axis):
        return pltpu.make_async_remote_copy(
            src_ref=src.at[pl.ds(pl.multiple_of(k * rows, 8), rows), :],
            dst_ref=dst.at[pl.ds(pl.multiple_of(k * rows, 8), rows), :],
            send_sem=send.at[k],
            recv_sem=recv.at[k],
            device_id={axis: k},
            device_id_type=MESH,
        )

    def count_of(axis):
        return NJ if axis == "gy" else NI

    def send_all(src, dst, send, recv, rows, axis):
        n = count_of(axis)
        here = j if axis == "gy" else i
        mine = pl.ds(pl.multiple_of(here * rows, 8), rows)

        def step(d, _):
            exchange(src, dst, send, recv, rows, lax.rem(here + d, n), axis).start()
            return 0

        lax.fori_loop(1, n, step, 0)
        dst[mine, :] = src[mine, :]

    def recv_all(src, dst, send, recv, rows, axis):
        n = count_of(axis)
        here = j if axis == "gy" else i

        def step(d, _):
            arrival(src, dst, send, recv, rows, lax.rem(here + d, n), axis).wait_recv()
            return 0

        lax.fori_loop(1, n, step, 0)

    def sent_all(src, dst, send, recv, rows, axis):
        n = count_of(axis)
        here = j if axis == "gy" else i

        def step(d, _):
            arrival(src, dst, send, recv, rows, lax.rem(here + d, n), axis).wait_send()
            return 0

        lax.fori_loop(1, n, step, 0)

    coup_y = (csy, rcy, s_cy, r_cy, 8, "gy")
    coup_x = (csx, rcx, s_cx, r_cx, 8, "gx")
    tot_y = (sty, tty, s_ty, r_ty, PACK, "gy")
    ret_y = (oty, rty, s_oy, r_oy, PACK, "gy")
    tot_x = (stx, ttx, s_tx, r_tx, PACK, "gx")
    ret_x = (otx, rtx, s_ox, r_ox, PACK, "gx")

    def face(src, dst, send, recv, slot, axis, to):
        return pltpu.make_async_remote_copy(
            src_ref=src.at[slot], dst_ref=dst.at[slot], send_sem=send.at[slot], recv_sem=recv.at[slot],
            device_id={axis: to}, device_id_type=MESH,
        )

    faces = [
        face(fsy, fry, s_fy, r_fy, 0, "gy", jprev),
        face(fsy, fry, s_fy, r_fy, 1, "gy", jnext),
        face(fsx, frx, s_fx, r_fx, 0, "gx", iprev),
        face(fsx, frx, s_fx, r_fx, 1, "gx", inext),
    ]
    send_all(*coup_y)
    send_all(*coup_x)
    for f in faces:
        f.start()

    seg = lax.broadcasted_iota(jnp.int32, (8, Z), 0)
    span = Z // 8
    tiles = LINES // Z
    for t in range(tiles):
        et[t] = ec[t * Z : (t + 1) * Z, :].T
    ones = jnp.ones((8, Z), f32)
    zeros = jnp.zeros((8, Z), f32)

    def cell(t, step):
        return et[t, pl.ds(step, 8, stride=span), :]

    starts = []
    for t in range(tiles):
        p11, p12, p21, p22 = ones, zeros, zeros, ones
        for step in range(span):
            e = cell(t, step)
            p21 = p21 + e * p11
            p22 = p22 + e * p12
            p11 = p11 + p21
            p12 = p12 + p22
        for shift in (1, 2, 4):
            keep = seg < shift
            q11 = jnp.where(keep, 1.0, pltpu.roll(p11, shift, 0))
            q12 = jnp.where(keep, 0.0, pltpu.roll(p12, shift, 0))
            q21 = jnp.where(keep, 0.0, pltpu.roll(p21, shift, 0))
            q22 = jnp.where(keep, 1.0, pltpu.roll(p22, shift, 0))
            p11, p12, p21, p22 = (
                p11 * q11 + p12 * q21,
                p11 * q12 + p12 * q22,
                p21 * q11 + p22 * q21,
                p21 * q12 + p22 * q22,
            )
        theta = jnp.where(seg < 1, 1.0, pltpu.roll(p11 + p12, 1, 0))
        delta = jnp.where(seg < 1, 1.0, pltpu.roll(p21 + p22, 1, 0))
        starts.append((theta, delta))
    for t in range(tiles):
        theta, delta = starts[t]
        for step in range(span):
            delta = delta + cell(t, step) * theta
            theta = theta + delta
            et[t, pl.ds(step, 8, stride=span), :] = theta
    lane = lax.broadcasted_iota(jnp.int32, (Z, Z), 1)
    for t in range(tiles):
        rows = pl.ds(t * Z, Z)
        theta = et[t].T
        before = jnp.where(lane < 1, 1.0, pltpu.roll(theta, 1, 1))
        zt[rows, :] = before
        zw[rows, :] = 1.0 / (theta * before)
        zo[rows, :] = before * ec[rows, :]

    row = lax.rem(lax.broadcasted_iota(jnp.int32, (2 * Z, Z), 0), Z)
    col = lax.broadcasted_iota(jnp.int32, (2 * Z, Z), 1)
    tri[0] = (row <= col).astype(f32).astype(jnp.bfloat16)
    tri[1] = (row >= col).astype(f32).astype(jnp.bfloat16)

    loads[2].wait()

    def z_and_y(q):
        rows = pl.ds(q * 8 * Y, 8 * Y)
        scale, weight, finish = zt[rows, :], zw[rows, :], zo[rows, :]
        sums = [
            jnp.dot(split(cot[c, rows, :] * scale), tri[0], preferred_element_type=f32) for c in range(C)
        ]
        for c in range(C):
            whole = jnp.dot(split(sums[c] * weight), tri[1], preferred_element_type=f32)
            zb[c, rows, :] = whole * finish
        xs = pl.ds(q * 8, 8)
        heads = [jnp.zeros((8, Z), f32) for _ in range(C)]
        tails = [jnp.zeros((8, Z), f32) for _ in range(C)]
        for y in range(Y):
            a, b = ya[y, xs, :], yb[y, xs, :]
            for c in range(C):
                value = zb[c, pl.ds(q * 8 * Y + y, 8, stride=Y), :]
                heads[c] = heads[c] + a * value
                tails[c] = tails[c] + b * value
                yf[c, y, xs, :] = tails[c]
        at = (q % 2) * 8 * PACK + (q // 2) * C
        for c in range(C):
            sty[pl.ds(at + c, 8, stride=PACK), :] = heads[c]
            sty[pl.ds(at + HALF + c, 8, stride=PACK), :] = tails[c]

    def wave(w):
        def step(d, _):
            k = lax.rem(j + d, 8) + 8 * w

            @pl.when(k != j)
            def _():
                exchange(*tot_y[:5], k, "gy").start()

            return 0

        lax.fori_loop(0, 8, step, 0)

    z_and_y(0)
    z_and_y(2)
    wave(0)
    z_and_y(1)
    z_and_y(3)
    wave(1)
    mine_y = pl.ds(pl.multiple_of(j * PACK, 8), PACK)
    tty[mine_y, :] = sty[mine_y, :]

    def reduce_factor(count, couplings, factors):
        def pair(base, t):
            return jnp.concatenate(
                [
                    jnp.broadcast_to(couplings[pl.ds(base + 2 * t, 1), :], (C, Z)),
                    jnp.broadcast_to(couplings[pl.ds(base + 2 * t + 1, 1), :], (C, Z)),
                ],
                axis=0,
            )

        edge = jnp.zeros((HALF, Z), f32)
        for m in range(count):
            a1, b1, bn = pair(m * 8, 0), pair(m * 8, 1), pair(m * 8, 2)
            alpha = 1.0 / (1.0 - a1 * edge)
            alpha_a = a1 * alpha
            forward = b1 * alpha
            back = b1 * edge
            factors[0, m, 0:HALF, :] = alpha
            factors[1, m, 0:HALF, :] = alpha_a
            factors[2, m, 0:HALF, :] = forward
            factors[3, m, 0:HALF, :] = edge
            factors[4, m, 0:HALF, :] = back * alpha
            factors[5, m, 0:HALF, :] = b1 + back * alpha_a
            edge = bn + back * forward

    def reduce_solve(count, totals, factors, results):
        gain = jnp.zeros((HALF, Z), f32)
        for m in range(count):
            head = totals[m * PACK : m * PACK + HALF, :]
            tail = totals[m * PACK + HALF : m * PACK + PACK, :]
            gl[0, m, 0:HALF, :] = gain
            gl[1, m, 0:HALF, :] = factors[0, m, 0:HALF, :] * head + factors[1, m, 0:HALF, :] * gain
            gain = tail + factors[4, m, 0:HALF, :] * head + factors[5, m, 0:HALF, :] * gain
        later = jnp.zeros((HALF, Z), f32)
        for m in range(count - 1, -1, -1):
            results[m * PACK + HALF : m * PACK + PACK, :] = later
            later = gl[1, m, 0:HALF, :] + factors[2, m, 0:HALF, :] * later
            results[m * PACK : m * PACK + HALF, :] = gl[0, m, 0:HALF, :] + factors[3, m, 0:HALF, :] * later

    recv_all(*coup_y)
    reduce_factor(NJ, rcy, ky)

    recv_all(*tot_y)
    reduce_solve(NJ, tty, ky, oty)
    send_all(*ret_y)

    recv_all(*coup_x)
    reduce_factor(NI, rcx, kx)
    for f in faces:
        f.wait_recv()

    for x in range(X):
        xe[x, 16:24, :] = jnp.broadcast_to(fry[1, 0, x : x + 1, :], (8, Z))
        xe[x, 24:32, :] = jnp.broadcast_to(fry[0, 0, x : x + 1, :], (8, Z))
    x_factor(16)

    low_ok = jnp.where(j > 0, 1.0, 0.0).astype(f32)
    high_ok = jnp.where(j < NJ - 1, 1.0, 0.0).astype(f32)
    lane16 = lax.broadcasted_iota(jnp.int32, (Y, Z), 1)

    def coefficients(x, _):
        rows = pl.ds(pl.multiple_of(x * Y, Y), Y)
        shifted = pl.ds(pl.multiple_of(x * Y + Y, Y), Y)
        padded = pl.ds(pl.multiple_of(x * PAD + 8, 8), Y)
        flux = [cou[d, rows, :] for d in range(3)]
        ahead = [upw[d, rows, :].astype(f32) * flux[d] for d in range(3)]
        behind = [flux[d] - ahead[d] for d in range(3)]
        c0[rows, :] = 1.0 + (behind[0] - ahead[0]) + (behind[1] - ahead[1]) + (behind[2] - ahead[2])
        ax[shifted, :] = ahead[0]
        bx[shifted, :] = behind[0]
        ayp[padded, :] = ahead[1]
        byp[padded, :] = behind[1]
        azn[rows, :] = jnp.where(lane16 < Z - 1, pltpu.roll(ahead[2], Z - 1, 1), 0.0)
        bzp[rows, :] = jnp.where(lane16 > 0, pltpu.roll(behind[2], 1, 1), 0.0)
        return 0

    lax.fori_loop(0, X, coefficients, 0, unroll=2)
    bx[0:Y, :] = frx[1]
    ax[(X + 1) * Y : (X + 2) * Y, :] = frx[0]
    byp[pl.ds(7, X, stride=PAD), :] = fry[1, 1] * low_ok
    ayp[pl.ds(PAD, X, stride=PAD), :] = fry[0, 1] * high_ok
    ayh[...] = jnp.zeros_like(ayh)

    recv_all(*ret_y)

    for q in (0, 2, 1, 3):
        xs = pl.ds(q * 8, 8)
        at = (q % 2) * 8 * PACK + (q // 2) * C
        below, above, live = [], [], []
        for c in range(C):
            left = rty[pl.ds(at + c, 8, stride=PACK), :]
            right = rty[pl.ds(at + HALF + c, 8, stride=PACK), :]
            ayh[pl.ds(q * 8 * 16 + c, 8, stride=16), :] = left * fry[1, 0, xs, :]
            ayh[pl.ds(q * 8 * 16 + 8 + c, 8, stride=16), :] = right * fry[0, 0, xs, :]
            below.append(left * yr[xs, :])
            live.append(right)
        for y in range(Y - 1, -1, -1):
            weight, finish = yw[y, xs, :], yo[y, xs, :]
            for c in range(C):
                live[c] = live[c] + weight * (yf[c, y, xs, :] + below[c])
                ay[c, pl.ds(q * 8 * Y + y, 8, stride=Y), :] = live[c] * finish

    def x_totals(x, carry):
        heads, tails, halo = carry
        rows = pl.ds(pl.multiple_of(x * Y, Y), Y)
        a, b = xa[x, 0:Y, :], xb[x, 0:Y, :]
        new_heads, new_tails = [], []
        for c in range(C):
            value = ay[c, rows, :]
            new_heads.append(heads[c] + a * value)
            tail = tails[c] + b * value
            new_tails.append(tail)
            ay[c, rows, :] = tail
        halo = halo + xb[x, 16:32, :] * ayh[rows, :]
        ayh[rows, :] = halo
        return tuple(new_heads), tuple(new_tails), halo

    none = jnp.zeros((Y, Z), f32)
    heads, tails, _ = lax.fori_loop(0, X, x_totals, ((none,) * C, (none,) * C, none), unroll=2)
    for c in range(C):
        for r in range(2):
            stx[pl.ds(r * C + c, 8, stride=PACK), :] = heads[c][r * 8 : r * 8 + 8]
            stx[pl.ds(HALF + r * C + c, 8, stride=PACK), :] = tails[c][r * 8 : r * 8 + 8]
    send_all(*tot_x)
    sent_all(*coup_y)
    sent_all(*coup_x)
    sent_all(*tot_y)
    sent_all(*ret_y)
    for f in faces:
        f.wait_send()
    recv_all(*tot_x)
    reduce_solve(NI, ttx, kx, otx)
    send_all(*ret_x)

    def extra(m, slot, to):
        return pltpu.make_async_remote_copy(
            src_ref=otx.at[pl.ds(pl.multiple_of(m * PACK, 8), PACK), :],
            dst_ref=ext.at[slot, pl.ds(0, PACK), :],
            send_sem=s_ex.at[slot, m],
            recv_sem=r_ex.at[slot],
            device_id=(m, to),
            device_id_type=MESH,
        )

    @pl.when(i == 0)
    def _():
        for m in range(NI):
            extra(m, 1, jprev).start()

    @pl.when(i == NI - 1)
    def _():
        for m in range(NI):
            extra(m, 0, jnext).start()

    recv_all(*ret_x)
    extra(0, 0, jnext).wait_recv()
    extra(0, 1, jprev).wait_recv()

    lefts, rights = [], []
    for c in range(C):
        left = jnp.concatenate([rtx[pl.ds(r * C + c, 8, stride=PACK), :] for r in range(2)], axis=0)
        right = jnp.concatenate([rtx[pl.ds(HALF + r * C + c, 8, stride=PACK), :] for r in range(2)], axis=0)
        fb[pl.ds(c * PITCH + 8, Y), :] = left
        fb[pl.ds(c * PITCH + (X + 1) * PAD + 8, Y), :] = right
        lefts.append(left * xr[0:Y, :])
        rights.append(right)
    left_halo = jnp.concatenate([ext[0, 6:14, :], ext[1, 0:8, :]], axis=0) * xr[16:32, :]
    right_halo = jnp.concatenate([ext[0, 18:26, :], ext[1, 12:20, :]], axis=0)

    def x_finish(step, carry):
        x = X - 1 - step
        live, halo = carry
        rows = pl.ds(pl.multiple_of(x * Y, Y), Y)
        weight, finish = xw[x, 0:Y, :], xo[x, 0:Y, :]
        out = []
        for c in range(C):
            value = live[c] + weight * (ay[c, rows, :] + lefts[c])
            fb[pl.ds(pl.multiple_of(c * PITCH + (x + 1) * PAD + 8, 8), Y), :] = value * finish
            out.append(value)
        halo = halo + xw[x, 16:32, :] * (ayh[rows, :] + left_halo)
        edge = halo * xo[x, 16:32, :]
        fb[pl.ds((x + 1) * PAD + 7, 8, stride=PITCH), :] = edge[0:8]
        fb[pl.ds((x + 2) * PAD, 8, stride=PITCH), :] = edge[8:16]
        return tuple(out), halo

    lax.fori_loop(0, X, x_finish, (tuple(rights), right_halo), unroll=2)

    def advect(x, _):
        rows = pl.ds(pl.multiple_of(x * Y, Y), Y)
        middle = c0[rows, :]
        from_x, to_x = bx[rows, :], ax[pl.ds(pl.multiple_of((x + 2) * Y, Y), Y), :]
        from_y, to_y = byp[pl.ds(x * PAD + 7, Y), :], ayp[pl.ds(x * PAD + 9, Y), :]
        from_z, to_z = bzp[rows, :], azn[rows, :]
        for c in range(C):
            at = c * PITCH + (x + 1) * PAD + 8
            value = fb[pl.ds(pl.multiple_of(at, 8), Y), :]
            result = middle * value
            result += to_x * fb[pl.ds(pl.multiple_of(at + PAD, 8), Y), :]
            result -= from_x * fb[pl.ds(pl.multiple_of(at - PAD, 8), Y), :]
            result += to_y * fb[pl.ds(at + 1, Y), :]
            result -= from_y * fb[pl.ds(at - 1, Y), :]
            result += to_z * pltpu.roll(value, Z - 1, 1)
            result -= from_z * pltpu.roll(value, 1, 1)
            out[c, rows, :] = result
        return 0

    lax.fori_loop(0, X, advect, 0, unroll=2)

    sent_all(*tot_x)
    sent_all(*ret_x)

    @pl.when(i == 0)
    def _():
        for m in range(NI):
            extra(m, 1, jprev).wait_send()

    @pl.when(i == NI - 1)
    def _():
        for m in range(NI):
            extra(m, 0, jnext).wait_send()


def on_device(cotangent, diffusion, phase, courant, upwind):
    def vm(*shape, dtype=f32):
        return pltpu.VMEM(shape, dtype)

    dma = pltpu.SemaphoreType.DMA
    scratch = [
        vm(C, LINES, Z), vm(LINES, Z), vm(LINES, Z, dtype=jnp.int32), vm(3, LINES, Z), vm(3, LINES, Z, dtype=jnp.int32),
        vm(LINES, Z),
        vm(LINES // Z, Z, Z), vm(LINES, Z), vm(LINES, Z), vm(LINES, Z), vm(C, LINES, Z), vm(2, 2 * Z, Z, dtype=jnp.bfloat16),
        vm(Y, X, Z), vm(Y, X, Z), vm(Y, X, Z), vm(Y, X, Z), vm(X, Z), vm(C, Y, X, Z), vm(C, LINES, Z), vm(X * 16, Z),
        vm(X, 32, Z), vm(X, 32, Z), vm(X, 32, Z), vm(X, 32, Z), vm(X, 32, Z), vm(32, Z),
        vm(NJ * 8, Z), vm(NI * 8, Z), vm(NJ * 8, Z), vm(NI * 8, Z), vm(6, NJ, 16, Z), vm(6, NI, 16, Z), vm(2, NJ, 16, Z),
        vm(NJ * PACK, Z), vm(NJ * PACK, Z), vm(NJ * PACK, Z), vm(NJ * PACK, Z),
        vm(NI * PACK, Z), vm(NI * PACK, Z), vm(NI * PACK, Z), vm(NI * PACK, Z), vm(2, 32, Z),
        vm(2, 2, X, Z), vm(2, 2, X, Z), vm(2, Y, Z), vm(2, Y, Z),
        vm(LINES, Z), vm(LINES + 2 * Y, Z), vm(LINES + 2 * Y, Z), vm(X * PAD + 8, Z), vm(X * PAD + 8, Z), vm(LINES, Z), vm(LINES, Z),
        vm(8 * PITCH, Z),
        dma((5,)),
        dma((NJ,)), dma((NJ,)), dma((NI,)), dma((NI,)), dma((2,)), dma((2,)), dma((2,)), dma((2,)),
        dma((NJ,)), dma((NJ,)), dma((NJ,)), dma((NJ,)), dma((NI,)), dma((NI,)), dma((NI,)), dma((NI,)),
        dma((2, NI)), dma((2,)),
    ]
    out = pl.pallas_call(
        body,
        out_shape=jax.ShapeDtypeStruct((C, LINES, Z), f32),
        in_specs=[pl.BlockSpec(memory_space=pltpu.HBM)] * 5,
        out_specs=pl.BlockSpec(memory_space=pltpu.VMEM),
        scratch_shapes=scratch,
        compiler_params=pltpu.CompilerParams(
            collective_id=0, has_side_effects=True, vmem_limit_bytes=48 * 1024 * 1024
        ),
    )(
        *(
            pltpu.with_memory_space_constraint(given, pltpu.HBM)
            for given in (
                cotangent.reshape(C, LINES, Z),
                diffusion.reshape(LINES, Z),
                phase.reshape(LINES, Z),
                courant.reshape(3, LINES, Z),
                upwind.reshape(3, LINES, Z),
            )
        )
    )
    return out.reshape(C, X, Y, Z)


def solution(mesh):
    placed = (
        P(None, "gx", "gy", None),
        P("gx", "gy", None),
        P("gx", "gy", None),
        P(None, "gx", "gy", None),
        P(None, "gx", "gy", None),
    )
    return jax.shard_map(
        on_device, mesh=mesh, in_specs=placed, out_specs=P(None, "gx", "gy", None), check_vma=False
    )
```

```python
import functools

import jax
import jax.numpy as jnp
from jax import lax
from jax.experimental import pallas as pl
from jax.experimental.pallas import tpu as pltpu
from jax.sharding import PartitionSpec as P

MESH = pl.DeviceIdType.MESH
C, X, Y, Z = 6, 32, 16, 128
NI, NJ = 8, 16
LINES = X * Y
PAD = 24
PLANES = X + 2
PITCH = PLANES * PAD + 8
HALF = C * 2
PACK = 2 * HALF
f32 = jnp.float32


def split(values):
    high = values.astype(jnp.bfloat16)
    low = (values - high.astype(f32)).astype(jnp.bfloat16)
    return jnp.concatenate([high, low], axis=1)


def body(
    cot_h, dif_h, pha_h, cou_h, upw_h, out,
    cot, dif, pha, cou, upw, ec,
    et, zt, zw, zo, zb, tri,
    yb, ya, yw, yo, yr, yf, ay, ayh,
    xe, xb, xa, xw, xo, xr,
    csy, csx, rcy, rcx, ky, kx, gl,
    sty, tty, oty, rty, stx, ttx, otx, rtx, ext,
    fse, fre, fsy, fry, fsx, frx,
    c0, ax, bx, ayp, byp, azn, bzp, fb,
    in_sem,
    s_cy, r_cy, s_cx, r_cx, s_fe, r_fe, s_fy, r_fy, s_fx, r_fx,
    s_ty, r_ty, s_oy, r_oy, s_tx, r_tx, s_ox, r_ox, s_ex, r_ex,
):
    i = lax.axis_index("gx")
    j = lax.axis_index("gy")
    inext, iprev = lax.rem(i + 1, NI), lax.rem(i + NI - 1, NI)
    jnext, jprev = lax.rem(j + 1, NJ), lax.rem(j + NJ - 1, NJ)

    loads = [
        pltpu.make_async_copy(dif_h, dif, in_sem.at[0]),
        pltpu.make_async_copy(pha_h, pha, in_sem.at[1]),
        pltpu.make_async_copy(cot_h, cot, in_sem.at[2]),
        pltpu.make_async_copy(cou_h, cou, in_sem.at[3]),
        pltpu.make_async_copy(upw_h, upw, in_sem.at[4]),
    ]
    for load in loads[:3]:
        load.start()

    barrier = pltpu.get_barrier_semaphore()

    def greet_y(d, _):
        pl.semaphore_signal(barrier, inc=1, device_id=(i, lax.rem(j + d, NJ)), device_id_type=MESH)
        return 0

    def greet_x(d, _):
        pl.semaphore_signal(barrier, inc=1, device_id=(lax.rem(i + d, NI), j), device_id_type=MESH)
        return 0

    lax.fori_loop(1, NJ, greet_y, 0)
    lax.fori_loop(1, NI, greet_x, 0)

    @pl.when(i != 0)
    def _():
        pl.semaphore_signal(barrier, inc=1, device_id=(0, jnext), device_id_type=MESH)

    @pl.when(i != NI - 1)
    def _():
        pl.semaphore_signal(barrier, inc=1, device_id=(NI - 1, jprev), device_id_type=MESH)

    loads[0].wait()
    loads[1].wait()
    ec[...] = 1.0 / (dif[...] * (1.0 + 3.0 * pha[...].astype(f32)))

    for q in range(X // 8):
        xs = pl.ds(q * 8, 8)
        cells = [ec[pl.ds(q * 8 * Y + y, 8, stride=Y), :] for y in range(Y)]
        theta = jnp.ones((8, Z), f32)
        delta = jnp.ones((8, Z), f32)
        for y in range(Y):
            yb[y, xs, :] = theta
            delta = delta + cells[y] * theta
            theta = theta + delta
        rn = 1.0 / theta
        yr[xs, :] = rn
        phi = jnp.ones((8, Z), f32)
        delta = jnp.ones((8, Z), f32)
        after = jnp.ones((8, Z), f32)
        at = (q % 2) * 8 * 8 + q // 2
        for y in range(Y - 1, -1, -1):
            a = phi * rn
            b = yb[y, xs, :] * rn
            ya[y, xs, :] = a
            yb[y, xs, :] = b
            yw[y, xs, :] = 1.0 / (b * after)
            yo[y, xs, :] = b * cells[y]
            if y == Y - 1:
                csy[pl.ds(at + 4, 8, stride=8), :] = b
            if y == 0:
                csy[pl.ds(at, 8, stride=8), :] = a
            after = b
            delta = delta + cells[y] * phi
            phi = phi + delta
        csy[pl.ds(at + 2, 8, stride=8), :] = rn

    seg = lax.broadcasted_iota(jnp.int32, (8, Z), 0)
    span = Z // 8
    tiles = LINES // Z
    for t in range(tiles):
        et[t] = ec[t * Z : (t + 1) * Z, :].T
    ones = jnp.ones((8, Z), f32)
    zeros = jnp.zeros((8, Z), f32)

    def cell(t, step):
        return et[t, pl.ds(step, 8, stride=span), :]

    starts = []
    for t in range(tiles):
        p11, p12, p21, p22 = ones, zeros, zeros, ones
        for step in range(span):
            e = cell(t, step)
            p21 = p21 + e * p11
            p22 = p22 + e * p12
            p11 = p11 + p21
            p12 = p12 + p22
        for shift in (1, 2, 4):
            keep = seg < shift
            q11 = jnp.where(keep, 1.0, pltpu.roll(p11, shift, 0))
            q12 = jnp.where(keep, 0.0, pltpu.roll(p12, shift, 0))
            q21 = jnp.where(keep, 0.0, pltpu.roll(p21, shift, 0))
            q22 = jnp.where(keep, 1.0, pltpu.roll(p22, shift, 0))
            p11, p12, p21, p22 = (
                p11 * q11 + p12 * q21,
                p11 * q12 + p12 * q22,
                p21 * q11 + p22 * q21,
                p21 * q12 + p22 * q22,
            )
        theta = jnp.where(seg < 1, 1.0, pltpu.roll(p11 + p12, 1, 0))
        delta = jnp.where(seg < 1, 1.0, pltpu.roll(p21 + p22, 1, 0))
        starts.append((theta, delta))
    for t in range(tiles):
        theta, delta = starts[t]
        for step in range(span):
            delta = delta + cell(t, step) * theta
            theta = theta + delta
            et[t, pl.ds(step, 8, stride=span), :] = theta
    lane = lax.broadcasted_iota(jnp.int32, (Z, Z), 1)
    for t in range(tiles):
        rows = pl.ds(t * Z, Z)
        theta = et[t].T
        before = jnp.where(lane < 1, 1.0, pltpu.roll(theta, 1, 1))
        zt[rows, :] = before
        zw[rows, :] = 1.0 / (theta * before)
        zo[rows, :] = before * ec[rows, :]

    row = lax.rem(lax.broadcasted_iota(jnp.int32, (2 * Z, Z), 0), Z)
    col = lax.broadcasted_iota(jnp.int32, (2 * Z, Z), 1)
    tri[0] = (row <= col).astype(f32).astype(jnp.bfloat16)
    tri[1] = (row >= col).astype(f32).astype(jnp.bfloat16)

    outer = (i == 0) | (i == NI - 1)
    pl.semaphore_wait(barrier, NI + NJ - 2 + jnp.where(outer, NI - 1, 0))

    def exchange(src, dst, send, recv, rows, k, axis):
        here = j if axis == "gy" else i
        return pltpu.make_async_remote_copy(
            src_ref=src.at[pl.ds(pl.multiple_of(k * rows, 8), rows), :],
            dst_ref=dst.at[pl.ds(pl.multiple_of(here * rows, 8), rows), :],
            send_sem=send.at[k],
            recv_sem=recv.at[here],
            device_id={axis: k},
            device_id_type=MESH,
        )

    def arrival(src, dst, send, recv, rows, k, axis):
        return pltpu.make_async_remote_copy(
            src_ref=src.at[pl.ds(pl.multiple_of(k * rows, 8), rows), :],
            dst_ref=dst.at[pl.ds(pl.multiple_of(k * rows, 8), rows), :],
            send_sem=send.at[k],
            recv_sem=recv.at[k],
            device_id={axis: k},
            device_id_type=MESH,
        )

    def count_of(axis):
        return NJ if axis == "gy" else NI

    def send_all(src, dst, send, recv, rows, axis):
        n = count_of(axis)
        here = j if axis == "gy" else i
        mine = pl.ds(pl.multiple_of(here * rows, 8), rows)

        def step(d, _):
            exchange(src, dst, send, recv, rows, lax.rem(here + d, n), axis).start()
            return 0

        lax.fori_loop(1, n, step, 0)
        dst[mine, :] = src[mine, :]

    def recv_all(src, dst, send, recv, rows, axis):
        n = count_of(axis)
        here = j if axis == "gy" else i

        def step(d, _):
            arrival(src, dst, send, recv, rows, lax.rem(here + d, n), axis).wait_recv()
            return 0

        lax.fori_loop(1, n, step, 0)

    def sent_all(src, dst, send, recv, rows, axis):
        n = count_of(axis)
        here = j if axis == "gy" else i

        def step(d, _):
            arrival(src, dst, send, recv, rows, lax.rem(here + d, n), axis).wait_send()
            return 0

        lax.fori_loop(1, n, step, 0)

    coup_y = (csy, rcy, s_cy, r_cy, 8, "gy")
    coup_x = (csx, rcx, s_cx, r_cx, 8, "gx")
    tot_y = (sty, tty, s_ty, r_ty, PACK, "gy")
    ret_y = (oty, rty, s_oy, r_oy, PACK, "gy")
    tot_x = (stx, ttx, s_tx, r_tx, PACK, "gx")
    ret_x = (otx, rtx, s_ox, r_ox, PACK, "gx")

    def face(src, dst, send, recv, slot, axis, to):
        return pltpu.make_async_remote_copy(
            src_ref=src.at[slot], dst_ref=dst.at[slot], send_sem=send.at[slot], recv_sem=recv.at[slot],
            device_id={axis: to}, device_id_type=MESH,
        )

    edges = [
        face(fse, fre, s_fe, r_fe, 0, "gy", jprev),
        face(fse, fre, s_fe, r_fe, 1, "gy", jnext),
    ]
    faces = [
        face(fsy, fry, s_fy, r_fy, 0, "gy", jprev),
        face(fsy, fry, s_fy, r_fy, 1, "gy", jnext),
        face(fsx, frx, s_fx, r_fx, 0, "gx", iprev),
        face(fsx, frx, s_fx, r_fx, 1, "gx", inext),
    ]
    send_all(*coup_y)
    fse[0] = ec[pl.ds(0, X, stride=Y), :]
    fse[1] = ec[pl.ds(Y - 1, X, stride=Y), :]
    for e in edges:
        e.start()
    loads[2].wait()
    loads[3].start()
    loads[4].start()

    def z_and_y(q):
        rows = pl.ds(q * 8 * Y, 8 * Y)
        scale, weight, finish = zt[rows, :], zw[rows, :], zo[rows, :]
        sums = [
            jnp.dot(split(cot[c, rows, :] * scale), tri[0], preferred_element_type=f32) for c in range(C)
        ]
        for c in range(C):
            whole = jnp.dot(split(sums[c] * weight), tri[1], preferred_element_type=f32)
            zb[c, rows, :] = whole * finish
        xs = pl.ds(q * 8, 8)
        heads = [jnp.zeros((8, Z), f32) for _ in range(C)]
        tails = [jnp.zeros((8, Z), f32) for _ in range(C)]
        for y in range(Y):
            a, b = ya[y, xs, :], yb[y, xs, :]
            for c in range(C):
                value = zb[c, pl.ds(q * 8 * Y + y, 8, stride=Y), :]
                heads[c] = heads[c] + a * value
                tails[c] = tails[c] + b * value
                yf[c, y, xs, :] = tails[c]
        at = (q % 2) * 8 * PACK + (q // 2) * C
        for c in range(C):
            sty[pl.ds(at + c, 8, stride=PACK), :] = heads[c]
            sty[pl.ds(at + HALF + c, 8, stride=PACK), :] = tails[c]

    def wave(w):
        def step(d, _):
            k = lax.rem(j + d, 8) + 8 * w

            @pl.when(k != j)
            def _():
                exchange(*tot_y[:5], k, "gy").start()

            return 0

        lax.fori_loop(0, 8, step, 0)

    z_and_y(0)
    z_and_y(2)
    wave(0)
    z_and_y(1)
    z_and_y(3)
    wave(1)
    mine_y = pl.ds(pl.multiple_of(j * PACK, 8), PACK)
    tty[mine_y, :] = sty[mine_y, :]

    def x_factor():
        rows = pl.ds(0, 32)
        one = jnp.ones((32, Z), f32)

        def up(x, carry):
            theta, delta = carry
            xb[x, rows, :] = theta
            delta = delta + xe[x, rows, :] * theta
            return theta + delta, delta

        theta, _ = lax.fori_loop(0, X, up, (one, one), unroll=8)
        rn = 1.0 / theta
        xr[rows, :] = rn

        def down(step, carry):
            x = X - 1 - step
            phi, delta, after, _ = carry
            cell = xe[x, rows, :]
            a = phi * rn
            b = xb[x, rows, :] * rn
            xa[x, rows, :] = a
            xb[x, rows, :] = b
            xw[x, rows, :] = 1.0 / (b * after)
            xo[x, rows, :] = b * cell
            delta = delta + cell * phi
            return phi + delta, delta, b, a

        _, _, _, first = lax.fori_loop(0, X, down, (one, one, one, one), unroll=8)
        return first, rn

    for e in edges:
        e.wait_recv()
    for x in range(X):
        xe[x, 0:Y, :] = ec[x * Y : (x + 1) * Y, :]
        xe[x, 16:24, :] = jnp.broadcast_to(fre[1, x : x + 1, :], (8, Z))
        xe[x, 24:32, :] = jnp.broadcast_to(fre[0, x : x + 1, :], (8, Z))
    first, rn = x_factor()
    last = xb[X - 1, 0:Y, :]
    for r in range(2):
        csx[pl.ds(r, 8, stride=8), :] = first[r * 8 : r * 8 + 8]
        csx[pl.ds(2 + r, 8, stride=8), :] = rn[r * 8 : r * 8 + 8]
        csx[pl.ds(4 + r, 8, stride=8), :] = last[r * 8 : r * 8 + 8]

    loads[3].wait()
    loads[4].wait()
    fsy[0] = upw[1, pl.ds(0, X, stride=Y), :].astype(f32) * cou[1, pl.ds(0, X, stride=Y), :]
    fsy[1] = (1.0 - upw[1, pl.ds(Y - 1, X, stride=Y), :].astype(f32)) * cou[1, pl.ds(Y - 1, X, stride=Y), :]
    fsx[0] = upw[0, 0:Y, :].astype(f32) * cou[0, 0:Y, :] * ec[0:Y, :]
    fsx[1] = (1.0 - upw[0, LINES - Y : LINES, :].astype(f32)) * cou[0, LINES - Y : LINES, :] * ec[LINES - Y : LINES, :]

    send_all(*coup_x)
    for f in faces:
        f.start()

    def reduce_factor(count, couplings, factors):
        def pair(base, t):
            return jnp.concatenate(
                [
                    jnp.broadcast_to(couplings[pl.ds(base + 2 * t, 1), :], (C, Z)),
                    jnp.broadcast_to(couplings[pl.ds(base + 2 * t + 1, 1), :], (C, Z)),
                ],
                axis=0,
            )

        edge = jnp.zeros((HALF, Z), f32)
        for m in range(count):
            a1, b1, bn = pair(m * 8, 0), pair(m * 8, 1), pair(m * 8, 2)
            alpha = 1.0 / (1.0 - a1 * edge)
            alpha_a = a1 * alpha
            forward = b1 * alpha
            back = b1 * edge
            factors[0, m, 0:HALF, :] = alpha
            factors[1, m, 0:HALF, :] = alpha_a
            factors[2, m, 0:HALF, :] = forward
            factors[3, m, 0:HALF, :] = edge
            factors[4, m, 0:HALF, :] = back * alpha
            factors[5, m, 0:HALF, :] = b1 + back * alpha_a
            edge = bn + back * forward

    def reduce_solve(count, totals, factors, results):
        gain = jnp.zeros((HALF, Z), f32)
        for m in range(count):
            head = totals[m * PACK : m * PACK + HALF, :]
            tail = totals[m * PACK + HALF : m * PACK + PACK, :]
            gl[0, m, 0:HALF, :] = gain
            gl[1, m, 0:HALF, :] = factors[0, m, 0:HALF, :] * head + factors[1, m, 0:HALF, :] * gain
            gain = tail + factors[4, m, 0:HALF, :] * head + factors[5, m, 0:HALF, :] * gain
        later = jnp.zeros((HALF, Z), f32)
        for m in range(count - 1, -1, -1):
            results[m * PACK + HALF : m * PACK + PACK, :] = later
            later = gl[1, m, 0:HALF, :] + factors[2, m, 0:HALF, :] * later
            results[m * PACK : m * PACK + HALF, :] = gl[0, m, 0:HALF, :] + factors[3, m, 0:HALF, :] * later

    recv_all(*coup_y)
    reduce_factor(NJ, rcy, ky)

    recv_all(*tot_y)
    reduce_solve(NJ, tty, ky, oty)
    send_all(*ret_y)

    recv_all(*coup_x)
    reduce_factor(NI, rcx, kx)
    for f in faces:
        f.wait_recv()

    low_ok = jnp.where(j > 0, 1.0, 0.0).astype(f32)
    high_ok = jnp.where(j < NJ - 1, 1.0, 0.0).astype(f32)
    lane16 = lax.broadcasted_iota(jnp.int32, (Y, Z), 1)

    def coefficients(x, _):
        rows = pl.ds(pl.multiple_of(x * Y, Y), Y)
        shifted = pl.ds(pl.multiple_of(x * Y + Y, Y), Y)
        padded = pl.ds(pl.multiple_of(x * PAD + 8, 8), Y)
        flux = [cou[d, rows, :] for d in range(3)]
        ahead = [upw[d, rows, :].astype(f32) * flux[d] for d in range(3)]
        behind = [flux[d] - ahead[d] for d in range(3)]
        c0[rows, :] = 1.0 + (behind[0] - ahead[0]) + (behind[1] - ahead[1]) + (behind[2] - ahead[2])
        ax[shifted, :] = ahead[0]
        bx[shifted, :] = behind[0]
        ayp[padded, :] = ahead[1]
        byp[padded, :] = behind[1]
        azn[rows, :] = jnp.where(lane16 < Z - 1, pltpu.roll(ahead[2], Z - 1, 1), 0.0)
        bzp[rows, :] = jnp.where(lane16 > 0, pltpu.roll(behind[2], 1, 1), 0.0)
        return 0

    lax.fori_loop(0, X, coefficients, 0, unroll=8)
    bx[0:Y, :] = frx[1]
    ax[(X + 1) * Y : (X + 2) * Y, :] = frx[0]
    byp[pl.ds(7, X, stride=PAD), :] = fry[1] * low_ok
    ayp[pl.ds(PAD, X, stride=PAD), :] = fry[0] * high_ok
    ayh[...] = jnp.zeros_like(ayh)

    recv_all(*ret_y)

    for q in (0, 2, 1, 3):
        xs = pl.ds(q * 8, 8)
        at = (q % 2) * 8 * PACK + (q // 2) * C
        below, above, live = [], [], []
        for c in range(C):
            left = rty[pl.ds(at + c, 8, stride=PACK), :]
            right = rty[pl.ds(at + HALF + c, 8, stride=PACK), :]
            ayh[pl.ds(q * 8 * 16 + c, 8, stride=16), :] = left * fre[1, xs, :]
            ayh[pl.ds(q * 8 * 16 + 8 + c, 8, stride=16), :] = right * fre[0, xs, :]
            below.append(left * yr[xs, :])
            live.append(right)
        for y in range(Y - 1, -1, -1):
            weight, finish = yw[y, xs, :], yo[y, xs, :]
            for c in range(C):
                live[c] = live[c] + weight * (yf[c, y, xs, :] + below[c])
                ay[c, pl.ds(q * 8 * Y + y, 8, stride=Y), :] = live[c] * finish

    def x_totals(x, carry):
        heads, tails, halo = carry
        rows = pl.ds(pl.multiple_of(x * Y, Y), Y)
        a, b = xa[x, 0:Y, :], xb[x, 0:Y, :]
        new_heads, new_tails = [], []
        for c in range(C):
            value = ay[c, rows, :]
            new_heads.append(heads[c] + a * value)
            tail = tails[c] + b * value
            new_tails.append(tail)
            ay[c, rows, :] = tail
        halo = halo + xb[x, 16:32, :] * ayh[rows, :]
        ayh[rows, :] = halo
        return tuple(new_heads), tuple(new_tails), halo

    none = jnp.zeros((Y, Z), f32)
    heads, tails, _ = lax.fori_loop(0, X, x_totals, ((none,) * C, (none,) * C, none), unroll=8)
    for c in range(C):
        for r in range(2):
            stx[pl.ds(r * C + c, 8, stride=PACK), :] = heads[c][r * 8 : r * 8 + 8]
            stx[pl.ds(HALF + r * C + c, 8, stride=PACK), :] = tails[c][r * 8 : r * 8 + 8]
    send_all(*tot_x)
    sent_all(*coup_y)
    sent_all(*coup_x)
    sent_all(*tot_y)
    sent_all(*ret_y)
    for f in edges + faces:
        f.wait_send()
    recv_all(*tot_x)
    reduce_solve(NI, ttx, kx, otx)
    send_all(*ret_x)

    def extra(m, slot, to):
        return pltpu.make_async_remote_copy(
            src_ref=otx.at[pl.ds(pl.multiple_of(m * PACK, 8), PACK), :],
            dst_ref=ext.at[slot, pl.ds(0, PACK), :],
            send_sem=s_ex.at[slot, m],
            recv_sem=r_ex.at[slot],
            device_id=(m, to),
            device_id_type=MESH,
        )

    @pl.when(i == 0)
    def _():
        for m in range(NI):
            extra(m, 1, jprev).start()

    @pl.when(i == NI - 1)
    def _():
        for m in range(NI):
            extra(m, 0, jnext).start()

    recv_all(*ret_x)
    extra(0, 0, jnext).wait_recv()
    extra(0, 1, jprev).wait_recv()

    lefts, rights = [], []
    for c in range(C):
        left = jnp.concatenate([rtx[pl.ds(r * C + c, 8, stride=PACK), :] for r in range(2)], axis=0)
        right = jnp.concatenate([rtx[pl.ds(HALF + r * C + c, 8, stride=PACK), :] for r in range(2)], axis=0)
        fb[pl.ds(c * PITCH + 8, Y), :] = left
        fb[pl.ds(c * PITCH + (X + 1) * PAD + 8, Y), :] = right
        lefts.append(left * xr[0:Y, :])
        rights.append(right)
    left_halo = jnp.concatenate([ext[0, 6:14, :], ext[1, 0:8, :]], axis=0) * xr[16:32, :]
    right_halo = jnp.concatenate([ext[0, 18:26, :], ext[1, 12:20, :]], axis=0)

    def x_finish(step, carry):
        x = X - 1 - step
        live, halo = carry
        rows = pl.ds(pl.multiple_of(x * Y, Y), Y)
        weight, finish = xw[x, 0:Y, :], xo[x, 0:Y, :]
        out = []
        for c in range(C):
            value = live[c] + weight * (ay[c, rows, :] + lefts[c])
            fb[pl.ds(pl.multiple_of(c * PITCH + (x + 1) * PAD + 8, 8), Y), :] = value * finish
            out.append(value)
        halo = halo + xw[x, 16:32, :] * (ayh[rows, :] + left_halo)
        edge = halo * xo[x, 16:32, :]
        fb[pl.ds((x + 1) * PAD + 7, 8, stride=PITCH), :] = edge[0:8]
        fb[pl.ds((x + 2) * PAD, 8, stride=PITCH), :] = edge[8:16]
        return tuple(out), halo

    lax.fori_loop(0, X, x_finish, (tuple(rights), right_halo), unroll=4)

    def advect(x, _):
        rows = pl.ds(pl.multiple_of(x * Y, Y), Y)
        middle = c0[rows, :]
        from_x, to_x = bx[rows, :], ax[pl.ds(pl.multiple_of((x + 2) * Y, Y), Y), :]
        from_y, to_y = byp[pl.ds(x * PAD + 7, Y), :], ayp[pl.ds(x * PAD + 9, Y), :]
        from_z, to_z = bzp[rows, :], azn[rows, :]
        for c in range(C):
            at = c * PITCH + (x + 1) * PAD + 8
            value = fb[pl.ds(pl.multiple_of(at, 8), Y), :]
            result = middle * value
            result += to_x * fb[pl.ds(pl.multiple_of(at + PAD, 8), Y), :]
            result -= from_x * fb[pl.ds(pl.multiple_of(at - PAD, 8), Y), :]
            result += to_y * fb[pl.ds(at + 1, Y), :]
            result -= from_y * fb[pl.ds(at - 1, Y), :]
            result += to_z * pltpu.roll(value, Z - 1, 1)
            result -= from_z * pltpu.roll(value, 1, 1)
            out[c, rows, :] = result
        return 0

    lax.fori_loop(0, X, advect, 0, unroll=8)

    sent_all(*tot_x)
    sent_all(*ret_x)

    @pl.when(i == 0)
    def _():
        for m in range(NI):
            extra(m, 1, jprev).wait_send()

    @pl.when(i == NI - 1)
    def _():
        for m in range(NI):
            extra(m, 0, jnext).wait_send()


def on_device(cotangent, diffusion, phase, courant, upwind):
    def vm(*shape, dtype=f32):
        return pltpu.VMEM(shape, dtype)

    dma = pltpu.SemaphoreType.DMA
    scratch = [
        vm(C, LINES, Z), vm(LINES, Z), vm(LINES, Z, dtype=jnp.int32), vm(3, LINES, Z), vm(3, LINES, Z, dtype=jnp.int32),
        vm(LINES, Z),
        vm(LINES // Z, Z, Z), vm(LINES, Z), vm(LINES, Z), vm(LINES, Z), vm(C, LINES, Z), vm(2, 2 * Z, Z, dtype=jnp.bfloat16),
        vm(Y, X, Z), vm(Y, X, Z), vm(Y, X, Z), vm(Y, X, Z), vm(X, Z), vm(C, Y, X, Z), vm(C, LINES, Z), vm(X * 16, Z),
        vm(X, 32, Z), vm(X, 32, Z), vm(X, 32, Z), vm(X, 32, Z), vm(X, 32, Z), vm(32, Z),
        vm(NJ * 8, Z), vm(NI * 8, Z), vm(NJ * 8, Z), vm(NI * 8, Z), vm(6, NJ, 16, Z), vm(6, NI, 16, Z), vm(2, NJ, 16, Z),
        vm(NJ * PACK, Z), vm(NJ * PACK, Z), vm(NJ * PACK, Z), vm(NJ * PACK, Z),
        vm(NI * PACK, Z), vm(NI * PACK, Z), vm(NI * PACK, Z), vm(NI * PACK, Z), vm(2, 32, Z),
        vm(2, X, Z), vm(2, X, Z), vm(2, X, Z), vm(2, X, Z), vm(2, Y, Z), vm(2, Y, Z),
        vm(LINES, Z), vm(LINES + 2 * Y, Z), vm(LINES + 2 * Y, Z), vm(X * PAD + 8, Z), vm(X * PAD + 8, Z), vm(LINES, Z), vm(LINES, Z),
        vm(8 * PITCH, Z),
        dma((5,)),
        dma((NJ,)), dma((NJ,)), dma((NI,)), dma((NI,)), dma((2,)), dma((2,)), dma((2,)), dma((2,)), dma((2,)), dma((2,)),
        dma((NJ,)), dma((NJ,)), dma((NJ,)), dma((NJ,)), dma((NI,)), dma((NI,)), dma((NI,)), dma((NI,)),
        dma((2, NI)), dma((2,)),
    ]
    out = pl.pallas_call(
        body,
        out_shape=jax.ShapeDtypeStruct((C, LINES, Z), f32),
        in_specs=[pl.BlockSpec(memory_space=pltpu.HBM)] * 5,
        out_specs=pl.BlockSpec(memory_space=pltpu.VMEM),
        scratch_shapes=scratch,
        compiler_params=pltpu.CompilerParams(
            collective_id=0, has_side_effects=True, vmem_limit_bytes=48 * 1024 * 1024
        ),
    )(
        *(
            pltpu.with_memory_space_constraint(given, pltpu.HBM)
            for given in (
                cotangent.reshape(C, LINES, Z),
                diffusion.reshape(LINES, Z),
                phase.reshape(LINES, Z),
                courant.reshape(3, LINES, Z),
                upwind.reshape(3, LINES, Z),
            )
        )
    )
    return out.reshape(C, X, Y, Z)


def solution(mesh):
    placed = (
        P(None, "gx", "gy", None),
        P("gx", "gy", None),
        P("gx", "gy", None),
        P(None, "gx", "gy", None),
        P(None, "gx", "gy", None),
    )
    return jax.shard_map(
        on_device, mesh=mesh, in_specs=placed, out_specs=P(None, "gx", "gy", None), check_vma=False
    )
```

```python
import functools

import jax
import jax.numpy as jnp
from jax import lax
from jax.experimental import pallas as pl
from jax.experimental.pallas import tpu as pltpu
from jax.sharding import PartitionSpec as P

MESH = pl.DeviceIdType.MESH
C, X, Y, Z = 6, 32, 16, 128
NI, NJ = 8, 16
LINES = X * Y
PAD = 24
PLANES = X + 2
PITCH = PLANES * PAD + 8
HALF = C * 2
PACK = 2 * HALF
f32 = jnp.float32
FAR = sorted(((a, b) for a in range(4) for b in range(4) if a or b), key=lambda d: -min(d[0], 4 - d[0]) - min(d[1], 4 - d[1]))
FAR_X = [(2, 1), (2, 0), (3, 1), (1, 1), (3, 0), (1, 0), (0, 1)]


def split(values):
    high = values.astype(jnp.bfloat16)
    low = (values - high.astype(f32)).astype(jnp.bfloat16)
    return jnp.concatenate([high, low], axis=1)


def body(
    cot_h, dif_h, pha_h, cou_h, upw_h,
    fb, c0, ax, bx, ayp, byp, azn, bzp,
    cot, dif, pha, cou, upw, ec,
    et, zt, zw, zo, zb, tri,
    yb, ya, yw, yo, yr, yf, ay, ayh,
    xe, xb, xa, xw, xo, xr,
    csy, csx, rcy, rcx, ky, kx, gl,
    sty, tty, oty, rty, stx, ttx, otx, rtx, ext,
    fse, fre, fsy, fry, fsx, frx,
    in_sem,
    s_cy, r_cy, s_cx, r_cx, s_fe, r_fe, s_fy, r_fy, s_fx, r_fx,
    s_ty, r_ty, s_oy, r_oy, s_tx, r_tx, s_ox, r_ox, s_ex, r_ex,
):
    i = lax.axis_index("gx")
    j = lax.axis_index("gy")
    inext, iprev = lax.rem(i + 1, NI), lax.rem(i + NI - 1, NI)
    jnext, jprev = lax.rem(j + 1, NJ), lax.rem(j + NJ - 1, NJ)

    loads = [
        pltpu.make_async_copy(dif_h, dif, in_sem.at[0]),
        pltpu.make_async_copy(pha_h, pha, in_sem.at[1]),
        pltpu.make_async_copy(cot_h, cot, in_sem.at[2]),
        pltpu.make_async_copy(cou_h, cou, in_sem.at[3]),
        pltpu.make_async_copy(upw_h, upw, in_sem.at[4]),
    ]
    for load in loads[:3]:
        load.start()

    barrier = pltpu.get_barrier_semaphore()

    def greet_y(d, _):
        pl.semaphore_signal(barrier, inc=1, device_id=(i, lax.rem(j + d, NJ)), device_id_type=MESH)
        return 0

    def greet_x(d, _):
        pl.semaphore_signal(barrier, inc=1, device_id=(lax.rem(i + d, NI), j), device_id_type=MESH)
        return 0

    lax.fori_loop(1, NJ, greet_y, 0)
    lax.fori_loop(1, NI, greet_x, 0)

    @pl.when(i != 0)
    def _():
        pl.semaphore_signal(barrier, inc=1, device_id=(0, jnext), device_id_type=MESH)

    @pl.when(i != NI - 1)
    def _():
        pl.semaphore_signal(barrier, inc=1, device_id=(NI - 1, jprev), device_id_type=MESH)

    loads[0].wait()
    loads[1].wait()
    ec[...] = 1.0 / (dif[...] * (1.0 + 3.0 * pha[...].astype(f32)))

    for q in range(X // 8):
        xs = pl.ds(q * 8, 8)
        cells = [ec[pl.ds(q * 8 * Y + y, 8, stride=Y), :] for y in range(Y)]
        theta = jnp.ones((8, Z), f32)
        delta = jnp.ones((8, Z), f32)
        for y in range(Y):
            yb[y, xs, :] = theta
            delta = delta + cells[y] * theta
            theta = theta + delta
        rn = 1.0 / theta
        yr[xs, :] = rn
        phi = jnp.ones((8, Z), f32)
        delta = jnp.ones((8, Z), f32)
        after = jnp.ones((8, Z), f32)
        at = (q % 2) * 8 * 8 + q // 2
        for y in range(Y - 1, -1, -1):
            a = phi * rn
            b = yb[y, xs, :] * rn
            ya[y, xs, :] = a
            yb[y, xs, :] = b
            yw[y, xs, :] = 1.0 / (b * after)
            yo[y, xs, :] = b * cells[y]
            if y == Y - 1:
                csy[pl.ds(at + 4, 8, stride=8), :] = b
            if y == 0:
                csy[pl.ds(at, 8, stride=8), :] = a
            after = b
            delta = delta + cells[y] * phi
            phi = phi + delta
        csy[pl.ds(at + 2, 8, stride=8), :] = rn

    seg = lax.broadcasted_iota(jnp.int32, (8, Z), 0)
    span = Z // 8
    tiles = LINES // Z
    for t in range(tiles):
        et[t] = ec[t * Z : (t + 1) * Z, :].T
    ones = jnp.ones((8, Z), f32)
    zeros = jnp.zeros((8, Z), f32)

    def cell(t, step):
        return et[t, pl.ds(step, 8, stride=span), :]

    starts = []
    for t in range(tiles):
        p11, p12, p21, p22 = ones, zeros, zeros, ones
        for step in range(span):
            e = cell(t, step)
            p21 = p21 + e * p11
            p22 = p22 + e * p12
            p11 = p11 + p21
            p12 = p12 + p22
        for shift in (1, 2, 4):
            keep = seg < shift
            q11 = jnp.where(keep, 1.0, pltpu.roll(p11, shift, 0))
            q12 = jnp.where(keep, 0.0, pltpu.roll(p12, shift, 0))
            q21 = jnp.where(keep, 0.0, pltpu.roll(p21, shift, 0))
            q22 = jnp.where(keep, 1.0, pltpu.roll(p22, shift, 0))
            p11, p12, p21, p22 = (
                p11 * q11 + p12 * q21,
                p11 * q12 + p12 * q22,
                p21 * q11 + p22 * q21,
                p21 * q12 + p22 * q22,
            )
        theta = jnp.where(seg < 1, 1.0, pltpu.roll(p11 + p12, 1, 0))
        delta = jnp.where(seg < 1, 1.0, pltpu.roll(p21 + p22, 1, 0))
        starts.append((theta, delta))
    for t in range(tiles):
        theta, delta = starts[t]
        for step in range(span):
            delta = delta + cell(t, step) * theta
            theta = theta + delta
            et[t, pl.ds(step, 8, stride=span), :] = theta
    lane = lax.broadcasted_iota(jnp.int32, (Z, Z), 1)
    for t in range(tiles):
        rows = pl.ds(t * Z, Z)
        theta = et[t].T
        before = jnp.where(lane < 1, 1.0, pltpu.roll(theta, 1, 1))
        zt[rows, :] = before
        zw[rows, :] = 1.0 / (theta * before)
        zo[rows, :] = before * ec[rows, :]

    row = lax.rem(lax.broadcasted_iota(jnp.int32, (2 * Z, Z), 0), Z)
    col = lax.broadcasted_iota(jnp.int32, (2 * Z, Z), 1)
    tri[0] = (row <= col).astype(f32).astype(jnp.bfloat16)
    tri[1] = (row >= col).astype(f32).astype(jnp.bfloat16)

    outer = (i == 0) | (i == NI - 1)
    pl.semaphore_wait(barrier, NI + NJ - 2 + jnp.where(outer, NI - 1, 0))

    def exchange(src, dst, send, recv, rows, k, axis):
        here = j if axis == "gy" else i
        return pltpu.make_async_remote_copy(
            src_ref=src.at[pl.ds(pl.multiple_of(k * rows, 8), rows), :],
            dst_ref=dst.at[pl.ds(pl.multiple_of(here * rows, 8), rows), :],
            send_sem=send.at[k],
            recv_sem=recv.at[here],
            device_id={axis: k},
            device_id_type=MESH,
        )

    def arrival(src, dst, send, recv, rows, k, axis):
        return pltpu.make_async_remote_copy(
            src_ref=src.at[pl.ds(pl.multiple_of(k * rows, 8), rows), :],
            dst_ref=dst.at[pl.ds(pl.multiple_of(k * rows, 8), rows), :],
            send_sem=send.at[k],
            recv_sem=recv.at[k],
            device_id={axis: k},
            device_id_type=MESH,
        )

    def peers(axis):
        if axis == "gy":
            return [lax.rem(j // 4 + a, 4) * 4 + lax.rem(j + b, 4) for a, b in FAR]
        return [lax.rem(i // 2 + a, 4) * 2 + lax.rem(i + b, 2) for a, b in FAR_X]

    def send_all(src, dst, send, recv, rows, axis):
        here = j if axis == "gy" else i
        mine = pl.ds(pl.multiple_of(here * rows, 8), rows)
        for k in peers(axis):
            exchange(src, dst, send, recv, rows, k, axis).start()
        dst[mine, :] = src[mine, :]

    def recv_all(src, dst, send, recv, rows, axis):
        for k in reversed(peers(axis)):
            arrival(src, dst, send, recv, rows, k, axis).wait_recv()

    def sent_all(src, dst, send, recv, rows, axis):
        for k in peers(axis):
            arrival(src, dst, send, recv, rows, k, axis).wait_send()

    coup_y = (csy, rcy, s_cy, r_cy, 8, "gy")
    coup_x = (csx, rcx, s_cx, r_cx, 8, "gx")
    tot_y = (sty, tty, s_ty, r_ty, PACK, "gy")
    ret_y = (oty, rty, s_oy, r_oy, PACK, "gy")
    tot_x = (stx, ttx, s_tx, r_tx, PACK, "gx")
    ret_x = (otx, rtx, s_ox, r_ox, PACK, "gx")

    def face(src, dst, send, recv, slot, axis, to):
        return pltpu.make_async_remote_copy(
            src_ref=src.at[slot], dst_ref=dst.at[slot], send_sem=send.at[slot], recv_sem=recv.at[slot],
            device_id={axis: to}, device_id_type=MESH,
        )

    edges = [
        face(fse, fre, s_fe, r_fe, 0, "gy", jprev),
        face(fse, fre, s_fe, r_fe, 1, "gy", jnext),
    ]
    faces = [
        face(fsy, fry, s_fy, r_fy, 0, "gy", jprev),
        face(fsy, fry, s_fy, r_fy, 1, "gy", jnext),
        face(fsx, frx, s_fx, r_fx, 0, "gx", iprev),
        face(fsx, frx, s_fx, r_fx, 1, "gx", inext),
    ]
    send_all(*coup_y)
    fse[0] = ec[pl.ds(0, X, stride=Y), :]
    fse[1] = ec[pl.ds(Y - 1, X, stride=Y), :]
    for e in edges:
        e.start()
    loads[2].wait()
    loads[3].start()
    loads[4].start()

    def z_and_y(q):
        rows = pl.ds(q * 8 * Y, 8 * Y)
        scale, weight, finish = zt[rows, :], zw[rows, :], zo[rows, :]
        sums = [
            jnp.dot(split(cot[c, rows, :] * scale), tri[0], preferred_element_type=f32) for c in range(C)
        ]
        for c in range(C):
            whole = jnp.dot(split(sums[c] * weight), tri[1], preferred_element_type=f32)
            zb[c, rows, :] = whole * finish
        xs = pl.ds(q * 8, 8)
        heads = [jnp.zeros((8, Z), f32) for _ in range(C)]
        tails = [jnp.zeros((8, Z), f32) for _ in range(C)]
        for y in range(Y):
            a, b = ya[y, xs, :], yb[y, xs, :]
            for c in range(C):
                value = zb[c, pl.ds(q * 8 * Y + y, 8, stride=Y), :]
                heads[c] = heads[c] + a * value
                tails[c] = tails[c] + b * value
                yf[c, y, xs, :] = tails[c]
        at = (q % 2) * 8 * PACK + (q // 2) * C
        for c in range(C):
            sty[pl.ds(at + c, 8, stride=PACK), :] = heads[c]
            sty[pl.ds(at + HALF + c, 8, stride=PACK), :] = tails[c]

    def wave(w):
        for b in (2, 1, 3, 0):
            for a in range(2):
                k = 8 * w + 4 * a + lax.rem(j + b, 4)
                if b:
                    exchange(*tot_y[:5], k, "gy").start()
                else:

                    @pl.when(k != j)
                    def _():
                        exchange(*tot_y[:5], k, "gy").start()

    z_and_y(0)
    z_and_y(2)
    wave(0)
    z_and_y(1)
    z_and_y(3)
    wave(1)
    mine_y = pl.ds(pl.multiple_of(j * PACK, 8), PACK)
    tty[mine_y, :] = sty[mine_y, :]

    def x_factor():
        rows = pl.ds(0, 32)
        one = jnp.ones((32, Z), f32)

        def up(x, carry):
            theta, delta = carry
            xb[x, rows, :] = theta
            delta = delta + xe[x, rows, :] * theta
            return theta + delta, delta

        theta, _ = lax.fori_loop(0, X, up, (one, one), unroll=8)
        rn = 1.0 / theta
        xr[rows, :] = rn

        def down(step, carry):
            x = X - 1 - step
            phi, delta, after, _ = carry
            cell = xe[x, rows, :]
            a = phi * rn
            b = xb[x, rows, :] * rn
            xa[x, rows, :] = a
            xb[x, rows, :] = b
            xw[x, rows, :] = 1.0 / (b * after)
            xo[x, rows, :] = b * cell
            delta = delta + cell * phi
            return phi + delta, delta, b, a

        _, _, _, first = lax.fori_loop(0, X, down, (one, one, one, one), unroll=8)
        return first, rn

    for e in edges:
        e.wait_recv()
    for x in range(X):
        xe[x, 0:Y, :] = ec[x * Y : (x + 1) * Y, :]
        xe[x, 16:24, :] = jnp.broadcast_to(fre[1, x : x + 1, :], (8, Z))
        xe[x, 24:32, :] = jnp.broadcast_to(fre[0, x : x + 1, :], (8, Z))
    first, rn = x_factor()
    last = xb[X - 1, 0:Y, :]
    for r in range(2):
        csx[pl.ds(r, 8, stride=8), :] = first[r * 8 : r * 8 + 8]
        csx[pl.ds(2 + r, 8, stride=8), :] = rn[r * 8 : r * 8 + 8]
        csx[pl.ds(4 + r, 8, stride=8), :] = last[r * 8 : r * 8 + 8]

    loads[3].wait()
    loads[4].wait()
    fsy[0] = upw[1, pl.ds(0, X, stride=Y), :].astype(f32) * cou[1, pl.ds(0, X, stride=Y), :]
    fsy[1] = (1.0 - upw[1, pl.ds(Y - 1, X, stride=Y), :].astype(f32)) * cou[1, pl.ds(Y - 1, X, stride=Y), :]
    fsx[0] = upw[0, 0:Y, :].astype(f32) * cou[0, 0:Y, :] * ec[0:Y, :]
    fsx[1] = (1.0 - upw[0, LINES - Y : LINES, :].astype(f32)) * cou[0, LINES - Y : LINES, :] * ec[LINES - Y : LINES, :]

    send_all(*coup_x)
    for f in faces:
        f.start()

    def reduce_factor(count, couplings, factors):
        def pair(base, t):
            return jnp.concatenate(
                [
                    jnp.broadcast_to(couplings[pl.ds(base + 2 * t, 1), :], (C, Z)),
                    jnp.broadcast_to(couplings[pl.ds(base + 2 * t + 1, 1), :], (C, Z)),
                ],
                axis=0,
            )

        edge = jnp.zeros((HALF, Z), f32)
        for m in range(count):
            a1, b1, bn = pair(m * 8, 0), pair(m * 8, 1), pair(m * 8, 2)
            alpha = 1.0 / (1.0 - a1 * edge)
            alpha_a = a1 * alpha
            forward = b1 * alpha
            back = b1 * edge
            factors[0, m, 0:HALF, :] = alpha
            factors[1, m, 0:HALF, :] = alpha_a
            factors[2, m, 0:HALF, :] = forward
            factors[3, m, 0:HALF, :] = edge
            factors[4, m, 0:HALF, :] = back * alpha
            factors[5, m, 0:HALF, :] = b1 + back * alpha_a
            edge = bn + back * forward

    def reduce_solve(count, totals, factors, results):
        gain = jnp.zeros((HALF, Z), f32)
        for m in range(count):
            head = totals[m * PACK : m * PACK + HALF, :]
            tail = totals[m * PACK + HALF : m * PACK + PACK, :]
            gl[0, m, 0:HALF, :] = gain
            gl[1, m, 0:HALF, :] = factors[0, m, 0:HALF, :] * head + factors[1, m, 0:HALF, :] * gain
            gain = tail + factors[4, m, 0:HALF, :] * head + factors[5, m, 0:HALF, :] * gain
        later = jnp.zeros((HALF, Z), f32)
        for m in range(count - 1, -1, -1):
            results[m * PACK + HALF : m * PACK + PACK, :] = later
            later = gl[1, m, 0:HALF, :] + factors[2, m, 0:HALF, :] * later
            results[m * PACK : m * PACK + HALF, :] = gl[0, m, 0:HALF, :] + factors[3, m, 0:HALF, :] * later

    recv_all(*coup_y)
    reduce_factor(NJ, rcy, ky)

    recv_all(*tot_y)
    reduce_solve(NJ, tty, ky, oty)
    send_all(*ret_y)

    recv_all(*coup_x)
    reduce_factor(NI, rcx, kx)
    for f in faces:
        f.wait_recv()

    low_ok = jnp.where(j > 0, 1.0, 0.0).astype(f32)
    high_ok = jnp.where(j < NJ - 1, 1.0, 0.0).astype(f32)
    lane16 = lax.broadcasted_iota(jnp.int32, (Y, Z), 1)

    def coefficients(x, _):
        rows = pl.ds(pl.multiple_of(x * Y, Y), Y)
        shifted = pl.ds(pl.multiple_of(x * Y + Y, Y), Y)
        padded = pl.ds(pl.multiple_of(x * PAD + 8, 8), Y)
        flux = [cou[d, rows, :] for d in range(3)]
        ahead = [upw[d, rows, :].astype(f32) * flux[d] for d in range(3)]
        behind = [flux[d] - ahead[d] for d in range(3)]
        c0[rows, :] = 1.0 + (behind[0] - ahead[0]) + (behind[1] - ahead[1]) + (behind[2] - ahead[2])
        ax[shifted, :] = ahead[0]
        bx[shifted, :] = behind[0]
        ayp[padded, :] = ahead[1]
        byp[padded, :] = behind[1]
        azn[rows, :] = jnp.where(lane16 < Z - 1, pltpu.roll(ahead[2], Z - 1, 1), 0.0)
        bzp[rows, :] = jnp.where(lane16 > 0, pltpu.roll(behind[2], 1, 1), 0.0)
        return 0

    lax.fori_loop(0, X, coefficients, 0, unroll=8)
    bx[0:Y, :] = frx[1]
    ax[(X + 1) * Y : (X + 2) * Y, :] = frx[0]
    byp[pl.ds(7, X, stride=PAD), :] = fry[1] * low_ok
    ayp[pl.ds(PAD, X, stride=PAD), :] = fry[0] * high_ok
    ayh[...] = jnp.zeros_like(ayh)

    recv_all(*ret_y)

    for q in (0, 2, 1, 3):
        xs = pl.ds(q * 8, 8)
        at = (q % 2) * 8 * PACK + (q // 2) * C
        below, above, live = [], [], []
        for c in range(C):
            left = rty[pl.ds(at + c, 8, stride=PACK), :]
            right = rty[pl.ds(at + HALF + c, 8, stride=PACK), :]
            ayh[pl.ds(q * 8 * 16 + c, 8, stride=16), :] = left * fre[1, xs, :]
            ayh[pl.ds(q * 8 * 16 + 8 + c, 8, stride=16), :] = right * fre[0, xs, :]
            below.append(left * yr[xs, :])
            live.append(right)
        for y in range(Y - 1, -1, -1):
            weight, finish = yw[y, xs, :], yo[y, xs, :]
            for c in range(C):
                live[c] = live[c] + weight * (yf[c, y, xs, :] + below[c])
                ay[c, pl.ds(q * 8 * Y + y, 8, stride=Y), :] = live[c] * finish

    def x_totals(x, carry):
        heads, tails, halo = carry
        rows = pl.ds(pl.multiple_of(x * Y, Y), Y)
        a, b = xa[x, 0:Y, :], xb[x, 0:Y, :]
        new_heads, new_tails = [], []
        for c in range(C):
            value = ay[c, rows, :]
            new_heads.append(heads[c] + a * value)
            tail = tails[c] + b * value
            new_tails.append(tail)
            ay[c, rows, :] = tail
        halo = halo + xb[x, 16:32, :] * ayh[rows, :]
        ayh[rows, :] = halo
        return tuple(new_heads), tuple(new_tails), halo

    none = jnp.zeros((Y, Z), f32)
    heads, tails, _ = lax.fori_loop(0, X, x_totals, ((none,) * C, (none,) * C, none), unroll=8)
    for c in range(C):
        for r in range(2):
            stx[pl.ds(r * C + c, 8, stride=PACK), :] = heads[c][r * 8 : r * 8 + 8]
            stx[pl.ds(HALF + r * C + c, 8, stride=PACK), :] = tails[c][r * 8 : r * 8 + 8]
    send_all(*tot_x)
    sent_all(*coup_y)
    sent_all(*coup_x)
    sent_all(*tot_y)
    sent_all(*ret_y)
    for f in edges + faces:
        f.wait_send()
    recv_all(*tot_x)
    reduce_solve(NI, ttx, kx, otx)
    send_all(*ret_x)

    def extra(m, slot, to):
        return pltpu.make_async_remote_copy(
            src_ref=otx.at[pl.ds(pl.multiple_of(m * PACK, 8), PACK), :],
            dst_ref=ext.at[slot, pl.ds(0, PACK), :],
            send_sem=s_ex.at[slot, m],
            recv_sem=r_ex.at[slot],
            device_id=(m, to),
            device_id_type=MESH,
        )

    @pl.when(i == 0)
    def _():
        for m in range(NI):
            extra(m, 1, jprev).start()

    @pl.when(i == NI - 1)
    def _():
        for m in range(NI):
            extra(m, 0, jnext).start()

    sent_all(*tot_x)
    recv_all(*ret_x)
    extra(0, 0, jnext).wait_recv()
    extra(0, 1, jprev).wait_recv()

    lefts, rights = [], []
    for c in range(C):
        left = jnp.concatenate([rtx[pl.ds(r * C + c, 8, stride=PACK), :] for r in range(2)], axis=0)
        right = jnp.concatenate([rtx[pl.ds(HALF + r * C + c, 8, stride=PACK), :] for r in range(2)], axis=0)
        fb[pl.ds(c * PITCH + 8, Y), :] = left
        fb[pl.ds(c * PITCH + (X + 1) * PAD + 8, Y), :] = right
        lefts.append(left * xr[0:Y, :])
        rights.append(right)
    left_halo = jnp.concatenate([ext[0, 6:14, :], ext[1, 0:8, :]], axis=0) * xr[16:32, :]
    right_halo = jnp.concatenate([ext[0, 18:26, :], ext[1, 12:20, :]], axis=0)

    def x_finish(step, carry):
        x = X - 1 - step
        live, halo = carry
        rows = pl.ds(pl.multiple_of(x * Y, Y), Y)
        weight, finish = xw[x, 0:Y, :], xo[x, 0:Y, :]
        out = []
        for c in range(C):
            value = live[c] + weight * (ay[c, rows, :] + lefts[c])
            fb[pl.ds(pl.multiple_of(c * PITCH + (x + 1) * PAD + 8, 8), Y), :] = value * finish
            out.append(value)
        halo = halo + xw[x, 16:32, :] * (ayh[rows, :] + left_halo)
        edge = halo * xo[x, 16:32, :]
        fb[pl.ds((x + 1) * PAD + 7, 8, stride=PITCH), :] = edge[0:8]
        fb[pl.ds((x + 2) * PAD, 8, stride=PITCH), :] = edge[8:16]
        return tuple(out), halo

    lax.fori_loop(0, X, x_finish, (tuple(rights), right_halo), unroll=4)

    sent_all(*ret_x)

    @pl.when(i == 0)
    def _():
        for m in range(NI):
            extra(m, 1, jprev).wait_send()

    @pl.when(i == NI - 1)
    def _():
        for m in range(NI):
            extra(m, 0, jnext).wait_send()


def advection(fb, c0, ax, bx, ayp, byp, azn, bzp, out_h, out, sem):
    def advect(x, _):
        rows = pl.ds(pl.multiple_of(x * Y, Y), Y)
        middle = c0[rows, :]
        from_x, to_x = bx[rows, :], ax[pl.ds(pl.multiple_of((x + 2) * Y, Y), Y), :]
        from_y, to_y = byp[pl.ds(x * PAD + 7, Y), :], ayp[pl.ds(x * PAD + 9, Y), :]
        from_z, to_z = bzp[rows, :], azn[rows, :]
        for c in range(C):
            at = c * PITCH + (x + 1) * PAD + 8
            value = fb[pl.ds(pl.multiple_of(at, 8), Y), :]
            result = middle * value
            result += to_x * fb[pl.ds(pl.multiple_of(at + PAD, 8), Y), :]
            result -= from_x * fb[pl.ds(pl.multiple_of(at - PAD, 8), Y), :]
            result += to_y * fb[pl.ds(at + 1, Y), :]
            result -= from_y * fb[pl.ds(at - 1, Y), :]
            result += to_z * pltpu.roll(value, Z - 1, 1)
            result -= from_z * pltpu.roll(value, 1, 1)
            out[c, rows, :] = result
        return 0

    stores = []
    for part in range(4):
        lax.fori_loop(part * 8, part * 8 + 8, advect, 0, unroll=8)
        rows = pl.ds(part * 8 * Y, 8 * Y)
        store = pltpu.make_async_copy(out.at[:, rows, :], out_h.at[:, rows, :], sem.at[part])
        store.start()
        stores.append(store)
    for store in stores:
        store.wait()


def on_device(cotangent, diffusion, phase, courant, upwind):
    def vm(*shape, dtype=f32):
        return pltpu.VMEM(shape, dtype)

    dma = pltpu.SemaphoreType.DMA
    scratch = [
        vm(C, LINES, Z), vm(LINES, Z), vm(LINES, Z, dtype=jnp.int32), vm(3, LINES, Z), vm(3, LINES, Z, dtype=jnp.int32),
        vm(LINES, Z),
        vm(LINES // Z, Z, Z), vm(LINES, Z), vm(LINES, Z), vm(LINES, Z), vm(C, LINES, Z), vm(2, 2 * Z, Z, dtype=jnp.bfloat16),
        vm(Y, X, Z), vm(Y, X, Z), vm(Y, X, Z), vm(Y, X, Z), vm(X, Z), vm(C, Y, X, Z), vm(C, LINES, Z), vm(X * 16, Z),
        vm(X, 32, Z), vm(X, 32, Z), vm(X, 32, Z), vm(X, 32, Z), vm(X, 32, Z), vm(32, Z),
        vm(NJ * 8, Z), vm(NI * 8, Z), vm(NJ * 8, Z), vm(NI * 8, Z), vm(6, NJ, 16, Z), vm(6, NI, 16, Z), vm(2, NJ, 16, Z),
        vm(NJ * PACK, Z), vm(NJ * PACK, Z), vm(NJ * PACK, Z), vm(NJ * PACK, Z),
        vm(NI * PACK, Z), vm(NI * PACK, Z), vm(NI * PACK, Z), vm(NI * PACK, Z), vm(2, 32, Z),
        vm(2, X, Z), vm(2, X, Z), vm(2, X, Z), vm(2, X, Z), vm(2, Y, Z), vm(2, Y, Z),
        dma((5,)),
        dma((NJ,)), dma((NJ,)), dma((NI,)), dma((NI,)), dma((2,)), dma((2,)), dma((2,)), dma((2,)), dma((2,)), dma((2,)),
        dma((NJ,)), dma((NJ,)), dma((NJ,)), dma((NJ,)), dma((NI,)), dma((NI,)), dma((NI,)), dma((NI,)),
        dma((2, NI)), dma((2,)),
    ]
    vmem = pl.BlockSpec(memory_space=pltpu.VMEM)
    shapes = [(8 * PITCH, Z), (LINES, Z), (LINES + 2 * Y, Z), (LINES + 2 * Y, Z), (X * PAD + 8, Z), (X * PAD + 8, Z), (LINES, Z), (LINES, Z)]
    parts = pl.pallas_call(
        body,
        out_shape=[pltpu.VMEM(shape, f32) for shape in shapes],
        in_specs=[pl.BlockSpec(memory_space=pltpu.HBM)] * 5,
        out_specs=[vmem] * len(shapes),
        scratch_shapes=scratch,
        compiler_params=pltpu.CompilerParams(
            collective_id=0, has_side_effects=True, vmem_limit_bytes=40 * 1024 * 1024
        ),
    )(
        *(
            pltpu.with_memory_space_constraint(given, pltpu.HBM)
            for given in (
                cotangent.reshape(C, LINES, Z),
                diffusion.reshape(LINES, Z),
                phase.reshape(LINES, Z),
                courant.reshape(3, LINES, Z),
                upwind.reshape(3, LINES, Z),
            )
        )
    )
    out = pl.pallas_call(
        advection,
        out_shape=jax.ShapeDtypeStruct((C, LINES, Z), f32),
        in_specs=[vmem] * len(shapes),
        out_specs=pl.BlockSpec(memory_space=pl.ANY),
        scratch_shapes=[vm(C, LINES, Z), dma((4,))],
        compiler_params=pltpu.CompilerParams(vmem_limit_bytes=8 * 1024 * 1024),
    )(*(pltpu.with_memory_space_constraint(part, pltpu.VMEM) for part in parts))
    return out.reshape(C, X, Y, Z)


def solution(mesh):
    placed = (
        P(None, "gx", "gy", None),
        P("gx", "gy", None),
        P("gx", "gy", None),
        P(None, "gx", "gy", None),
        P(None, "gx", "gy", None),
    )
    return jax.shard_map(
        on_device, mesh=mesh, in_specs=placed, out_specs=P(None, "gx", "gy", None), check_vma=False
    )
```

```python
import functools

import jax
import jax.numpy as jnp
from jax import lax
from jax.experimental import pallas as pl
from jax.experimental.pallas import tpu as pltpu
from jax.sharding import PartitionSpec as P

MESH = pl.DeviceIdType.MESH
C, X, Y, Z = 6, 32, 16, 128
NI, NJ = 8, 16
LINES = X * Y
PAD = 24
PLANES = X + 2
PITCH = PLANES * PAD + 8
HALF = C * 2
PACK = 2 * HALF
f32 = jnp.float32
FAR = sorted(((a, b) for a in range(4) for b in range(4) if a or b), key=lambda d: -min(d[0], 4 - d[0]) - min(d[1], 4 - d[1]))
ORDER = (0, 2, 1, 3)
FAR_X = [(2, 1), (2, 0), (3, 1), (1, 1), (3, 0), (1, 0), (0, 1)]


def split(values):
    high = values.astype(jnp.bfloat16)
    low = (values - high.astype(f32)).astype(jnp.bfloat16)
    return jnp.concatenate([high, low], axis=1)


def body(
    cot_h, dif_h, pha_h, cou_h, upw_h,
    fb, c0, ax, bx, ayp, byp, azn, bzp,
    cot, dif, pha, cou, upw, ec,
    et, zt, zw, zo, zb, tri,
    yb, ya, yw, yo, yr, yf, ay, ayh,
    xe, xb, xa, xw, xo, xr,
    csy, csx, rcy, rcx, ky, kx, gl,
    sty, tty, oty, rty, stx, ttx, otx, rtx, ext,
    fse, fre, fsy, fry, fsx, frx,
    in_sem,
    sent, came,
):
    i = lax.axis_index("gx")
    j = lax.axis_index("gy")
    inext, iprev = lax.rem(i + 1, NI), lax.rem(i + NI - 1, NI)
    jnext, jprev = lax.rem(j + 1, NJ), lax.rem(j + NJ - 1, NJ)

    loads = [
        pltpu.make_async_copy(dif_h, dif, in_sem.at[0]),
        pltpu.make_async_copy(pha_h, pha, in_sem.at[1]),
        pltpu.make_async_copy(cou_h, cou, in_sem.at[2]),
        pltpu.make_async_copy(upw_h, upw, in_sem.at[3]),
    ]
    quarters = [pl.ds(q * 8 * Y, 8 * Y) for q in range(4)]
    fields = [
        pltpu.make_async_copy(cot_h.at[:, rows, :], cot.at[:, rows, :], in_sem.at[4 + q])
        for q, rows in enumerate(quarters)
    ]
    loads[0].start()
    loads[1].start()
    for q in ORDER:
        fields[q].start()

    barrier = pltpu.get_barrier_semaphore()

    def greet_y(d, _):
        pl.semaphore_signal(barrier, inc=1, device_id=(i, lax.rem(j + d, NJ)), device_id_type=MESH)
        return 0

    def greet_x(d, _):
        pl.semaphore_signal(barrier, inc=1, device_id=(lax.rem(i + d, NI), j), device_id_type=MESH)
        return 0

    lax.fori_loop(1, NJ, greet_y, 0)
    lax.fori_loop(1, NI, greet_x, 0)

    @pl.when(i != 0)
    def _():
        pl.semaphore_signal(barrier, inc=1, device_id=(0, jnext), device_id_type=MESH)

    @pl.when(i != NI - 1)
    def _():
        pl.semaphore_signal(barrier, inc=1, device_id=(NI - 1, jprev), device_id_type=MESH)

    loads[0].wait()
    loads[1].wait()
    ec[...] = 1.0 / (dif[...] * (1.0 + 3.0 * pha[...].astype(f32)))

    for q in range(X // 8):
        xs = pl.ds(q * 8, 8)
        cells = [ec[pl.ds(q * 8 * Y + y, 8, stride=Y), :] for y in range(Y)]
        theta = jnp.ones((8, Z), f32)
        delta = jnp.ones((8, Z), f32)
        for y in range(Y):
            yb[y, xs, :] = theta
            delta = delta + cells[y] * theta
            theta = theta + delta
        rn = 1.0 / theta
        yr[xs, :] = rn
        phi = jnp.ones((8, Z), f32)
        delta = jnp.ones((8, Z), f32)
        after = jnp.ones((8, Z), f32)
        at = (q % 2) * 8 * 8 + q // 2
        for y in range(Y - 1, -1, -1):
            a = phi * rn
            b = yb[y, xs, :] * rn
            ya[y, xs, :] = a
            yb[y, xs, :] = b
            yw[y, xs, :] = 1.0 / (b * after)
            yo[y, xs, :] = b * cells[y]
            if y == Y - 1:
                csy[pl.ds(at + 4, 8, stride=8), :] = b
            if y == 0:
                csy[pl.ds(at, 8, stride=8), :] = a
            after = b
            delta = delta + cells[y] * phi
            phi = phi + delta
        csy[pl.ds(at + 2, 8, stride=8), :] = rn

    seg = lax.broadcasted_iota(jnp.int32, (8, Z), 0)
    span = Z // 8
    tiles = LINES // Z
    for t in range(tiles):
        et[t] = ec[t * Z : (t + 1) * Z, :].T
    ones = jnp.ones((8, Z), f32)
    zeros = jnp.zeros((8, Z), f32)

    def cell(t, step):
        return et[t, pl.ds(step, 8, stride=span), :]

    starts = []
    for t in range(tiles):
        p11, p12, p21, p22 = ones, zeros, zeros, ones
        for step in range(span):
            e = cell(t, step)
            p21 = p21 + e * p11
            p22 = p22 + e * p12
            p11 = p11 + p21
            p12 = p12 + p22
        for shift in (1, 2, 4):
            keep = seg < shift
            q11 = jnp.where(keep, 1.0, pltpu.roll(p11, shift, 0))
            q12 = jnp.where(keep, 0.0, pltpu.roll(p12, shift, 0))
            q21 = jnp.where(keep, 0.0, pltpu.roll(p21, shift, 0))
            q22 = jnp.where(keep, 1.0, pltpu.roll(p22, shift, 0))
            p11, p12, p21, p22 = (
                p11 * q11 + p12 * q21,
                p11 * q12 + p12 * q22,
                p21 * q11 + p22 * q21,
                p21 * q12 + p22 * q22,
            )
        theta = jnp.where(seg < 1, 1.0, pltpu.roll(p11 + p12, 1, 0))
        delta = jnp.where(seg < 1, 1.0, pltpu.roll(p21 + p22, 1, 0))
        starts.append((theta, delta))
    for t in range(tiles):
        theta, delta = starts[t]
        for step in range(span):
            delta = delta + cell(t, step) * theta
            theta = theta + delta
            et[t, pl.ds(step, 8, stride=span), :] = theta
    lane = lax.broadcasted_iota(jnp.int32, (Z, Z), 1)
    for t in range(tiles):
        rows = pl.ds(t * Z, Z)
        theta = et[t].T
        before = jnp.where(lane < 1, 1.0, pltpu.roll(theta, 1, 1))
        zt[rows, :] = before
        zw[rows, :] = 1.0 / (theta * before)
        zo[rows, :] = before * ec[rows, :]

    row = lax.rem(lax.broadcasted_iota(jnp.int32, (2 * Z, Z), 0), Z)
    col = lax.broadcasted_iota(jnp.int32, (2 * Z, Z), 1)
    tri[0] = (row <= col).astype(f32).astype(jnp.bfloat16)
    tri[1] = (row >= col).astype(f32).astype(jnp.bfloat16)

    outer = (i == 0) | (i == NI - 1)
    pl.semaphore_wait(barrier, NI + NJ - 2 + jnp.where(outer, NI - 1, 0))

    def exchange(src, dst, slot, rows, k, axis):
        here = j if axis == "gy" else i
        return pltpu.make_async_remote_copy(
            src_ref=src.at[pl.ds(pl.multiple_of(k * rows, 8), rows), :],
            dst_ref=dst.at[pl.ds(pl.multiple_of(here * rows, 8), rows), :],
            send_sem=sent.at[slot],
            recv_sem=came.at[slot],
            device_id={axis: k},
            device_id_type=MESH,
        )

    def whole_round(src, dst, slot, rows, axis):
        total = pl.ds(0, rows * ((NJ if axis == "gy" else NI) - 1))
        return pltpu.make_async_remote_copy(
            src_ref=src.at[total, :],
            dst_ref=dst.at[total, :],
            send_sem=sent.at[slot],
            recv_sem=came.at[slot],
            device_id={axis: jnext if axis == "gy" else inext},
            device_id_type=MESH,
        )

    def peers(axis):
        if axis == "gy":
            return [lax.rem(j // 4 + a, 4) * 4 + lax.rem(j + b, 4) for a, b in FAR]
        return [lax.rem(i // 2 + a, 4) * 2 + lax.rem(i + b, 2) for a, b in FAR_X]

    def send_all(src, dst, slot, rows, axis):
        here = j if axis == "gy" else i
        mine = pl.ds(pl.multiple_of(here * rows, 8), rows)
        for k in peers(axis):
            exchange(src, dst, slot, rows, k, axis).start()
        dst[mine, :] = src[mine, :]

    def recv_all(src, dst, slot, rows, axis):
        whole_round(src, dst, slot, rows, axis).wait_recv()

    def sent_all(src, dst, slot, rows, axis):
        whole_round(src, dst, slot, rows, axis).wait_send()

    coup_y = (csy, rcy, 0, 8, "gy")
    coup_x = (csx, rcx, 1, 8, "gx")
    tot_y = (sty, tty, 2, PACK, "gy")
    ret_y = (oty, rty, 3, PACK, "gy")
    tot_x = (stx, ttx, 4, PACK, "gx")
    ret_x = (otx, rtx, 5, PACK, "gx")

    def face(src, dst, slot, part, axis, to):
        return pltpu.make_async_remote_copy(
            src_ref=src.at[part], dst_ref=dst.at[part], send_sem=sent.at[slot], recv_sem=came.at[slot],
            device_id={axis: to}, device_id_type=MESH,
        )

    def both(src, dst, slot):
        return pltpu.make_async_remote_copy(
            src_ref=src, dst_ref=dst, send_sem=sent.at[slot], recv_sem=came.at[slot],
            device_id={"gy": jnext}, device_id_type=MESH,
        )

    edges = [
        face(fse, fre, 6, 0, "gy", jprev),
        face(fse, fre, 6, 1, "gy", jnext),
    ]
    faces = [
        face(fsy, fry, 7, 0, "gy", jprev),
        face(fsy, fry, 7, 1, "gy", jnext),
        face(fsx, frx, 8, 0, "gx", iprev),
        face(fsx, frx, 8, 1, "gx", inext),
    ]
    pairs = [both(fse, fre, 6), both(fsy, fry, 7), both(fsx, frx, 8)]
    send_all(*coup_y)
    fse[0] = ec[pl.ds(0, X, stride=Y), :]
    fse[1] = ec[pl.ds(Y - 1, X, stride=Y), :]
    for e in edges:
        e.start()

    def z_and_y(q):
        rows = pl.ds(q * 8 * Y, 8 * Y)
        fields[q].wait()
        scale, weight, finish = zt[rows, :], zw[rows, :], zo[rows, :]
        sums = [
            jnp.dot(split(cot[c, rows, :] * scale), tri[0], preferred_element_type=f32) for c in range(C)
        ]
        for c in range(C):
            whole = jnp.dot(split(sums[c] * weight), tri[1], preferred_element_type=f32)
            zb[c, rows, :] = whole * finish
        xs = pl.ds(q * 8, 8)
        heads = [jnp.zeros((8, Z), f32) for _ in range(C)]
        tails = [jnp.zeros((8, Z), f32) for _ in range(C)]
        for y in range(Y):
            a, b = ya[y, xs, :], yb[y, xs, :]
            for c in range(C):
                value = zb[c, pl.ds(q * 8 * Y + y, 8, stride=Y), :]
                heads[c] = heads[c] + a * value
                tails[c] = tails[c] + b * value
                yf[c, y, xs, :] = tails[c]
        at = (q % 2) * 8 * PACK + (q // 2) * C
        for c in range(C):
            sty[pl.ds(at + c, 8, stride=PACK), :] = heads[c]
            sty[pl.ds(at + HALF + c, 8, stride=PACK), :] = tails[c]

    def wave(w):
        for b in (2, 1, 3, 0):
            for a in range(2):
                k = 8 * w + 4 * a + lax.rem(j + b, 4)
                if b:
                    exchange(*tot_y[:4], k, "gy").start()
                else:

                    @pl.when(k != j)
                    def _():
                        exchange(*tot_y[:4], k, "gy").start()

    z_and_y(0)
    z_and_y(2)
    loads[2].start()
    loads[3].start()
    wave(0)
    z_and_y(1)
    z_and_y(3)
    wave(1)
    mine_y = pl.ds(pl.multiple_of(j * PACK, 8), PACK)
    tty[mine_y, :] = sty[mine_y, :]

    def x_factor():
        rows = pl.ds(0, 32)
        one = jnp.ones((32, Z), f32)

        def up(x, carry):
            theta, delta = carry
            xb[x, rows, :] = theta
            delta = delta + xe[x, rows, :] * theta
            return theta + delta, delta

        theta, _ = lax.fori_loop(0, X, up, (one, one), unroll=8)
        rn = 1.0 / theta
        xr[rows, :] = rn

        def down(step, carry):
            x = X - 1 - step
            phi, delta, after, _ = carry
            cell = xe[x, rows, :]
            a = phi * rn
            b = xb[x, rows, :] * rn
            xa[x, rows, :] = a
            xb[x, rows, :] = b
            xw[x, rows, :] = 1.0 / (b * after)
            xo[x, rows, :] = b * cell
            delta = delta + cell * phi
            return phi + delta, delta, b, a

        _, _, _, first = lax.fori_loop(0, X, down, (one, one, one, one), unroll=8)
        return first, rn

    pairs[0].wait_recv()
    for x in range(X):
        xe[x, 0:Y, :] = ec[x * Y : (x + 1) * Y, :]
        xe[x, 16:24, :] = jnp.broadcast_to(fre[1, x : x + 1, :], (8, Z))
        xe[x, 24:32, :] = jnp.broadcast_to(fre[0, x : x + 1, :], (8, Z))
    first, rn = x_factor()
    last = xb[X - 1, 0:Y, :]
    for r in range(2):
        csx[pl.ds(r, 8, stride=8), :] = first[r * 8 : r * 8 + 8]
        csx[pl.ds(2 + r, 8, stride=8), :] = rn[r * 8 : r * 8 + 8]
        csx[pl.ds(4 + r, 8, stride=8), :] = last[r * 8 : r * 8 + 8]

    loads[2].wait()
    loads[3].wait()
    fsy[0] = upw[1, pl.ds(0, X, stride=Y), :].astype(f32) * cou[1, pl.ds(0, X, stride=Y), :]
    fsy[1] = (1.0 - upw[1, pl.ds(Y - 1, X, stride=Y), :].astype(f32)) * cou[1, pl.ds(Y - 1, X, stride=Y), :]
    fsx[0] = upw[0, 0:Y, :].astype(f32) * cou[0, 0:Y, :] * ec[0:Y, :]
    fsx[1] = (1.0 - upw[0, LINES - Y : LINES, :].astype(f32)) * cou[0, LINES - Y : LINES, :] * ec[LINES - Y : LINES, :]

    send_all(*coup_x)
    for f in faces:
        f.start()

    def reduce_factor(count, couplings, factors):
        def pair(base, t):
            return jnp.concatenate(
                [
                    jnp.broadcast_to(couplings[pl.ds(base + 2 * t, 1), :], (C, Z)),
                    jnp.broadcast_to(couplings[pl.ds(base + 2 * t + 1, 1), :], (C, Z)),
                ],
                axis=0,
            )

        edge = jnp.zeros((HALF, Z), f32)
        for m in range(count):
            a1, b1, bn = pair(m * 8, 0), pair(m * 8, 1), pair(m * 8, 2)
            alpha = 1.0 / (1.0 - a1 * edge)
            alpha_a = a1 * alpha
            forward = b1 * alpha
            back = b1 * edge
            factors[0, m, 0:HALF, :] = alpha
            factors[1, m, 0:HALF, :] = alpha_a
            factors[2, m, 0:HALF, :] = forward
            factors[3, m, 0:HALF, :] = edge
            factors[4, m, 0:HALF, :] = back * alpha
            factors[5, m, 0:HALF, :] = b1 + back * alpha_a
            edge = bn + back * forward

    def reduce_solve(count, totals, factors, results):
        gain = jnp.zeros((HALF, Z), f32)
        for m in range(count):
            head = totals[m * PACK : m * PACK + HALF, :]
            tail = totals[m * PACK + HALF : m * PACK + PACK, :]
            gl[0, m, 0:HALF, :] = gain
            gl[1, m, 0:HALF, :] = factors[0, m, 0:HALF, :] * head + factors[1, m, 0:HALF, :] * gain
            gain = tail + factors[4, m, 0:HALF, :] * head + factors[5, m, 0:HALF, :] * gain
        later = jnp.zeros((HALF, Z), f32)
        for m in range(count - 1, -1, -1):
            results[m * PACK + HALF : m * PACK + PACK, :] = later
            later = gl[1, m, 0:HALF, :] + factors[2, m, 0:HALF, :] * later
            results[m * PACK : m * PACK + HALF, :] = gl[0, m, 0:HALF, :] + factors[3, m, 0:HALF, :] * later

    recv_all(*coup_y)
    reduce_factor(NJ, rcy, ky)

    recv_all(*tot_y)
    reduce_solve(NJ, tty, ky, oty)
    send_all(*ret_y)

    recv_all(*coup_x)
    reduce_factor(NI, rcx, kx)
    pairs[1].wait_recv()
    pairs[2].wait_recv()

    low_ok = jnp.where(j > 0, 1.0, 0.0).astype(f32)
    high_ok = jnp.where(j < NJ - 1, 1.0, 0.0).astype(f32)
    lane16 = lax.broadcasted_iota(jnp.int32, (Y, Z), 1)

    def coefficients(x, _):
        rows = pl.ds(pl.multiple_of(x * Y, Y), Y)
        shifted = pl.ds(pl.multiple_of(x * Y + Y, Y), Y)
        padded = pl.ds(pl.multiple_of(x * PAD + 8, 8), Y)
        flux = [cou[d, rows, :] for d in range(3)]
        ahead = [upw[d, rows, :].astype(f32) * flux[d] for d in range(3)]
        behind = [flux[d] - ahead[d] for d in range(3)]
        c0[rows, :] = 1.0 + (behind[0] - ahead[0]) + (behind[1] - ahead[1]) + (behind[2] - ahead[2])
        ax[shifted, :] = ahead[0]
        bx[shifted, :] = behind[0]
        ayp[padded, :] = ahead[1]
        byp[padded, :] = behind[1]
        azn[rows, :] = jnp.where(lane16 < Z - 1, pltpu.roll(ahead[2], Z - 1, 1), 0.0)
        bzp[rows, :] = jnp.where(lane16 > 0, pltpu.roll(behind[2], 1, 1), 0.0)
        return 0

    lax.fori_loop(0, X, coefficients, 0, unroll=8)
    bx[0:Y, :] = frx[1]
    ax[(X + 1) * Y : (X + 2) * Y, :] = frx[0]
    byp[pl.ds(7, X, stride=PAD), :] = fry[1] * low_ok
    ayp[pl.ds(PAD, X, stride=PAD), :] = fry[0] * high_ok
    ayh[...] = jnp.zeros_like(ayh)

    recv_all(*ret_y)

    for q in ORDER:
        xs = pl.ds(q * 8, 8)
        at = (q % 2) * 8 * PACK + (q // 2) * C
        below, above, live = [], [], []
        for c in range(C):
            left = rty[pl.ds(at + c, 8, stride=PACK), :]
            right = rty[pl.ds(at + HALF + c, 8, stride=PACK), :]
            ayh[pl.ds(q * 8 * 16 + c, 8, stride=16), :] = left * fre[1, xs, :]
            ayh[pl.ds(q * 8 * 16 + 8 + c, 8, stride=16), :] = right * fre[0, xs, :]
            below.append(left * yr[xs, :])
            live.append(right)
        for y in range(Y - 1, -1, -1):
            weight, finish = yw[y, xs, :], yo[y, xs, :]
            for c in range(C):
                live[c] = live[c] + weight * (yf[c, y, xs, :] + below[c])
                ay[c, pl.ds(q * 8 * Y + y, 8, stride=Y), :] = live[c] * finish

    def x_totals(x, carry):
        heads, tails, halo = carry
        rows = pl.ds(pl.multiple_of(x * Y, Y), Y)
        a, b = xa[x, 0:Y, :], xb[x, 0:Y, :]
        new_heads, new_tails = [], []
        for c in range(C):
            value = ay[c, rows, :]
            new_heads.append(heads[c] + a * value)
            tail = tails[c] + b * value
            new_tails.append(tail)
            ay[c, rows, :] = tail
        halo = halo + xb[x, 16:32, :] * ayh[rows, :]
        ayh[rows, :] = halo
        return tuple(new_heads), tuple(new_tails), halo

    none = jnp.zeros((Y, Z), f32)
    heads, tails, _ = lax.fori_loop(0, X, x_totals, ((none,) * C, (none,) * C, none), unroll=8)
    for c in range(C):
        for r in range(2):
            stx[pl.ds(r * C + c, 8, stride=PACK), :] = heads[c][r * 8 : r * 8 + 8]
            stx[pl.ds(HALF + r * C + c, 8, stride=PACK), :] = tails[c][r * 8 : r * 8 + 8]
    send_all(*tot_x)
    sent_all(*coup_y)
    sent_all(*coup_x)
    sent_all(*tot_y)
    sent_all(*ret_y)
    for pair in pairs:
        pair.wait_send()
    recv_all(*tot_x)
    reduce_solve(NI, ttx, kx, otx)
    send_all(*ret_x)

    def extra(m, slot, to):
        return pltpu.make_async_remote_copy(
            src_ref=otx.at[pl.ds(pl.multiple_of(m * PACK, 8), PACK), :],
            dst_ref=ext.at[slot, pl.ds(0, PACK), :],
            send_sem=sent.at[9],
            recv_sem=came.at[9],
            device_id=(m, to),
            device_id_type=MESH,
        )

    @pl.when(i == 0)
    def _():
        for m in range(NI):
            extra(m, 1, jprev).start()

    @pl.when(i == NI - 1)
    def _():
        for m in range(NI):
            extra(m, 0, jnext).start()

    sent_all(*tot_x)
    recv_all(*ret_x)
    extras = pltpu.make_async_remote_copy(
        src_ref=otx,
        dst_ref=rtx.at[pl.ds(0, 2 * PACK), :],
        send_sem=sent.at[9],
        recv_sem=came.at[9],
        device_id={"gy": jnext},
        device_id_type=MESH,
    )
    extras.wait_recv()

    lefts, rights = [], []
    for c in range(C):
        left = jnp.concatenate([rtx[pl.ds(r * C + c, 8, stride=PACK), :] for r in range(2)], axis=0)
        right = jnp.concatenate([rtx[pl.ds(HALF + r * C + c, 8, stride=PACK), :] for r in range(2)], axis=0)
        fb[pl.ds(c * PITCH + 8, Y), :] = left
        fb[pl.ds(c * PITCH + (X + 1) * PAD + 8, Y), :] = right
        lefts.append(left * xr[0:Y, :])
        rights.append(right)
    left_halo = jnp.concatenate([ext[0, 6:14, :], ext[1, 0:8, :]], axis=0) * xr[16:32, :]
    right_halo = jnp.concatenate([ext[0, 18:26, :], ext[1, 12:20, :]], axis=0)

    def x_finish(step, carry):
        x = X - 1 - step
        live, halo = carry
        rows = pl.ds(pl.multiple_of(x * Y, Y), Y)
        weight, finish = xw[x, 0:Y, :], xo[x, 0:Y, :]
        out = []
        for c in range(C):
            value = live[c] + weight * (ay[c, rows, :] + lefts[c])
            fb[pl.ds(pl.multiple_of(c * PITCH + (x + 1) * PAD + 8, 8), Y), :] = value * finish
            out.append(value)
        halo = halo + xw[x, 16:32, :] * (ayh[rows, :] + left_halo)
        edge = halo * xo[x, 16:32, :]
        fb[pl.ds((x + 1) * PAD + 7, 8, stride=PITCH), :] = edge[0:8]
        fb[pl.ds((x + 2) * PAD, 8, stride=PITCH), :] = edge[8:16]
        return tuple(out), halo

    lax.fori_loop(0, X, x_finish, (tuple(rights), right_halo), unroll=4)

    sent_all(*ret_x)

    @pl.when(outer)
    def _():
        extras.wait_send()


def advection(fb, c0, ax, bx, ayp, byp, azn, bzp, out_h, out, sem):
    def advect(x, _):
        rows = pl.ds(pl.multiple_of(x * Y, Y), Y)
        middle = c0[rows, :]
        from_x, to_x = bx[rows, :], ax[pl.ds(pl.multiple_of((x + 2) * Y, Y), Y), :]
        from_y, to_y = byp[pl.ds(x * PAD + 7, Y), :], ayp[pl.ds(x * PAD + 9, Y), :]
        from_z, to_z = bzp[rows, :], azn[rows, :]
        for c in range(C):
            at = c * PITCH + (x + 1) * PAD + 8
            value = fb[pl.ds(pl.multiple_of(at, 8), Y), :]
            result = middle * value
            result += to_x * fb[pl.ds(pl.multiple_of(at + PAD, 8), Y), :]
            result -= from_x * fb[pl.ds(pl.multiple_of(at - PAD, 8), Y), :]
            result += to_y * fb[pl.ds(at + 1, Y), :]
            result -= from_y * fb[pl.ds(at - 1, Y), :]
            result += to_z * pltpu.roll(value, Z - 1, 1)
            result -= from_z * pltpu.roll(value, 1, 1)
            out[c, rows, :] = result
        return 0

    stores = []
    for part in range(4):
        lax.fori_loop(part * 8, part * 8 + 8, advect, 0, unroll=8)
        rows = pl.ds(part * 8 * Y, 8 * Y)
        store = pltpu.make_async_copy(out.at[:, rows, :], out_h.at[:, rows, :], sem.at[part])
        store.start()
        stores.append(store)
    for store in stores:
        store.wait()


def on_device(cotangent, diffusion, phase, courant, upwind):
    def vm(*shape, dtype=f32):
        return pltpu.VMEM(shape, dtype)

    dma = pltpu.SemaphoreType.DMA
    scratch = [
        vm(C, LINES, Z), vm(LINES, Z), vm(LINES, Z, dtype=jnp.int32), vm(3, LINES, Z), vm(3, LINES, Z, dtype=jnp.int32),
        vm(LINES, Z),
        vm(LINES // Z, Z, Z), vm(LINES, Z), vm(LINES, Z), vm(LINES, Z), vm(C, LINES, Z), vm(2, 2 * Z, Z, dtype=jnp.bfloat16),
        vm(Y, X, Z), vm(Y, X, Z), vm(Y, X, Z), vm(Y, X, Z), vm(X, Z), vm(C, Y, X, Z), vm(C, LINES, Z), vm(X * 16, Z),
        vm(X, 32, Z), vm(X, 32, Z), vm(X, 32, Z), vm(X, 32, Z), vm(X, 32, Z), vm(32, Z),
        vm(NJ * 8, Z), vm(NI * 8, Z), vm(NJ * 8, Z), vm(NI * 8, Z), vm(6, NJ, 16, Z), vm(6, NI, 16, Z), vm(2, NJ, 16, Z),
        vm(NJ * PACK, Z), vm(NJ * PACK, Z), vm(NJ * PACK, Z), vm(NJ * PACK, Z),
        vm(NI * PACK, Z), vm(NI * PACK, Z), vm(NI * PACK, Z), vm(NI * PACK, Z), vm(2, 32, Z),
        vm(2, X, Z), vm(2, X, Z), vm(2, X, Z), vm(2, X, Z), vm(2, Y, Z), vm(2, Y, Z),
        dma((8,)), dma((10,)), dma((10,)),
    ]
    vmem = pl.BlockSpec(memory_space=pltpu.VMEM)
    shapes = [(8 * PITCH, Z), (LINES, Z), (LINES + 2 * Y, Z), (LINES + 2 * Y, Z), (X * PAD + 8, Z), (X * PAD + 8, Z), (LINES, Z), (LINES, Z)]
    parts = pl.pallas_call(
        body,
        out_shape=[pltpu.VMEM(shape, f32) for shape in shapes],
        in_specs=[pl.BlockSpec(memory_space=pltpu.HBM)] * 5,
        out_specs=[vmem] * len(shapes),
        scratch_shapes=scratch,
        compiler_params=pltpu.CompilerParams(
            collective_id=0, has_side_effects=True, vmem_limit_bytes=40 * 1024 * 1024
        ),
    )(
        *(
            pltpu.with_memory_space_constraint(given, pltpu.HBM)
            for given in (
                cotangent.reshape(C, LINES, Z),
                diffusion.reshape(LINES, Z),
                phase.reshape(LINES, Z),
                courant.reshape(3, LINES, Z),
                upwind.reshape(3, LINES, Z),
            )
        )
    )
    out = pl.pallas_call(
        advection,
        out_shape=jax.ShapeDtypeStruct((C, LINES, Z), f32),
        in_specs=[vmem] * len(shapes),
        out_specs=pl.BlockSpec(memory_space=pl.ANY),
        scratch_shapes=[vm(C, LINES, Z), dma((4,))],
        compiler_params=pltpu.CompilerParams(vmem_limit_bytes=8 * 1024 * 1024),
    )(*(pltpu.with_memory_space_constraint(part, pltpu.VMEM) for part in parts))
    return out.reshape(C, X, Y, Z)


def solution(mesh):
    placed = (
        P(None, "gx", "gy", None),
        P("gx", "gy", None),
        P("gx", "gy", None),
        P(None, "gx", "gy", None),
        P(None, "gx", "gy", None),
    )
    return jax.shard_map(
        on_device, mesh=mesh, in_specs=placed, out_specs=P(None, "gx", "gy", None), check_vma=False
    )
```

```python
import functools

import jax
import jax.numpy as jnp
from jax import lax
from jax.experimental import pallas as pl
from jax.experimental.pallas import tpu as pltpu
from jax.sharding import PartitionSpec as P

MESH = pl.DeviceIdType.MESH
C, X, Y, Z = 6, 32, 16, 128
NI, NJ = 8, 16
LINES = X * Y
PAD = 24
PLANES = X + 2
PITCH = PLANES * PAD + 8
HALF = C * 2
PACK = 2 * HALF
HALF_X = HALF + 2
PACK_X = 2 * HALF_X
STEP_X = 32
f32 = jnp.float32
FAR = sorted(((a, b) for a in range(4) for b in range(4) if a or b), key=lambda d: -min(d[0], 4 - d[0]) - min(d[1], 4 - d[1]))
ORDER = (0, 2, 1, 3)
FAR_X = [(2, 1), (2, 0), (3, 1), (1, 1), (3, 0), (1, 0), (0, 1)]


def split(values):
    high = values.astype(jnp.bfloat16)
    low = (values - high.astype(f32)).astype(jnp.bfloat16)
    return jnp.concatenate([high, low], axis=1)


def body(
    cot_h, dif_h, pha_h, cou_h, upw_h,
    fb, c0, ax, bx, ayp, byp, azn, bzp,
    cot, dif, pha, cou, upw, ec,
    et, zt, zw, zo, zb, tri,
    yb, ya, yw, yo, yr, yf, ay, ayh,
    xe, xb, xa, xw, xo, xr,
    csy, csx, rcy, rcx, ky, kx, gl,
    sty, tty, oty, rty, stx, ttx, otx, rtx, ext,
    fse, fre, fsy, fry, fsx, frx,
    in_sem,
    sent, came,
):
    i = lax.axis_index("gx")
    j = lax.axis_index("gy")
    inext, iprev = lax.rem(i + 1, NI), lax.rem(i + NI - 1, NI)
    jnext, jprev = lax.rem(j + 1, NJ), lax.rem(j + NJ - 1, NJ)

    loads = [
        pltpu.make_async_copy(dif_h, dif, in_sem.at[0]),
        pltpu.make_async_copy(pha_h, pha, in_sem.at[1]),
        pltpu.make_async_copy(cou_h, cou, in_sem.at[2]),
        pltpu.make_async_copy(upw_h, upw, in_sem.at[3]),
    ]
    quarters = [pl.ds(q * 8 * Y, 8 * Y) for q in range(4)]
    fields = [
        pltpu.make_async_copy(cot_h.at[:, rows, :], cot.at[:, rows, :], in_sem.at[4 + q])
        for q, rows in enumerate(quarters)
    ]
    loads[0].start()
    loads[1].start()
    for q in ORDER:
        fields[q].start()

    barrier = pltpu.get_barrier_semaphore()

    def greet_y(d, _):
        pl.semaphore_signal(barrier, inc=1, device_id=(i, lax.rem(j + d, NJ)), device_id_type=MESH)
        return 0

    def greet_x(d, _):
        pl.semaphore_signal(barrier, inc=1, device_id=(lax.rem(i + d, NI), j), device_id_type=MESH)
        return 0

    lax.fori_loop(1, NJ, greet_y, 0)
    lax.fori_loop(1, NI, greet_x, 0)

    loads[0].wait()
    loads[1].wait()
    ec[...] = 1.0 / (dif[...] * (1.0 + 3.0 * pha[...].astype(f32)))

    for q in range(X // 8):
        xs = pl.ds(q * 8, 8)
        cells = [ec[pl.ds(q * 8 * Y + y, 8, stride=Y), :] for y in range(Y)]
        theta = jnp.ones((8, Z), f32)
        delta = jnp.ones((8, Z), f32)
        for y in range(Y):
            yb[y, xs, :] = theta
            delta = delta + cells[y] * theta
            theta = theta + delta
        rn = 1.0 / theta
        yr[xs, :] = rn
        phi = jnp.ones((8, Z), f32)
        delta = jnp.ones((8, Z), f32)
        after = jnp.ones((8, Z), f32)
        at = (q % 2) * 8 * 8 + q // 2
        for y in range(Y - 1, -1, -1):
            a = phi * rn
            b = yb[y, xs, :] * rn
            ya[y, xs, :] = a
            yb[y, xs, :] = b
            yw[y, xs, :] = 1.0 / (b * after)
            yo[y, xs, :] = b * cells[y]
            if y == Y - 1:
                csy[pl.ds(at + 4, 8, stride=8), :] = b
            if y == 0:
                csy[pl.ds(at, 8, stride=8), :] = a
            after = b
            delta = delta + cells[y] * phi
            phi = phi + delta
        csy[pl.ds(at + 2, 8, stride=8), :] = rn

    seg = lax.broadcasted_iota(jnp.int32, (8, Z), 0)
    span = Z // 8
    tiles = LINES // Z
    for t in range(tiles):
        et[t] = ec[t * Z : (t + 1) * Z, :].T
    ones = jnp.ones((8, Z), f32)
    zeros = jnp.zeros((8, Z), f32)

    def cell(t, step):
        return et[t, pl.ds(step, 8, stride=span), :]

    starts = []
    for t in range(tiles):
        p11, p12, p21, p22 = ones, zeros, zeros, ones
        for step in range(span):
            e = cell(t, step)
            p21 = p21 + e * p11
            p22 = p22 + e * p12
            p11 = p11 + p21
            p12 = p12 + p22
        for shift in (1, 2, 4):
            keep = seg < shift
            q11 = jnp.where(keep, 1.0, pltpu.roll(p11, shift, 0))
            q12 = jnp.where(keep, 0.0, pltpu.roll(p12, shift, 0))
            q21 = jnp.where(keep, 0.0, pltpu.roll(p21, shift, 0))
            q22 = jnp.where(keep, 1.0, pltpu.roll(p22, shift, 0))
            p11, p12, p21, p22 = (
                p11 * q11 + p12 * q21,
                p11 * q12 + p12 * q22,
                p21 * q11 + p22 * q21,
                p21 * q12 + p22 * q22,
            )
        theta = jnp.where(seg < 1, 1.0, pltpu.roll(p11 + p12, 1, 0))
        delta = jnp.where(seg < 1, 1.0, pltpu.roll(p21 + p22, 1, 0))
        starts.append((theta, delta))
    for t in range(tiles):
        theta, delta = starts[t]
        for step in range(span):
            delta = delta + cell(t, step) * theta
            theta = theta + delta
            et[t, pl.ds(step, 8, stride=span), :] = theta
    lane = lax.broadcasted_iota(jnp.int32, (Z, Z), 1)
    for t in range(tiles):
        rows = pl.ds(t * Z, Z)
        theta = et[t].T
        before = jnp.where(lane < 1, 1.0, pltpu.roll(theta, 1, 1))
        zt[rows, :] = before
        zw[rows, :] = 1.0 / (theta * before)
        zo[rows, :] = before * ec[rows, :]

    row = lax.rem(lax.broadcasted_iota(jnp.int32, (2 * Z, Z), 0), Z)
    col = lax.broadcasted_iota(jnp.int32, (2 * Z, Z), 1)
    tri[0] = (row <= col).astype(f32).astype(jnp.bfloat16)
    tri[1] = (row >= col).astype(f32).astype(jnp.bfloat16)

    pl.semaphore_wait(barrier, NI + NJ - 2)

    def exchange(src, dst, slot, pitch, rows, k, axis):
        here = j if axis == "gy" else i
        return pltpu.make_async_remote_copy(
            src_ref=src.at[pl.ds(pl.multiple_of(k * pitch, 8), rows), :],
            dst_ref=dst.at[pl.ds(pl.multiple_of(here * pitch, 8), rows), :],
            send_sem=sent.at[slot],
            recv_sem=came.at[slot],
            device_id={axis: k},
            device_id_type=MESH,
        )

    def whole_round(src, dst, slot, pitch, rows, axis):
        total = pl.ds(0, rows * ((NJ if axis == "gy" else NI) - 1))
        return pltpu.make_async_remote_copy(
            src_ref=src.at[total, :],
            dst_ref=dst.at[total, :],
            send_sem=sent.at[slot],
            recv_sem=came.at[slot],
            device_id={axis: jnext if axis == "gy" else inext},
            device_id_type=MESH,
        )

    def peers(axis):
        if axis == "gy":
            return [lax.rem(j // 4 + a, 4) * 4 + lax.rem(j + b, 4) for a, b in FAR]
        return [lax.rem(i // 2 + a, 4) * 2 + lax.rem(i + b, 2) for a, b in FAR_X]

    def send_all(src, dst, slot, pitch, rows, axis):
        here = j if axis == "gy" else i
        mine = pl.ds(pl.multiple_of(here * pitch, 8), rows)
        for k in peers(axis):
            exchange(src, dst, slot, pitch, rows, k, axis).start()
        dst[mine, :] = src[mine, :]

    def recv_all(src, dst, slot, pitch, rows, axis):
        whole_round(src, dst, slot, pitch, rows, axis).wait_recv()

    def sent_all(src, dst, slot, pitch, rows, axis):
        whole_round(src, dst, slot, pitch, rows, axis).wait_send()

    coup_y = (csy, rcy, 0, 8, 8, "gy")
    coup_x = (csx, rcx, 1, 16, 16, "gx")
    tot_y = (sty, tty, 2, PACK, PACK, "gy")
    ret_y = (oty, rty, 3, PACK, PACK, "gy")
    tot_x = (stx, ttx, 4, STEP_X, PACK_X, "gx")
    ret_x = (otx, rtx, 5, STEP_X, PACK_X, "gx")

    def face(src, dst, slot, part, axis, to):
        return pltpu.make_async_remote_copy(
            src_ref=src.at[part], dst_ref=dst.at[part], send_sem=sent.at[slot], recv_sem=came.at[slot],
            device_id={axis: to}, device_id_type=MESH,
        )

    def both(src, dst, slot):
        return pltpu.make_async_remote_copy(
            src_ref=src, dst_ref=dst, send_sem=sent.at[slot], recv_sem=came.at[slot],
            device_id={"gy": jnext}, device_id_type=MESH,
        )

    edges = [
        face(fse, fre, 6, 0, "gy", jprev),
        face(fse, fre, 6, 1, "gy", jnext),
    ]
    faces = [
        face(fsy, fry, 7, 0, "gy", jprev),
        face(fsy, fry, 7, 1, "gy", jnext),
        face(fsx, frx, 8, 0, "gx", iprev),
        face(fsx, frx, 8, 1, "gx", inext),
    ]
    pairs = [both(fse, fre, 6), both(fsy, fry, 7), both(fsx, frx, 8)]
    send_all(*coup_y)
    fse[0] = ec[pl.ds(0, X, stride=Y), :]
    fse[1] = ec[pl.ds(Y - 1, X, stride=Y), :]
    for e in edges:
        e.start()

    def z_and_y(q):
        rows = pl.ds(q * 8 * Y, 8 * Y)
        fields[q].wait()
        scale, weight, finish = zt[rows, :], zw[rows, :], zo[rows, :]
        sums = [
            jnp.dot(split(cot[c, rows, :] * scale), tri[0], preferred_element_type=f32) for c in range(C)
        ]
        for c in range(C):
            whole = jnp.dot(split(sums[c] * weight), tri[1], preferred_element_type=f32)
            zb[c, rows, :] = whole * finish
        xs = pl.ds(q * 8, 8)
        heads = [jnp.zeros((8, Z), f32) for _ in range(C)]
        tails = [jnp.zeros((8, Z), f32) for _ in range(C)]
        for y in range(Y):
            a, b = ya[y, xs, :], yb[y, xs, :]
            for c in range(C):
                value = zb[c, pl.ds(q * 8 * Y + y, 8, stride=Y), :]
                heads[c] = heads[c] + a * value
                tails[c] = tails[c] + b * value
                yf[c, y, xs, :] = tails[c]
        at = (q % 2) * 8 * PACK + (q // 2) * C
        for c in range(C):
            sty[pl.ds(at + c, 8, stride=PACK), :] = heads[c]
            sty[pl.ds(at + HALF + c, 8, stride=PACK), :] = tails[c]

    def wave(w):
        for b in (2, 1, 3, 0):
            for a in range(2):
                k = 8 * w + 4 * a + lax.rem(j + b, 4)
                if b:
                    exchange(*tot_y[:5], k, "gy").start()
                else:

                    @pl.when(k != j)
                    def _():
                        exchange(*tot_y[:5], k, "gy").start()

    z_and_y(0)
    z_and_y(2)
    loads[2].start()
    loads[3].start()
    wave(0)
    z_and_y(1)
    z_and_y(3)
    wave(1)
    mine_y = pl.ds(pl.multiple_of(j * PACK, 8), PACK)
    tty[mine_y, :] = sty[mine_y, :]

    def x_factor():
        rows = pl.ds(0, 32)
        one = jnp.ones((32, Z), f32)

        def up(x, carry):
            theta, delta = carry
            xb[x, rows, :] = theta
            delta = delta + xe[x, rows, :] * theta
            return theta + delta, delta

        theta, _ = lax.fori_loop(0, X, up, (one, one), unroll=8)
        rn = 1.0 / theta
        xr[rows, :] = rn

        def down(step, carry):
            x = X - 1 - step
            phi, delta, after, _ = carry
            cell = xe[x, rows, :]
            a = phi * rn
            b = xb[x, rows, :] * rn
            xa[x, rows, :] = a
            xb[x, rows, :] = b
            xw[x, rows, :] = 1.0 / (b * after)
            xo[x, rows, :] = b * cell
            delta = delta + cell * phi
            return phi + delta, delta, b, a

        _, _, _, first = lax.fori_loop(0, X, down, (one, one, one, one), unroll=8)
        return first, rn

    pairs[0].wait_recv()
    for x in range(X):
        xe[x, 0:Y, :] = ec[x * Y : (x + 1) * Y, :]
        xe[x, 16:24, :] = jnp.broadcast_to(fre[1, x : x + 1, :], (8, Z))
        xe[x, 24:32, :] = jnp.broadcast_to(fre[0, x : x + 1, :], (8, Z))
    first, rn = x_factor()
    for t, part in enumerate((first, rn, xb[X - 1])):
        for r in range(2):
            csx[pl.ds(4 * t + r, 8, stride=16), :] = part[r * 8 : r * 8 + 8]
        csx[pl.ds(4 * t + 2, C, stride=16), :] = part[16 : 16 + C]
        csx[pl.ds(C * 16 + 4 * t + 2, 8 - C, stride=16), :] = part[24 : 32 - C]
        csx[pl.ds(4 * t + 3, 8, stride=16), :] = part[24:32]

    loads[2].wait()
    loads[3].wait()
    fsy[0] = upw[1, pl.ds(0, X, stride=Y), :].astype(f32) * cou[1, pl.ds(0, X, stride=Y), :]
    fsy[1] = (1.0 - upw[1, pl.ds(Y - 1, X, stride=Y), :].astype(f32)) * cou[1, pl.ds(Y - 1, X, stride=Y), :]
    fsx[0] = upw[0, 0:Y, :].astype(f32) * cou[0, 0:Y, :] * ec[0:Y, :]
    fsx[1] = (1.0 - upw[0, LINES - Y : LINES, :].astype(f32)) * cou[0, LINES - Y : LINES, :] * ec[LINES - Y : LINES, :]

    send_all(*coup_x)
    for f in faces:
        f.start()

    def reduce_factor(count, pitch, lines, half, couplings, factors):
        def spread(base, t):
            at = base + len(lines) * t
            return jnp.concatenate(
                [jnp.broadcast_to(couplings[pl.ds(at + n, 1), :], (wide, Z)) for n, wide in enumerate(lines)],
                axis=0,
            )

        edge = jnp.zeros((half, Z), f32)
        for m in range(count):
            a1, b1, bn = spread(m * pitch, 0), spread(m * pitch, 1), spread(m * pitch, 2)
            alpha = 1.0 / (1.0 - a1 * edge)
            alpha_a = a1 * alpha
            forward = b1 * alpha
            back = b1 * edge
            factors[0, m, 0:half, :] = alpha
            factors[1, m, 0:half, :] = alpha_a
            factors[2, m, 0:half, :] = forward
            factors[3, m, 0:half, :] = edge
            factors[4, m, 0:half, :] = back * alpha
            factors[5, m, 0:half, :] = b1 + back * alpha_a
            edge = bn + back * forward

    def reduce_solve(count, pitch, half, totals, factors, results):
        gain = jnp.zeros((half, Z), f32)
        for m in range(count):
            head = totals[m * pitch : m * pitch + half, :]
            tail = totals[m * pitch + half : m * pitch + 2 * half, :]
            gl[0, m, 0:half, :] = gain
            gl[1, m, 0:half, :] = factors[0, m, 0:half, :] * head + factors[1, m, 0:half, :] * gain
            gain = tail + factors[4, m, 0:half, :] * head + factors[5, m, 0:half, :] * gain
        later = jnp.zeros((half, Z), f32)
        for m in range(count - 1, -1, -1):
            results[m * pitch + half : m * pitch + 2 * half, :] = later
            later = gl[1, m, 0:half, :] + factors[2, m, 0:half, :] * later
            results[m * pitch : m * pitch + half, :] = gl[0, m, 0:half, :] + factors[3, m, 0:half, :] * later

    recv_all(*coup_y)
    reduce_factor(NJ, 8, (C, C), HALF, rcy, ky)

    recv_all(*tot_y)
    reduce_solve(NJ, PACK, HALF, tty, ky, oty)
    send_all(*ret_y)

    recv_all(*coup_x)
    reduce_factor(NI, 16, (C, C, 1, 1), HALF_X, rcx, kx)
    pairs[1].wait_recv()
    pairs[2].wait_recv()

    low_ok = jnp.where(j > 0, 1.0, 0.0).astype(f32)
    high_ok = jnp.where(j < NJ - 1, 1.0, 0.0).astype(f32)
    lane16 = lax.broadcasted_iota(jnp.int32, (Y, Z), 1)

    def coefficients(x, _):
        rows = pl.ds(pl.multiple_of(x * Y, Y), Y)
        shifted = pl.ds(pl.multiple_of(x * Y + Y, Y), Y)
        padded = pl.ds(pl.multiple_of(x * PAD + 8, 8), Y)
        flux = [cou[d, rows, :] for d in range(3)]
        ahead = [upw[d, rows, :].astype(f32) * flux[d] for d in range(3)]
        behind = [flux[d] - ahead[d] for d in range(3)]
        c0[rows, :] = 1.0 + (behind[0] - ahead[0]) + (behind[1] - ahead[1]) + (behind[2] - ahead[2])
        ax[shifted, :] = ahead[0]
        bx[shifted, :] = behind[0]
        ayp[padded, :] = ahead[1]
        byp[padded, :] = behind[1]
        azn[rows, :] = jnp.where(lane16 < Z - 1, pltpu.roll(ahead[2], Z - 1, 1), 0.0)
        bzp[rows, :] = jnp.where(lane16 > 0, pltpu.roll(behind[2], 1, 1), 0.0)
        return 0

    lax.fori_loop(0, X, coefficients, 0, unroll=8)
    bx[0:Y, :] = frx[1]
    ax[(X + 1) * Y : (X + 2) * Y, :] = frx[0]
    byp[pl.ds(7, X, stride=PAD), :] = fry[1] * low_ok
    ayp[pl.ds(PAD, X, stride=PAD), :] = fry[0] * high_ok
    ayh[...] = jnp.zeros_like(ayh)

    recv_all(*ret_y)

    for q in ORDER:
        xs = pl.ds(q * 8, 8)
        at = (q % 2) * 8 * PACK + (q // 2) * C
        below, above, live = [], [], []
        for c in range(C):
            left = rty[pl.ds(at + c, 8, stride=PACK), :]
            right = rty[pl.ds(at + HALF + c, 8, stride=PACK), :]
            ayh[pl.ds(q * 8 * 16 + c, 8, stride=16), :] = left * fre[1, xs, :]
            ayh[pl.ds(q * 8 * 16 + 8 + c, 8, stride=16), :] = right * fre[0, xs, :]
            below.append(left * yr[xs, :])
            live.append(right)
        for y in range(Y - 1, -1, -1):
            weight, finish = yw[y, xs, :], yo[y, xs, :]
            for c in range(C):
                live[c] = live[c] + weight * (yf[c, y, xs, :] + below[c])
                ay[c, pl.ds(q * 8 * Y + y, 8, stride=Y), :] = live[c] * finish

    def x_totals(x, carry):
        heads, tails, halo_head, halo = carry
        rows = pl.ds(pl.multiple_of(x * Y, Y), Y)
        a, b = xa[x, 0:Y, :], xb[x, 0:Y, :]
        new_heads, new_tails = [], []
        for c in range(C):
            value = ay[c, rows, :]
            new_heads.append(heads[c] + a * value)
            tail = tails[c] + b * value
            new_tails.append(tail)
            ay[c, rows, :] = tail
        value = ayh[rows, :]
        halo_head = halo_head + xa[x, 16:32, :] * value
        halo = halo + xb[x, 16:32, :] * value
        ayh[rows, :] = halo
        return tuple(new_heads), tuple(new_tails), halo_head, halo

    none = jnp.zeros((Y, Z), f32)
    heads, tails, *edge_pair = lax.fori_loop(0, X, x_totals, ((none,) * C, (none,) * C, none, none), unroll=8)
    for c in range(C):
        for r in range(2):
            stx[pl.ds(r * C + c, 8, stride=STEP_X), :] = heads[c][r * 8 : r * 8 + 8]
            stx[pl.ds(HALF_X + r * C + c, 8, stride=STEP_X), :] = tails[c][r * 8 : r * 8 + 8]
    for end, part in enumerate(edge_pair):
        at = end * HALF_X + HALF
        stx[pl.ds(at, C, stride=STEP_X), :] = part[0:C]
        stx[pl.ds(C * STEP_X + at, 8 - C, stride=STEP_X), :] = part[8 : 16 - C]
        stx[pl.ds(at + 1, 2 * C - 8, stride=STEP_X), :] = part[16 - C : 8 + C]
    send_all(*tot_x)
    sent_all(*coup_y)
    sent_all(*coup_x)
    sent_all(*tot_y)
    sent_all(*ret_y)
    for pair in pairs:
        pair.wait_send()
    recv_all(*tot_x)
    reduce_solve(NI, STEP_X, HALF_X, ttx, kx, otx)
    send_all(*ret_x)

    sent_all(*tot_x)
    recv_all(*ret_x)

    lefts, rights = [], []
    for c in range(C):
        left = jnp.concatenate([rtx[pl.ds(r * C + c, 8, stride=STEP_X), :] for r in range(2)], axis=0)
        right = jnp.concatenate([rtx[pl.ds(HALF_X + r * C + c, 8, stride=STEP_X), :] for r in range(2)], axis=0)
        fb[pl.ds(c * PITCH + 8, Y), :] = left
        fb[pl.ds(c * PITCH + (X + 1) * PAD + 8, Y), :] = right
        lefts.append(left * xr[0:Y, :])
        rights.append(right)
    for end in range(2):
        at = end * HALF_X + HALF
        ext[end, 0:C, :] = rtx[pl.ds(at, C, stride=STEP_X), :]
        ext[end, 8 : 16 - C, :] = rtx[pl.ds(C * STEP_X + at, 8 - C, stride=STEP_X), :]
        ext[end, 16 - C : 8 + C, :] = rtx[pl.ds(at + 1, 2 * C - 8, stride=STEP_X), :]
    left_halo = ext[0] * xr[16:32, :]
    right_halo = ext[1]

    def x_finish(step, carry):
        x = X - 1 - step
        live, halo = carry
        rows = pl.ds(pl.multiple_of(x * Y, Y), Y)
        weight, finish = xw[x, 0:Y, :], xo[x, 0:Y, :]
        out = []
        for c in range(C):
            value = live[c] + weight * (ay[c, rows, :] + lefts[c])
            fb[pl.ds(pl.multiple_of(c * PITCH + (x + 1) * PAD + 8, 8), Y), :] = value * finish
            out.append(value)
        halo = halo + xw[x, 16:32, :] * (ayh[rows, :] + left_halo)
        edge = halo * xo[x, 16:32, :]
        fb[pl.ds((x + 1) * PAD + 7, 8, stride=PITCH), :] = edge[0:8]
        fb[pl.ds((x + 2) * PAD, 8, stride=PITCH), :] = edge[8:16]
        return tuple(out), halo

    lax.fori_loop(0, X, x_finish, (tuple(rights), right_halo), unroll=4)

    sent_all(*ret_x)


def advection(fb, c0, ax, bx, ayp, byp, azn, bzp, out_h, out, sem):
    def advect(x, _):
        rows = pl.ds(pl.multiple_of(x * Y, Y), Y)
        middle = c0[rows, :]
        from_x, to_x = bx[rows, :], ax[pl.ds(pl.multiple_of((x + 2) * Y, Y), Y), :]
        from_y, to_y = byp[pl.ds(x * PAD + 7, Y), :], ayp[pl.ds(x * PAD + 9, Y), :]
        from_z, to_z = bzp[rows, :], azn[rows, :]
        for c in range(C):
            at = c * PITCH + (x + 1) * PAD + 8
            value = fb[pl.ds(pl.multiple_of(at, 8), Y), :]
            result = middle * value
            result += to_x * fb[pl.ds(pl.multiple_of(at + PAD, 8), Y), :]
            result -= from_x * fb[pl.ds(pl.multiple_of(at - PAD, 8), Y), :]
            result += to_y * fb[pl.ds(at + 1, Y), :]
            result -= from_y * fb[pl.ds(at - 1, Y), :]
            result += to_z * pltpu.roll(value, Z - 1, 1)
            result -= from_z * pltpu.roll(value, 1, 1)
            out[c, rows, :] = result
        return 0

    stores = []
    for part in range(4):
        lax.fori_loop(part * 8, part * 8 + 8, advect, 0, unroll=8)
        rows = pl.ds(part * 8 * Y, 8 * Y)
        store = pltpu.make_async_copy(out.at[:, rows, :], out_h.at[:, rows, :], sem.at[part])
        store.start()
        stores.append(store)
    for store in stores:
        store.wait()


def on_device(cotangent, diffusion, phase, courant, upwind):
    def vm(*shape, dtype=f32):
        return pltpu.VMEM(shape, dtype)

    dma = pltpu.SemaphoreType.DMA
    scratch = [
        vm(C, LINES, Z), vm(LINES, Z), vm(LINES, Z, dtype=jnp.int32), vm(3, LINES, Z), vm(3, LINES, Z, dtype=jnp.int32),
        vm(LINES, Z),
        vm(LINES // Z, Z, Z), vm(LINES, Z), vm(LINES, Z), vm(LINES, Z), vm(C, LINES, Z), vm(2, 2 * Z, Z, dtype=jnp.bfloat16),
        vm(Y, X, Z), vm(Y, X, Z), vm(Y, X, Z), vm(Y, X, Z), vm(X, Z), vm(C, Y, X, Z), vm(C, LINES, Z), vm(X * 16, Z),
        vm(X, 32, Z), vm(X, 32, Z), vm(X, 32, Z), vm(X, 32, Z), vm(X, 32, Z), vm(32, Z),
        vm(NJ * 8, Z), vm(NI * 16, Z), vm(NJ * 8, Z), vm(NI * 16, Z), vm(6, NJ, 16, Z), vm(6, NI, 16, Z), vm(2, NJ, 16, Z),
        vm(NJ * PACK, Z), vm(NJ * PACK, Z), vm(NJ * PACK, Z), vm(NJ * PACK, Z),
        vm(NI * STEP_X, Z), vm(NI * STEP_X, Z), vm(NI * STEP_X, Z), vm(NI * STEP_X, Z), vm(2, 16, Z),
        vm(2, X, Z), vm(2, X, Z), vm(2, X, Z), vm(2, X, Z), vm(2, Y, Z), vm(2, Y, Z),
        dma((8,)), dma((9,)), dma((9,)),
    ]
    vmem = pl.BlockSpec(memory_space=pltpu.VMEM)
    shapes = [(8 * PITCH, Z), (LINES, Z), (LINES + 2 * Y, Z), (LINES + 2 * Y, Z), (X * PAD + 8, Z), (X * PAD + 8, Z), (LINES, Z), (LINES, Z)]
    parts = pl.pallas_call(
        body,
        out_shape=[pltpu.VMEM(shape, f32) for shape in shapes],
        in_specs=[pl.BlockSpec(memory_space=pltpu.HBM)] * 5,
        out_specs=[vmem] * len(shapes),
        scratch_shapes=scratch,
        compiler_params=pltpu.CompilerParams(
            collective_id=0, has_side_effects=True, vmem_limit_bytes=40 * 1024 * 1024
        ),
    )(
        *(
            pltpu.with_memory_space_constraint(given, pltpu.HBM)
            for given in (
                cotangent.reshape(C, LINES, Z),
                diffusion.reshape(LINES, Z),
                phase.reshape(LINES, Z),
                courant.reshape(3, LINES, Z),
                upwind.reshape(3, LINES, Z),
            )
        )
    )
    out = pl.pallas_call(
        advection,
        out_shape=jax.ShapeDtypeStruct((C, LINES, Z), f32),
        in_specs=[vmem] * len(shapes),
        out_specs=pl.BlockSpec(memory_space=pl.ANY),
        scratch_shapes=[vm(C, LINES, Z), dma((4,))],
        compiler_params=pltpu.CompilerParams(vmem_limit_bytes=8 * 1024 * 1024),
    )(*(pltpu.with_memory_space_constraint(part, pltpu.VMEM) for part in parts))
    return out.reshape(C, X, Y, Z)


def solution(mesh):
    placed = (
        P(None, "gx", "gy", None),
        P("gx", "gy", None),
        P("gx", "gy", None),
        P(None, "gx", "gy", None),
        P(None, "gx", "gy", None),
    )
    return jax.shard_map(
        on_device, mesh=mesh, in_specs=placed, out_specs=P(None, "gx", "gy", None), check_vma=False
    )
```

```python
import functools

import jax
import jax.numpy as jnp
from jax import lax
from jax.experimental import pallas as pl
from jax.experimental.pallas import tpu as pltpu
from jax.sharding import PartitionSpec as P

MESH = pl.DeviceIdType.MESH
C, X, Y, Z = 6, 32, 16, 128
NI, NJ = 8, 16
LINES = X * Y
PAD = 24
PLANES = X + 2
PITCH = PLANES * PAD + 8
HALF = C * 2
PACK = 2 * HALF
HALF_X = HALF + 2
PACK_X = 2 * HALF_X
STEP_X = 32
f32 = jnp.float32
FAR = sorted(((a, b) for a in range(4) for b in range(4) if a or b), key=lambda d: -min(d[0], 4 - d[0]) - min(d[1], 4 - d[1]))
ORDER = (0, 2, 1, 3)
FAR_X = [(2, 1), (2, 0), (3, 1), (1, 1), (3, 0), (1, 0), (0, 1)]


def split(values):
    high = values.astype(jnp.bfloat16)
    low = (values - high.astype(f32)).astype(jnp.bfloat16)
    return jnp.concatenate([high, low], axis=1)


def body(
    cot_h, dif_h, pha_h, cou_h, upw_h,
    fb, c0, ax, bx, ayp, byp, azn, bzp,
    cot, dif, pha, cou, upw, ec,
    et, zt, zw, zo, zb, tri,
    yb, ya, yw, yo, yr, yf, ay, ayh,
    xe, xb, xa, xw, xo, xr,
    csy, csx, rcy, rcx, ky, kx, gl,
    sty, tty, oty, rty, stx, ttx, otx, rtx, ext,
    fse, fre, fsy, fry, fsx, frx,
    in_sem,
    sent, came,
):
    i = lax.axis_index("gx")
    j = lax.axis_index("gy")
    inext, iprev = lax.rem(i + 1, NI), lax.rem(i + NI - 1, NI)
    jnext, jprev = lax.rem(j + 1, NJ), lax.rem(j + NJ - 1, NJ)

    loads = [
        pltpu.make_async_copy(dif_h, dif, in_sem.at[0]),
        pltpu.make_async_copy(pha_h, pha, in_sem.at[1]),
        pltpu.make_async_copy(cou_h, cou, in_sem.at[2]),
        pltpu.make_async_copy(upw_h, upw, in_sem.at[3]),
    ]
    quarters = [pl.ds(q * 8 * Y, 8 * Y) for q in range(4)]
    fields = [
        pltpu.make_async_copy(cot_h.at[:, rows, :], cot.at[:, rows, :], in_sem.at[4 + q])
        for q, rows in enumerate(quarters)
    ]
    loads[0].start()
    loads[1].start()
    for q in ORDER:
        fields[q].start()

    barrier = pltpu.get_barrier_semaphore()

    def greet_y(d, _):
        pl.semaphore_signal(barrier, inc=1, device_id=(i, lax.rem(j + d, NJ)), device_id_type=MESH)
        return 0

    def greet_x(d, _):
        pl.semaphore_signal(barrier, inc=1, device_id=(lax.rem(i + d, NI), j), device_id_type=MESH)
        return 0

    lax.fori_loop(1, NJ, greet_y, 0)
    lax.fori_loop(1, NI, greet_x, 0)

    loads[0].wait()
    loads[1].wait()
    ec[...] = 1.0 / (dif[...] * (1.0 + 3.0 * pha[...].astype(f32)))

    for q in range(X // 8):
        xs = pl.ds(q * 8, 8)
        cells = [ec[pl.ds(q * 8 * Y + y, 8, stride=Y), :] for y in range(Y)]
        theta = jnp.ones((8, Z), f32)
        delta = jnp.ones((8, Z), f32)
        for y in range(Y):
            yb[y, xs, :] = theta
            delta = delta + cells[y] * theta
            theta = theta + delta
        rn = 1.0 / theta
        yr[xs, :] = rn
        phi = jnp.ones((8, Z), f32)
        delta = jnp.ones((8, Z), f32)
        after = jnp.ones((8, Z), f32)
        at = (q % 2) * 8 * 8 + q // 2
        for y in range(Y - 1, -1, -1):
            a = phi * rn
            b = yb[y, xs, :] * rn
            ya[y, xs, :] = a
            yb[y, xs, :] = b
            yw[y, xs, :] = 1.0 / (b * after)
            yo[y, xs, :] = b * cells[y]
            if y == Y - 1:
                csy[pl.ds(at + 4, 8, stride=8), :] = b
            if y == 0:
                csy[pl.ds(at, 8, stride=8), :] = a
            after = b
            delta = delta + cells[y] * phi
            phi = phi + delta
        csy[pl.ds(at + 2, 8, stride=8), :] = rn

    seg = lax.broadcasted_iota(jnp.int32, (8, Z), 0)
    span = Z // 8
    tiles = LINES // Z
    for t in range(tiles):
        et[t] = ec[t * Z : (t + 1) * Z, :].T
    ones = jnp.ones((8, Z), f32)
    zeros = jnp.zeros((8, Z), f32)

    def cell(t, step):
        return et[t, pl.ds(step, 8, stride=span), :]

    starts = []
    for t in range(tiles):
        p11, p12, p21, p22 = ones, zeros, zeros, ones
        for step in range(span):
            e = cell(t, step)
            p21 = p21 + e * p11
            p22 = p22 + e * p12
            p11 = p11 + p21
            p12 = p12 + p22
        for shift in (1, 2, 4):
            keep = seg < shift
            q11 = jnp.where(keep, 1.0, pltpu.roll(p11, shift, 0))
            q12 = jnp.where(keep, 0.0, pltpu.roll(p12, shift, 0))
            q21 = jnp.where(keep, 0.0, pltpu.roll(p21, shift, 0))
            q22 = jnp.where(keep, 1.0, pltpu.roll(p22, shift, 0))
            p11, p12, p21, p22 = (
                p11 * q11 + p12 * q21,
                p11 * q12 + p12 * q22,
                p21 * q11 + p22 * q21,
                p21 * q12 + p22 * q22,
            )
        theta = jnp.where(seg < 1, 1.0, pltpu.roll(p11 + p12, 1, 0))
        delta = jnp.where(seg < 1, 1.0, pltpu.roll(p21 + p22, 1, 0))
        starts.append((theta, delta))
    for t in range(tiles):
        theta, delta = starts[t]
        for step in range(span):
            delta = delta + cell(t, step) * theta
            theta = theta + delta
            et[t, pl.ds(step, 8, stride=span), :] = theta
    lane = lax.broadcasted_iota(jnp.int32, (Z, Z), 1)
    for t in range(tiles):
        rows = pl.ds(t * Z, Z)
        theta = et[t].T
        before = jnp.where(lane < 1, 1.0, pltpu.roll(theta, 1, 1))
        zt[rows, :] = before
        zw[rows, :] = 1.0 / (theta * before)
        zo[rows, :] = before * ec[rows, :]

    row = lax.rem(lax.broadcasted_iota(jnp.int32, (2 * Z, Z), 0), Z)
    col = lax.broadcasted_iota(jnp.int32, (2 * Z, Z), 1)
    tri[0] = (row <= col).astype(f32).astype(jnp.bfloat16)
    tri[1] = (row >= col).astype(f32).astype(jnp.bfloat16)

    def exchange(src, dst, slot, pitch, rows, k, axis):
        here = j if axis == "gy" else i
        return pltpu.make_async_remote_copy(
            src_ref=src.at[pl.ds(pl.multiple_of(k * pitch, 8), rows), :],
            dst_ref=dst.at[pl.ds(pl.multiple_of(here * pitch, 8), rows), :],
            send_sem=sent.at[slot],
            recv_sem=came.at[slot],
            device_id={axis: k},
            device_id_type=MESH,
        )

    def whole_round(src, dst, slot, pitch, rows, axis):
        total = pl.ds(0, rows * ((NJ if axis == "gy" else NI) - 1))
        return pltpu.make_async_remote_copy(
            src_ref=src.at[total, :],
            dst_ref=dst.at[total, :],
            send_sem=sent.at[slot],
            recv_sem=came.at[slot],
            device_id={axis: jnext if axis == "gy" else inext},
            device_id_type=MESH,
        )

    def peers(axis):
        if axis == "gy":
            return [lax.rem(j // 4 + a, 4) * 4 + lax.rem(j + b, 4) for a, b in FAR]
        return [lax.rem(i // 2 + a, 4) * 2 + lax.rem(i + b, 2) for a, b in FAR_X]

    def send_all(src, dst, slot, pitch, rows, axis):
        here = j if axis == "gy" else i
        mine = pl.ds(pl.multiple_of(here * pitch, 8), rows)
        for k in peers(axis):
            exchange(src, dst, slot, pitch, rows, k, axis).start()
        dst[mine, :] = src[mine, :]

    def recv_all(src, dst, slot, pitch, rows, axis):
        whole_round(src, dst, slot, pitch, rows, axis).wait_recv()

    def sent_all(src, dst, slot, pitch, rows, axis):
        whole_round(src, dst, slot, pitch, rows, axis).wait_send()

    coup_y = (csy, rcy, 0, 8, 8, "gy")
    coup_x = (csx, rcx, 1, 16, 16, "gx")
    tot_y = (sty, tty, 2, PACK, PACK, "gy")
    ret_y = (oty, rty, 3, PACK, PACK, "gy")
    tot_x = (stx, ttx, 4, STEP_X, PACK_X, "gx")
    ret_x = (otx, rtx, 5, STEP_X, PACK_X, "gx")

    def face(src, dst, slot, part, axis, to):
        return pltpu.make_async_remote_copy(
            src_ref=src.at[part], dst_ref=dst.at[part], send_sem=sent.at[slot], recv_sem=came.at[slot],
            device_id={axis: to}, device_id_type=MESH,
        )

    def both(src, dst, slot):
        return pltpu.make_async_remote_copy(
            src_ref=src, dst_ref=dst, send_sem=sent.at[slot], recv_sem=came.at[slot],
            device_id={"gy": jnext}, device_id_type=MESH,
        )

    edges = [
        face(fse, fre, 6, 0, "gy", jprev),
        face(fse, fre, 6, 1, "gy", jnext),
    ]
    faces = [
        face(fsy, fry, 7, 0, "gy", jprev),
        face(fsy, fry, 7, 1, "gy", jnext),
        face(fsx, frx, 8, 0, "gx", iprev),
        face(fsx, frx, 8, 1, "gx", inext),
    ]
    pairs = [both(fse, fre, 6), both(fsy, fry, 7), both(fsx, frx, 8)]
    def z_lower(q):
        rows = quarters[q]
        scale, weight = zt[rows, :], zw[rows, :]
        for c in range(C):
            zb[c, rows, :] = weight * jnp.dot(
                split(cot[c, rows, :] * scale), tri[0], preferred_element_type=f32
            )

    def z_upper(q):
        rows = quarters[q]
        finish = zo[rows, :]
        for c in range(C):
            zb[c, rows, :] = finish * jnp.dot(split(zb[c, rows, :]), tri[1], preferred_element_type=f32)

    def y_totals(q):
        xs = pl.ds(q * 8, 8)
        heads = [jnp.zeros((8, Z), f32) for _ in range(C)]
        tails = [jnp.zeros((8, Z), f32) for _ in range(C)]
        for y in range(Y):
            a, b = ya[y, xs, :], yb[y, xs, :]
            for c in range(C):
                value = zb[c, pl.ds(q * 8 * Y + y, 8, stride=Y), :]
                heads[c] = heads[c] + a * value
                tails[c] = tails[c] + b * value
                yf[c, y, xs, :] = tails[c]
        at = (q % 2) * 8 * PACK + (q // 2) * C
        for c in range(C):
            sty[pl.ds(at + c, 8, stride=PACK), :] = heads[c]
            sty[pl.ds(at + HALF + c, 8, stride=PACK), :] = tails[c]

    for q in ORDER:
        fields[q].wait()
    loads[2].start()
    loads[3].start()
    z_lower(0)
    for q in range(4):
        if q < 3:
            z_lower(q + 1)
        z_upper(q)
        y_totals(q)

    pl.semaphore_wait(barrier, NI + NJ - 2)
    send_all(*tot_y)
    send_all(*coup_y)
    fse[0] = ec[pl.ds(0, X, stride=Y), :]
    fse[1] = ec[pl.ds(Y - 1, X, stride=Y), :]
    for e in edges:
        e.start()

    def x_factor():
        rows = pl.ds(0, 32)
        one = jnp.ones((32, Z), f32)

        def up(x, carry):
            theta, delta = carry
            xb[x, rows, :] = theta
            delta = delta + xe[x, rows, :] * theta
            return theta + delta, delta

        theta, _ = lax.fori_loop(0, X, up, (one, one), unroll=8)
        rn = 1.0 / theta
        xr[rows, :] = rn

        def down(step, carry):
            x = X - 1 - step
            phi, delta, after, _ = carry
            cell = xe[x, rows, :]
            a = phi * rn
            b = xb[x, rows, :] * rn
            xa[x, rows, :] = a
            xb[x, rows, :] = b
            xw[x, rows, :] = 1.0 / (b * after)
            xo[x, rows, :] = b * cell
            delta = delta + cell * phi
            return phi + delta, delta, b, a

        _, _, _, first = lax.fori_loop(0, X, down, (one, one, one, one), unroll=8)
        return first, rn

    pairs[0].wait_recv()
    for x in range(X):
        xe[x, 0:Y, :] = ec[x * Y : (x + 1) * Y, :]
        xe[x, 16:24, :] = jnp.broadcast_to(fre[1, x : x + 1, :], (8, Z))
        xe[x, 24:32, :] = jnp.broadcast_to(fre[0, x : x + 1, :], (8, Z))
    first, rn = x_factor()
    for t, part in enumerate((first, rn, xb[X - 1])):
        for r in range(2):
            csx[pl.ds(4 * t + r, 8, stride=16), :] = part[r * 8 : r * 8 + 8]
        csx[pl.ds(4 * t + 2, C, stride=16), :] = part[16 : 16 + C]
        csx[pl.ds(C * 16 + 4 * t + 2, 8 - C, stride=16), :] = part[24 : 32 - C]
        csx[pl.ds(4 * t + 3, 8, stride=16), :] = part[24:32]

    loads[2].wait()
    loads[3].wait()
    fsy[0] = upw[1, pl.ds(0, X, stride=Y), :].astype(f32) * cou[1, pl.ds(0, X, stride=Y), :]
    fsy[1] = (1.0 - upw[1, pl.ds(Y - 1, X, stride=Y), :].astype(f32)) * cou[1, pl.ds(Y - 1, X, stride=Y), :]
    fsx[0] = upw[0, 0:Y, :].astype(f32) * cou[0, 0:Y, :] * ec[0:Y, :]
    fsx[1] = (1.0 - upw[0, LINES - Y : LINES, :].astype(f32)) * cou[0, LINES - Y : LINES, :] * ec[LINES - Y : LINES, :]

    send_all(*coup_x)
    for f in faces:
        f.start()

    def reduce_factor(count, pitch, lines, half, couplings, factors):
        def spread(base, t):
            at = base + len(lines) * t
            return jnp.concatenate(
                [jnp.broadcast_to(couplings[pl.ds(at + n, 1), :], (wide, Z)) for n, wide in enumerate(lines)],
                axis=0,
            )

        edge = jnp.zeros((half, Z), f32)
        for m in range(count):
            a1, b1, bn = spread(m * pitch, 0), spread(m * pitch, 1), spread(m * pitch, 2)
            alpha = 1.0 / (1.0 - a1 * edge)
            alpha_a = a1 * alpha
            forward = b1 * alpha
            back = b1 * edge
            factors[0, m, 0:half, :] = alpha
            factors[1, m, 0:half, :] = alpha_a
            factors[2, m, 0:half, :] = forward
            factors[3, m, 0:half, :] = edge
            factors[4, m, 0:half, :] = back * alpha
            factors[5, m, 0:half, :] = b1 + back * alpha_a
            edge = bn + back * forward

    def reduce_solve(count, pitch, half, totals, factors, results):
        gain = jnp.zeros((half, Z), f32)
        for m in range(count):
            head = totals[m * pitch : m * pitch + half, :]
            tail = totals[m * pitch + half : m * pitch + 2 * half, :]
            gl[0, m, 0:half, :] = gain
            gl[1, m, 0:half, :] = factors[0, m, 0:half, :] * head + factors[1, m, 0:half, :] * gain
            gain = tail + factors[4, m, 0:half, :] * head + factors[5, m, 0:half, :] * gain
        later = jnp.zeros((half, Z), f32)
        for m in range(count - 1, -1, -1):
            results[m * pitch + half : m * pitch + 2 * half, :] = later
            later = gl[1, m, 0:half, :] + factors[2, m, 0:half, :] * later
            results[m * pitch : m * pitch + half, :] = gl[0, m, 0:half, :] + factors[3, m, 0:half, :] * later

    recv_all(*coup_y)
    reduce_factor(NJ, 8, (C, C), HALF, rcy, ky)

    recv_all(*tot_y)
    reduce_solve(NJ, PACK, HALF, tty, ky, oty)
    send_all(*ret_y)

    recv_all(*coup_x)
    reduce_factor(NI, 16, (C, C, 1, 1), HALF_X, rcx, kx)
    pairs[1].wait_recv()
    pairs[2].wait_recv()

    low_ok = jnp.where(j > 0, 1.0, 0.0).astype(f32)
    high_ok = jnp.where(j < NJ - 1, 1.0, 0.0).astype(f32)
    lane16 = lax.broadcasted_iota(jnp.int32, (Y, Z), 1)

    def coefficients(x, _):
        rows = pl.ds(pl.multiple_of(x * Y, Y), Y)
        shifted = pl.ds(pl.multiple_of(x * Y + Y, Y), Y)
        padded = pl.ds(pl.multiple_of(x * PAD + 8, 8), Y)
        flux = [cou[d, rows, :] for d in range(3)]
        ahead = [upw[d, rows, :].astype(f32) * flux[d] for d in range(3)]
        behind = [flux[d] - ahead[d] for d in range(3)]
        c0[rows, :] = 1.0 + (behind[0] - ahead[0]) + (behind[1] - ahead[1]) + (behind[2] - ahead[2])
        ax[shifted, :] = ahead[0]
        bx[shifted, :] = behind[0]
        ayp[padded, :] = ahead[1]
        byp[padded, :] = behind[1]
        azn[rows, :] = jnp.where(lane16 < Z - 1, pltpu.roll(ahead[2], Z - 1, 1), 0.0)
        bzp[rows, :] = jnp.where(lane16 > 0, pltpu.roll(behind[2], 1, 1), 0.0)
        return 0

    lax.fori_loop(0, X, coefficients, 0, unroll=8)
    bx[0:Y, :] = frx[1]
    ax[(X + 1) * Y : (X + 2) * Y, :] = frx[0]
    byp[pl.ds(7, X, stride=PAD), :] = fry[1] * low_ok
    ayp[pl.ds(PAD, X, stride=PAD), :] = fry[0] * high_ok
    ayh[...] = jnp.zeros_like(ayh)

    recv_all(*ret_y)

    for q in ORDER:
        xs = pl.ds(q * 8, 8)
        at = (q % 2) * 8 * PACK + (q // 2) * C
        below, above, live = [], [], []
        for c in range(C):
            left = rty[pl.ds(at + c, 8, stride=PACK), :]
            right = rty[pl.ds(at + HALF + c, 8, stride=PACK), :]
            ayh[pl.ds(q * 8 * 16 + c, 8, stride=16), :] = left * fre[1, xs, :]
            ayh[pl.ds(q * 8 * 16 + 8 + c, 8, stride=16), :] = right * fre[0, xs, :]
            below.append(left * yr[xs, :])
            live.append(right)
        for y in range(Y - 1, -1, -1):
            weight, finish = yw[y, xs, :], yo[y, xs, :]
            for c in range(C):
                live[c] = live[c] + weight * (yf[c, y, xs, :] + below[c])
                ay[c, pl.ds(q * 8 * Y + y, 8, stride=Y), :] = live[c] * finish

    def x_totals(x, carry):
        heads, tails, halo_head, halo = carry
        rows = pl.ds(pl.multiple_of(x * Y, Y), Y)
        a, b = xa[x, 0:Y, :], xb[x, 0:Y, :]
        new_heads, new_tails = [], []
        for c in range(C):
            value = ay[c, rows, :]
            new_heads.append(heads[c] + a * value)
            tail = tails[c] + b * value
            new_tails.append(tail)
            ay[c, rows, :] = tail
        value = ayh[rows, :]
        halo_head = halo_head + xa[x, 16:32, :] * value
        halo = halo + xb[x, 16:32, :] * value
        ayh[rows, :] = halo
        return tuple(new_heads), tuple(new_tails), halo_head, halo

    none = jnp.zeros((Y, Z), f32)
    heads, tails, *edge_pair = lax.fori_loop(0, X, x_totals, ((none,) * C, (none,) * C, none, none), unroll=8)
    for c in range(C):
        for r in range(2):
            stx[pl.ds(r * C + c, 8, stride=STEP_X), :] = heads[c][r * 8 : r * 8 + 8]
            stx[pl.ds(HALF_X + r * C + c, 8, stride=STEP_X), :] = tails[c][r * 8 : r * 8 + 8]
    for end, part in enumerate(edge_pair):
        at = end * HALF_X + HALF
        stx[pl.ds(at, C, stride=STEP_X), :] = part[0:C]
        stx[pl.ds(C * STEP_X + at, 8 - C, stride=STEP_X), :] = part[8 : 16 - C]
        stx[pl.ds(at + 1, 2 * C - 8, stride=STEP_X), :] = part[16 - C : 8 + C]
    send_all(*tot_x)
    sent_all(*coup_y)
    sent_all(*coup_x)
    sent_all(*tot_y)
    sent_all(*ret_y)
    for pair in pairs:
        pair.wait_send()
    recv_all(*tot_x)
    reduce_solve(NI, STEP_X, HALF_X, ttx, kx, otx)
    send_all(*ret_x)

    sent_all(*tot_x)
    recv_all(*ret_x)

    lefts, rights = [], []
    for c in range(C):
        left = jnp.concatenate([rtx[pl.ds(r * C + c, 8, stride=STEP_X), :] for r in range(2)], axis=0)
        right = jnp.concatenate([rtx[pl.ds(HALF_X + r * C + c, 8, stride=STEP_X), :] for r in range(2)], axis=0)
        fb[pl.ds(c * PITCH + 8, Y), :] = left
        fb[pl.ds(c * PITCH + (X + 1) * PAD + 8, Y), :] = right
        lefts.append(left * xr[0:Y, :])
        rights.append(right)
    for end in range(2):
        at = end * HALF_X + HALF
        ext[end, 0:C, :] = rtx[pl.ds(at, C, stride=STEP_X), :]
        ext[end, 8 : 16 - C, :] = rtx[pl.ds(C * STEP_X + at, 8 - C, stride=STEP_X), :]
        ext[end, 16 - C : 8 + C, :] = rtx[pl.ds(at + 1, 2 * C - 8, stride=STEP_X), :]
    left_halo = ext[0] * xr[16:32, :]
    right_halo = ext[1]

    def x_finish(step, carry):
        x = X - 1 - step
        live, halo = carry
        rows = pl.ds(pl.multiple_of(x * Y, Y), Y)
        weight, finish = xw[x, 0:Y, :], xo[x, 0:Y, :]
        out = []
        for c in range(C):
            value = live[c] + weight * (ay[c, rows, :] + lefts[c])
            fb[pl.ds(pl.multiple_of(c * PITCH + (x + 1) * PAD + 8, 8), Y), :] = value * finish
            out.append(value)
        halo = halo + xw[x, 16:32, :] * (ayh[rows, :] + left_halo)
        edge = halo * xo[x, 16:32, :]
        fb[pl.ds((x + 1) * PAD + 7, 8, stride=PITCH), :] = edge[0:8]
        fb[pl.ds((x + 2) * PAD, 8, stride=PITCH), :] = edge[8:16]
        return tuple(out), halo

    lax.fori_loop(0, X, x_finish, (tuple(rights), right_halo), unroll=4)

    sent_all(*ret_x)


def advection(fb, c0, ax, bx, ayp, byp, azn, bzp, out_h, out, sem):
    def advect(x, _):
        rows = pl.ds(pl.multiple_of(x * Y, Y), Y)
        middle = c0[rows, :]
        from_x, to_x = bx[rows, :], ax[pl.ds(pl.multiple_of((x + 2) * Y, Y), Y), :]
        from_y, to_y = byp[pl.ds(x * PAD + 7, Y), :], ayp[pl.ds(x * PAD + 9, Y), :]
        from_z, to_z = bzp[rows, :], azn[rows, :]
        for c in range(C):
            at = c * PITCH + (x + 1) * PAD + 8
            value = fb[pl.ds(pl.multiple_of(at, 8), Y), :]
            result = middle * value
            result += to_x * fb[pl.ds(pl.multiple_of(at + PAD, 8), Y), :]
            result -= from_x * fb[pl.ds(pl.multiple_of(at - PAD, 8), Y), :]
            result += to_y * fb[pl.ds(at + 1, Y), :]
            result -= from_y * fb[pl.ds(at - 1, Y), :]
            result += to_z * pltpu.roll(value, Z - 1, 1)
            result -= from_z * pltpu.roll(value, 1, 1)
            out[c, rows, :] = result
        return 0

    stores = []
    for part in range(4):
        lax.fori_loop(part * 8, part * 8 + 8, advect, 0, unroll=8)
        rows = pl.ds(part * 8 * Y, 8 * Y)
        store = pltpu.make_async_copy(out.at[:, rows, :], out_h.at[:, rows, :], sem.at[part])
        store.start()
        stores.append(store)
    for store in stores:
        store.wait()


def on_device(cotangent, diffusion, phase, courant, upwind):
    def vm(*shape, dtype=f32):
        return pltpu.VMEM(shape, dtype)

    dma = pltpu.SemaphoreType.DMA
    scratch = [
        vm(C, LINES, Z), vm(LINES, Z), vm(LINES, Z, dtype=jnp.int32), vm(3, LINES, Z), vm(3, LINES, Z, dtype=jnp.int32),
        vm(LINES, Z),
        vm(LINES // Z, Z, Z), vm(LINES, Z), vm(LINES, Z), vm(LINES, Z), vm(C, LINES, Z), vm(2, 2 * Z, Z, dtype=jnp.bfloat16),
        vm(Y, X, Z), vm(Y, X, Z), vm(Y, X, Z), vm(Y, X, Z), vm(X, Z), vm(C, Y, X, Z), vm(C, LINES, Z), vm(X * 16, Z),
        vm(X, 32, Z), vm(X, 32, Z), vm(X, 32, Z), vm(X, 32, Z), vm(X, 32, Z), vm(32, Z),
        vm(NJ * 8, Z), vm(NI * 16, Z), vm(NJ * 8, Z), vm(NI * 16, Z), vm(6, NJ, 16, Z), vm(6, NI, 16, Z), vm(2, NJ, 16, Z),
        vm(NJ * PACK, Z), vm(NJ * PACK, Z), vm(NJ * PACK, Z), vm(NJ * PACK, Z),
        vm(NI * STEP_X, Z), vm(NI * STEP_X, Z), vm(NI * STEP_X, Z), vm(NI * STEP_X, Z), vm(2, 16, Z),
        vm(2, X, Z), vm(2, X, Z), vm(2, X, Z), vm(2, X, Z), vm(2, Y, Z), vm(2, Y, Z),
        dma((8,)), dma((9,)), dma((9,)),
    ]
    vmem = pl.BlockSpec(memory_space=pltpu.VMEM)
    shapes = [(8 * PITCH, Z), (LINES, Z), (LINES + 2 * Y, Z), (LINES + 2 * Y, Z), (X * PAD + 8, Z), (X * PAD + 8, Z), (LINES, Z), (LINES, Z)]
    parts = pl.pallas_call(
        body,
        out_shape=[pltpu.VMEM(shape, f32) for shape in shapes],
        in_specs=[pl.BlockSpec(memory_space=pltpu.HBM)] * 5,
        out_specs=[vmem] * len(shapes),
        scratch_shapes=scratch,
        compiler_params=pltpu.CompilerParams(
            collective_id=0, has_side_effects=True, vmem_limit_bytes=40 * 1024 * 1024
        ),
    )(
        *(
            pltpu.with_memory_space_constraint(given, pltpu.HBM)
            for given in (
                cotangent.reshape(C, LINES, Z),
                diffusion.reshape(LINES, Z),
                phase.reshape(LINES, Z),
                courant.reshape(3, LINES, Z),
                upwind.reshape(3, LINES, Z),
            )
        )
    )
    out = pl.pallas_call(
        advection,
        out_shape=jax.ShapeDtypeStruct((C, LINES, Z), f32),
        in_specs=[vmem] * len(shapes),
        out_specs=pl.BlockSpec(memory_space=pl.ANY),
        scratch_shapes=[vm(C, LINES, Z), dma((4,))],
        compiler_params=pltpu.CompilerParams(vmem_limit_bytes=8 * 1024 * 1024),
    )(*(pltpu.with_memory_space_constraint(part, pltpu.VMEM) for part in parts))
    return out.reshape(C, X, Y, Z)


def solution(mesh):
    placed = (
        P(None, "gx", "gy", None),
        P("gx", "gy", None),
        P("gx", "gy", None),
        P(None, "gx", "gy", None),
        P(None, "gx", "gy", None),
    )
    return jax.shard_map(
        on_device, mesh=mesh, in_specs=placed, out_specs=P(None, "gx", "gy", None), check_vma=False
    )
```

```python
import functools

import jax
import jax.numpy as jnp
from jax import lax
from jax.experimental import pallas as pl
from jax.experimental.pallas import tpu as pltpu
from jax.sharding import PartitionSpec as P

MESH = pl.DeviceIdType.MESH
C, X, Y, Z = 6, 32, 16, 128
NI, NJ = 8, 16
LINES = X * Y
PAD = 24
PLANES = X + 2
PITCH = PLANES * PAD + 8
HALF = C * 2
PACK = 2 * HALF
HALF_X = HALF + 2
PACK_X = 2 * HALF_X
STEP_X = 32
f32 = jnp.float32
FAR = sorted(((a, b) for a in range(4) for b in range(4) if a or b), key=lambda d: -min(d[0], 4 - d[0]) - min(d[1], 4 - d[1]))
ORDER = (0, 2, 1, 3)
FAR_X = [(2, 1), (2, 0), (3, 1), (1, 1), (3, 0), (1, 0), (0, 1)]


def split(values):
    high = values.astype(jnp.bfloat16)
    low = (values - high.astype(f32)).astype(jnp.bfloat16)
    return jnp.concatenate([high, low], axis=1)


def body(
    cot_h, dif_h, pha_h, cou_h, upw_h,
    fb, c0, ax, bx, ayp, byp, azn, bzp,
    cot, dif, pha, cou, upw, ec,
    et, zt, zw, zo, zb, tri,
    yb, ya, yw, yo, yr, yf, ay, ayh, ynl, ynr, ends,
    xe, xb, xa, xw, xo, xr,
    csy, csx, rcy, rcx, ky, kx, gl,
    sty, tty, oty, rty, stx, ttx, otx, rtx, ext,
    fse, fre, fsy, fry, fsx, frx,
    in_sem,
    sent, came,
):
    i = lax.axis_index("gx")
    j = lax.axis_index("gy")
    inext, iprev = lax.rem(i + 1, NI), lax.rem(i + NI - 1, NI)
    jnext, jprev = lax.rem(j + 1, NJ), lax.rem(j + NJ - 1, NJ)

    loads = [
        pltpu.make_async_copy(dif_h, dif, in_sem.at[0]),
        pltpu.make_async_copy(pha_h, pha, in_sem.at[1]),
        pltpu.make_async_copy(cou_h, cou, in_sem.at[2]),
        pltpu.make_async_copy(upw_h, upw, in_sem.at[3]),
    ]
    quarters = [pl.ds(q * 8 * Y, 8 * Y) for q in range(4)]
    fields = [
        pltpu.make_async_copy(cot_h.at[:, rows, :], cot.at[:, rows, :], in_sem.at[4 + q])
        for q, rows in enumerate(quarters)
    ]
    loads[0].start()
    loads[1].start()
    for q in ORDER:
        fields[q].start()

    barrier = pltpu.get_barrier_semaphore()

    def greet_y(d, _):
        pl.semaphore_signal(barrier, inc=1, device_id=(i, lax.rem(j + d, NJ)), device_id_type=MESH)
        return 0

    def greet_x(d, _):
        pl.semaphore_signal(barrier, inc=1, device_id=(lax.rem(i + d, NI), j), device_id_type=MESH)
        return 0

    lax.fori_loop(1, NJ, greet_y, 0)
    lax.fori_loop(1, NI, greet_x, 0)

    loads[0].wait()
    loads[1].wait()
    ec[...] = 1.0 / (dif[...] * (1.0 + 3.0 * pha[...].astype(f32)))

    for q in range(X // 8):
        xs = pl.ds(q * 8, 8)
        cells = [ec[pl.ds(q * 8 * Y + y, 8, stride=Y), :] for y in range(Y)]
        theta = jnp.ones((8, Z), f32)
        delta = jnp.ones((8, Z), f32)
        for y in range(Y):
            yb[y, xs, :] = theta
            delta = delta + cells[y] * theta
            theta = theta + delta
        rn = 1.0 / theta
        yr[xs, :] = rn
        phi = jnp.ones((8, Z), f32)
        delta = jnp.ones((8, Z), f32)
        after = jnp.ones((8, Z), f32)
        at = (q % 2) * 8 * 8 + q // 2
        for y in range(Y - 1, -1, -1):
            a = phi * rn
            b = yb[y, xs, :] * rn
            ya[y, xs, :] = a
            yb[y, xs, :] = b
            yw[y, xs, :] = 1.0 / (b * after)
            yo[y, xs, :] = b * cells[y]
            if y == Y - 1:
                csy[pl.ds(at + 4, 8, stride=8), :] = b
            if y == 0:
                csy[pl.ds(at, 8, stride=8), :] = a
            after = b
            delta = delta + cells[y] * phi
            phi = phi + delta
        csy[pl.ds(at + 2, 8, stride=8), :] = rn

    seg = lax.broadcasted_iota(jnp.int32, (8, Z), 0)
    span = Z // 8
    tiles = LINES // Z
    for t in range(tiles):
        et[t] = ec[t * Z : (t + 1) * Z, :].T
    ones = jnp.ones((8, Z), f32)
    zeros = jnp.zeros((8, Z), f32)

    def cell(t, step):
        return et[t, pl.ds(step, 8, stride=span), :]

    starts = []
    for t in range(tiles):
        p11, p12, p21, p22 = ones, zeros, zeros, ones
        for step in range(span):
            e = cell(t, step)
            p21 = p21 + e * p11
            p22 = p22 + e * p12
            p11 = p11 + p21
            p12 = p12 + p22
        for shift in (1, 2, 4):
            keep = seg < shift
            q11 = jnp.where(keep, 1.0, pltpu.roll(p11, shift, 0))
            q12 = jnp.where(keep, 0.0, pltpu.roll(p12, shift, 0))
            q21 = jnp.where(keep, 0.0, pltpu.roll(p21, shift, 0))
            q22 = jnp.where(keep, 1.0, pltpu.roll(p22, shift, 0))
            p11, p12, p21, p22 = (
                p11 * q11 + p12 * q21,
                p11 * q12 + p12 * q22,
                p21 * q11 + p22 * q21,
                p21 * q12 + p22 * q22,
            )
        theta = jnp.where(seg < 1, 1.0, pltpu.roll(p11 + p12, 1, 0))
        delta = jnp.where(seg < 1, 1.0, pltpu.roll(p21 + p22, 1, 0))
        starts.append((theta, delta))
    for t in range(tiles):
        theta, delta = starts[t]
        for step in range(span):
            delta = delta + cell(t, step) * theta
            theta = theta + delta
            et[t, pl.ds(step, 8, stride=span), :] = theta
    lane = lax.broadcasted_iota(jnp.int32, (Z, Z), 1)
    for t in range(tiles):
        rows = pl.ds(t * Z, Z)
        theta = et[t].T
        before = jnp.where(lane < 1, 1.0, pltpu.roll(theta, 1, 1))
        zt[rows, :] = before
        zw[rows, :] = 1.0 / (theta * before)
        zo[rows, :] = before * ec[rows, :]

    row = lax.rem(lax.broadcasted_iota(jnp.int32, (2 * Z, Z), 0), Z)
    col = lax.broadcasted_iota(jnp.int32, (2 * Z, Z), 1)
    tri[0] = (row <= col).astype(f32).astype(jnp.bfloat16)
    tri[1] = (row >= col).astype(f32).astype(jnp.bfloat16)

    def exchange(src, dst, slot, pitch, rows, k, axis):
        here = j if axis == "gy" else i
        return pltpu.make_async_remote_copy(
            src_ref=src.at[pl.ds(pl.multiple_of(k * pitch, 8), rows), :],
            dst_ref=dst.at[pl.ds(pl.multiple_of(here * pitch, 8), rows), :],
            send_sem=sent.at[slot],
            recv_sem=came.at[slot],
            device_id={axis: k},
            device_id_type=MESH,
        )

    def whole_round(src, dst, slot, pitch, rows, axis):
        total = pl.ds(0, rows * ((NJ if axis == "gy" else NI) - 1))
        return pltpu.make_async_remote_copy(
            src_ref=src.at[total, :],
            dst_ref=dst.at[total, :],
            send_sem=sent.at[slot],
            recv_sem=came.at[slot],
            device_id={axis: jnext if axis == "gy" else inext},
            device_id_type=MESH,
        )

    def peers(axis):
        if axis == "gy":
            return [lax.rem(j // 4 + a, 4) * 4 + lax.rem(j + b, 4) for a, b in FAR]
        return [lax.rem(i // 2 + a, 4) * 2 + lax.rem(i + b, 2) for a, b in FAR_X]

    def send_all(src, dst, slot, pitch, rows, axis):
        here = j if axis == "gy" else i
        mine = pl.ds(pl.multiple_of(here * pitch, 8), rows)
        for k in peers(axis):
            exchange(src, dst, slot, pitch, rows, k, axis).start()
        dst[mine, :] = src[mine, :]

    def recv_all(src, dst, slot, pitch, rows, axis):
        whole_round(src, dst, slot, pitch, rows, axis).wait_recv()

    def sent_all(src, dst, slot, pitch, rows, axis):
        whole_round(src, dst, slot, pitch, rows, axis).wait_send()

    coup_y = (csy, rcy, 0, 8, 8, "gy")
    coup_x = (csx, rcx, 1, 16, 16, "gx")
    tot_y = (sty, tty, 2, PACK, PACK, "gy")
    ret_y = (oty, rty, 3, PACK, PACK, "gy")
    tot_x = (stx, ttx, 4, STEP_X, PACK_X, "gx")
    ret_x = (otx, rtx, 5, STEP_X, PACK_X, "gx")

    def face(src, dst, slot, part, axis, to):
        return pltpu.make_async_remote_copy(
            src_ref=src.at[part], dst_ref=dst.at[part], send_sem=sent.at[slot], recv_sem=came.at[slot],
            device_id={axis: to}, device_id_type=MESH,
        )

    def both(src, dst, slot):
        return pltpu.make_async_remote_copy(
            src_ref=src, dst_ref=dst, send_sem=sent.at[slot], recv_sem=came.at[slot],
            device_id={"gy": jnext}, device_id_type=MESH,
        )

    edges = [
        face(fse, fre, 6, 0, "gy", jprev),
        face(fse, fre, 6, 1, "gy", jnext),
    ]
    faces = [
        face(fsy, fry, 7, 0, "gy", jprev),
        face(fsy, fry, 7, 1, "gy", jnext),
        face(fsx, frx, 8, 0, "gx", iprev),
        face(fsx, frx, 8, 1, "gx", inext),
    ]
    pairs = [both(fse, fre, 6), both(fsy, fry, 7), both(fsx, frx, 8)]
    def z_lower(q):
        rows = quarters[q]
        scale, weight = zt[rows, :], zw[rows, :]
        for c in range(C):
            zb[c, rows, :] = weight * jnp.dot(
                split(cot[c, rows, :] * scale), tri[0], preferred_element_type=f32
            )

    def z_upper(q):
        rows = quarters[q]
        finish = zo[rows, :]
        for c in range(C):
            zb[c, rows, :] = finish * jnp.dot(split(zb[c, rows, :]), tri[1], preferred_element_type=f32)

    def y_totals(q):
        xs = pl.ds(q * 8, 8)
        heads = [jnp.zeros((8, Z), f32) for _ in range(C)]
        tails = [jnp.zeros((8, Z), f32) for _ in range(C)]
        for y in range(Y):
            a, b = ya[y, xs, :], yb[y, xs, :]
            for c in range(C):
                value = zb[c, pl.ds(q * 8 * Y + y, 8, stride=Y), :]
                heads[c] = heads[c] + a * value
                tails[c] = tails[c] + b * value
                yf[c, y, xs, :] = tails[c]
        at = (q % 2) * 8 * PACK + (q // 2) * C
        for c in range(C):
            sty[pl.ds(at + c, 8, stride=PACK), :] = heads[c]
            sty[pl.ds(at + HALF + c, 8, stride=PACK), :] = tails[c]

    for q in ORDER:
        fields[q].wait()
    loads[2].start()
    loads[3].start()
    z_lower(0)
    for q in range(4):
        if q < 3:
            z_lower(q + 1)
        z_upper(q)
        y_totals(q)

    pl.semaphore_wait(barrier, NI + NJ - 2)
    send_all(*tot_y)
    send_all(*coup_y)
    fse[0] = ec[pl.ds(0, X, stride=Y), :]
    fse[1] = ec[pl.ds(Y - 1, X, stride=Y), :]
    for e in edges:
        e.start()

    def x_factor():
        rows = pl.ds(0, 32)
        one = jnp.ones((32, Z), f32)

        def up(x, carry):
            theta, delta = carry
            xb[x, rows, :] = theta
            delta = delta + xe[x, rows, :] * theta
            return theta + delta, delta

        theta, _ = lax.fori_loop(0, X, up, (one, one), unroll=8)
        rn = 1.0 / theta
        xr[rows, :] = rn

        def down(step, carry):
            x = X - 1 - step
            phi, delta, after, _ = carry
            cell = xe[x, rows, :]
            a = phi * rn
            b = xb[x, rows, :] * rn
            xa[x, rows, :] = a
            xb[x, rows, :] = b
            xw[x, rows, :] = 1.0 / (b * after)
            xo[x, rows, :] = b * cell
            delta = delta + cell * phi
            return phi + delta, delta, b, a

        _, _, _, first = lax.fori_loop(0, X, down, (one, one, one, one), unroll=8)
        return first, rn

    pairs[0].wait_recv()
    for x in range(X):
        xe[x, 0:Y, :] = ec[x * Y : (x + 1) * Y, :]
        xe[x, 16:24, :] = jnp.broadcast_to(fre[1, x : x + 1, :], (8, Z))
        xe[x, 24:32, :] = jnp.broadcast_to(fre[0, x : x + 1, :], (8, Z))
    first, rn = x_factor()
    for t, part in enumerate((first, rn, xb[X - 1])):
        for r in range(2):
            csx[pl.ds(4 * t + r, 8, stride=16), :] = part[r * 8 : r * 8 + 8]
        csx[pl.ds(4 * t + 2, C, stride=16), :] = part[16 : 16 + C]
        csx[pl.ds(C * 16 + 4 * t + 2, 8 - C, stride=16), :] = part[24 : 32 - C]
        csx[pl.ds(4 * t + 3, 8, stride=16), :] = part[24:32]

    loads[2].wait()
    loads[3].wait()
    fsy[0] = upw[1, pl.ds(0, X, stride=Y), :].astype(f32) * cou[1, pl.ds(0, X, stride=Y), :]
    fsy[1] = (1.0 - upw[1, pl.ds(Y - 1, X, stride=Y), :].astype(f32)) * cou[1, pl.ds(Y - 1, X, stride=Y), :]
    fsx[0] = upw[0, 0:Y, :].astype(f32) * cou[0, 0:Y, :] * ec[0:Y, :]
    fsx[1] = (1.0 - upw[0, LINES - Y : LINES, :].astype(f32)) * cou[0, LINES - Y : LINES, :] * ec[LINES - Y : LINES, :]

    send_all(*coup_x)
    for f in faces:
        f.start()

    def reduce_factor(count, pitch, lines, half, couplings, factors):
        def spread(base, t):
            at = base + len(lines) * t
            return jnp.concatenate(
                [jnp.broadcast_to(couplings[pl.ds(at + n, 1), :], (wide, Z)) for n, wide in enumerate(lines)],
                axis=0,
            )

        edge = jnp.zeros((half, Z), f32)
        for m in range(count):
            a1, b1, bn = spread(m * pitch, 0), spread(m * pitch, 1), spread(m * pitch, 2)
            alpha = 1.0 / (1.0 - a1 * edge)
            alpha_a = a1 * alpha
            forward = b1 * alpha
            back = b1 * edge
            factors[0, m, 0:half, :] = alpha
            factors[1, m, 0:half, :] = alpha_a
            factors[2, m, 0:half, :] = forward
            factors[3, m, 0:half, :] = edge
            factors[4, m, 0:half, :] = back * alpha
            factors[5, m, 0:half, :] = b1 + back * alpha_a
            edge = bn + back * forward

    def reduce_solve(count, pitch, half, totals, factors, results):
        gain = jnp.zeros((half, Z), f32)
        for m in range(count):
            head = totals[m * pitch : m * pitch + half, :]
            tail = totals[m * pitch + half : m * pitch + 2 * half, :]
            gl[0, m, 0:half, :] = gain
            gl[1, m, 0:half, :] = factors[0, m, 0:half, :] * head + factors[1, m, 0:half, :] * gain
            gain = tail + factors[4, m, 0:half, :] * head + factors[5, m, 0:half, :] * gain
        later = jnp.zeros((half, Z), f32)
        for m in range(count - 1, -1, -1):
            results[m * pitch + half : m * pitch + 2 * half, :] = later
            later = gl[1, m, 0:half, :] + factors[2, m, 0:half, :] * later
            results[m * pitch : m * pitch + half, :] = gl[0, m, 0:half, :] + factors[3, m, 0:half, :] * later

    recv_all(*coup_y)
    reduce_factor(NJ, 8, (C, C), HALF, rcy, ky)

    recv_all(*tot_y)
    reduce_solve(NJ, PACK, HALF, tty, ky, oty)
    send_all(*ret_y)

    recv_all(*coup_x)
    reduce_factor(NI, 16, (C, C, 1, 1), HALF_X, rcx, kx)
    pairs[1].wait_recv()
    pairs[2].wait_recv()

    low_ok = jnp.where(j > 0, 1.0, 0.0).astype(f32)
    high_ok = jnp.where(j < NJ - 1, 1.0, 0.0).astype(f32)
    lane16 = lax.broadcasted_iota(jnp.int32, (Y, Z), 1)

    def coefficients(x, _):
        rows = pl.ds(pl.multiple_of(x * Y, Y), Y)
        shifted = pl.ds(pl.multiple_of(x * Y + Y, Y), Y)
        padded = pl.ds(pl.multiple_of(x * PAD + 8, 8), Y)
        flux = [cou[d, rows, :] for d in range(3)]
        ahead = [upw[d, rows, :].astype(f32) * flux[d] for d in range(3)]
        behind = [flux[d] - ahead[d] for d in range(3)]
        c0[rows, :] = 1.0 + (behind[0] - ahead[0]) + (behind[1] - ahead[1]) + (behind[2] - ahead[2])
        ax[shifted, :] = ahead[0]
        bx[shifted, :] = behind[0]
        ayp[padded, :] = ahead[1]
        byp[padded, :] = behind[1]
        azn[rows, :] = jnp.where(lane16 < Z - 1, pltpu.roll(ahead[2], Z - 1, 1), 0.0)
        bzp[rows, :] = jnp.where(lane16 > 0, pltpu.roll(behind[2], 1, 1), 0.0)
        return 0

    lax.fori_loop(0, X, coefficients, 0, unroll=8)
    bx[0:Y, :] = frx[1]
    ax[(X + 1) * Y : (X + 2) * Y, :] = frx[0]
    byp[pl.ds(7, X, stride=PAD), :] = fry[1] * low_ok
    ayp[pl.ds(PAD, X, stride=PAD), :] = fry[0] * high_ok
    ayh[...] = jnp.zeros_like(ayh)

    for q in range(4):
        xs = pl.ds(q * 8, 8)
        live = [jnp.zeros((8, Z), f32) for _ in range(C)]
        summed = jnp.zeros((8, Z), f32)
        for y in range(Y - 1, -1, -1):
            cells = pl.ds(q * 8 * Y + y, 8, stride=Y)
            weight, finish = yw[y, xs, :], yo[y, xs, :]
            summed = summed + weight
            ynl[cells, :] = finish * (summed * yr[xs, :])
            ynr[cells, :] = finish
            for c in range(C):
                live[c] = live[c] + weight * yf[c, y, xs, :]
                ay[c, cells, :] = live[c] * finish

    def x_totals(x, carry):
        heads, tails = carry
        rows = pl.ds(pl.multiple_of(x * Y, Y), Y)
        a, b = xa[x, 0:Y, :], xb[x, 0:Y, :]
        left, right = ynl[rows, :], ynr[rows, :]
        ends[0, rows, :] = a * left
        ends[1, rows, :] = a * right
        ends[2, rows, :] = b * left
        ends[3, rows, :] = b * right
        values = [ay[c, rows, :] for c in range(C)]
        return (
            tuple(heads[c] + a * values[c] for c in range(C)),
            tuple(tails[c] + b * values[c] for c in range(C)),
        )

    none = jnp.zeros((Y, Z), f32)
    heads, tails = lax.fori_loop(0, X, x_totals, ((none,) * C, (none,) * C), unroll=8)
    heads, tails = list(heads), list(tails)

    recv_all(*ret_y)

    def end_values(x, c):
        at = lax.rem(x, NJ) * PACK + (x // NJ) * C + c
        return (
            jnp.broadcast_to(rty[pl.ds(at, 1), :], (Y, Z)),
            jnp.broadcast_to(rty[pl.ds(at + HALF, 1), :], (Y, Z)),
        )

    for q in range(4):
        xs = pl.ds(q * 8, 8)
        at = (q % 2) * 8 * PACK + (q // 2) * C
        for c in range(C):
            left = rty[pl.ds(at + c, 8, stride=PACK), :]
            right = rty[pl.ds(at + HALF + c, 8, stride=PACK), :]
            ayh[pl.ds(q * 8 * 16 + c, 8, stride=16), :] = left * fre[1, xs, :]
            ayh[pl.ds(q * 8 * 16 + 8 + c, 8, stride=16), :] = right * fre[0, xs, :]

    def end_totals(x, carry):
        heads, tails, halo_head, halo_tail = carry
        rows = pl.ds(pl.multiple_of(x * Y, Y), Y)
        hl, hr, tl, tr = (ends[n, rows, :] for n in range(4))
        pairs_of = [end_values(x, c) for c in range(C)]
        value = ayh[rows, :]
        return (
            tuple(heads[c] + (hl * left + hr * right) for c, (left, right) in enumerate(pairs_of)),
            tuple(tails[c] + (tl * left + tr * right) for c, (left, right) in enumerate(pairs_of)),
            halo_head + xa[x, 16:32, :] * value,
            halo_tail + xb[x, 16:32, :] * value,
        )

    heads, tails, *edge_pair = lax.fori_loop(
        0, X, end_totals, (tuple(heads), tuple(tails), none, none), unroll=8
    )
    for c in range(C):
        for r in range(2):
            stx[pl.ds(r * C + c, 8, stride=STEP_X), :] = heads[c][r * 8 : r * 8 + 8]
            stx[pl.ds(HALF_X + r * C + c, 8, stride=STEP_X), :] = tails[c][r * 8 : r * 8 + 8]
    for end, part in enumerate(edge_pair):
        at = end * HALF_X + HALF
        stx[pl.ds(at, C, stride=STEP_X), :] = part[0:C]
        stx[pl.ds(C * STEP_X + at, 8 - C, stride=STEP_X), :] = part[8 : 16 - C]
        stx[pl.ds(at + 1, 2 * C - 8, stride=STEP_X), :] = part[16 - C : 8 + C]
    send_all(*tot_x)

    def x_prefix(x, carry):
        tails, halo = carry
        rows = pl.ds(pl.multiple_of(x * Y, Y), Y)
        b = xb[x, 0:Y, :]
        by_left, by_right = ynl[rows, :], ynr[rows, :]
        out = []
        for c in range(C):
            left, right = end_values(x, c)
            tail = tails[c] + b * (ay[c, rows, :] + by_left * left + by_right * right)
            ay[c, rows, :] = tail
            out.append(tail)
        halo = halo + xb[x, 16:32, :] * ayh[rows, :]
        ayh[rows, :] = halo
        return tuple(out), halo

    lax.fori_loop(0, X, x_prefix, ((none,) * C, none), unroll=8)
    sent_all(*coup_y)
    sent_all(*coup_x)
    sent_all(*tot_y)
    sent_all(*ret_y)
    for pair in pairs:
        pair.wait_send()
    recv_all(*tot_x)
    reduce_solve(NI, STEP_X, HALF_X, ttx, kx, otx)
    send_all(*ret_x)

    sent_all(*tot_x)
    recv_all(*ret_x)

    lefts, rights = [], []
    for c in range(C):
        left = jnp.concatenate([rtx[pl.ds(r * C + c, 8, stride=STEP_X), :] for r in range(2)], axis=0)
        right = jnp.concatenate([rtx[pl.ds(HALF_X + r * C + c, 8, stride=STEP_X), :] for r in range(2)], axis=0)
        fb[pl.ds(c * PITCH + 8, Y), :] = left
        fb[pl.ds(c * PITCH + (X + 1) * PAD + 8, Y), :] = right
        lefts.append(left * xr[0:Y, :])
        rights.append(right)
    for end in range(2):
        at = end * HALF_X + HALF
        ext[end, 0:C, :] = rtx[pl.ds(at, C, stride=STEP_X), :]
        ext[end, 8 : 16 - C, :] = rtx[pl.ds(C * STEP_X + at, 8 - C, stride=STEP_X), :]
        ext[end, 16 - C : 8 + C, :] = rtx[pl.ds(at + 1, 2 * C - 8, stride=STEP_X), :]
    left_halo = ext[0] * xr[16:32, :]
    right_halo = ext[1]

    def x_finish(step, carry):
        x = X - 1 - step
        live, halo = carry
        rows = pl.ds(pl.multiple_of(x * Y, Y), Y)
        weight, finish = xw[x, 0:Y, :], xo[x, 0:Y, :]
        out = []
        for c in range(C):
            value = live[c] + weight * (ay[c, rows, :] + lefts[c])
            fb[pl.ds(pl.multiple_of(c * PITCH + (x + 1) * PAD + 8, 8), Y), :] = value * finish
            out.append(value)
        halo = halo + xw[x, 16:32, :] * (ayh[rows, :] + left_halo)
        edge = halo * xo[x, 16:32, :]
        fb[pl.ds((x + 1) * PAD + 7, 8, stride=PITCH), :] = edge[0:8]
        fb[pl.ds((x + 2) * PAD, 8, stride=PITCH), :] = edge[8:16]
        return tuple(out), halo

    lax.fori_loop(0, X, x_finish, (tuple(rights), right_halo), unroll=4)

    sent_all(*ret_x)


def advection(fb, c0, ax, bx, ayp, byp, azn, bzp, out_h, out, sem):
    def advect(x, _):
        rows = pl.ds(pl.multiple_of(x * Y, Y), Y)
        middle = c0[rows, :]
        from_x, to_x = bx[rows, :], ax[pl.ds(pl.multiple_of((x + 2) * Y, Y), Y), :]
        from_y, to_y = byp[pl.ds(x * PAD + 7, Y), :], ayp[pl.ds(x * PAD + 9, Y), :]
        from_z, to_z = bzp[rows, :], azn[rows, :]
        for c in range(C):
            at = c * PITCH + (x + 1) * PAD + 8
            value = fb[pl.ds(pl.multiple_of(at, 8), Y), :]
            result = middle * value
            result += to_x * fb[pl.ds(pl.multiple_of(at + PAD, 8), Y), :]
            result -= from_x * fb[pl.ds(pl.multiple_of(at - PAD, 8), Y), :]
            result += to_y * fb[pl.ds(at + 1, Y), :]
            result -= from_y * fb[pl.ds(at - 1, Y), :]
            result += to_z * pltpu.roll(value, Z - 1, 1)
            result -= from_z * pltpu.roll(value, 1, 1)
            out[c, rows, :] = result
        return 0

    stores = []
    for part in range(4):
        lax.fori_loop(part * 8, part * 8 + 8, advect, 0, unroll=8)
        rows = pl.ds(part * 8 * Y, 8 * Y)
        store = pltpu.make_async_copy(out.at[:, rows, :], out_h.at[:, rows, :], sem.at[part])
        store.start()
        stores.append(store)
    for store in stores:
        store.wait()


def on_device(cotangent, diffusion, phase, courant, upwind):
    def vm(*shape, dtype=f32):
        return pltpu.VMEM(shape, dtype)

    dma = pltpu.SemaphoreType.DMA
    scratch = [
        vm(C, LINES, Z), vm(LINES, Z), vm(LINES, Z, dtype=jnp.int32), vm(3, LINES, Z), vm(3, LINES, Z, dtype=jnp.int32),
        vm(LINES, Z),
        vm(LINES // Z, Z, Z), vm(LINES, Z), vm(LINES, Z), vm(LINES, Z), vm(C, LINES, Z), vm(2, 2 * Z, Z, dtype=jnp.bfloat16),
        vm(Y, X, Z), vm(Y, X, Z), vm(Y, X, Z), vm(Y, X, Z), vm(X, Z), vm(C, Y, X, Z), vm(C, LINES, Z), vm(X * 16, Z), vm(LINES, Z), vm(LINES, Z), vm(4, LINES, Z),
        vm(X, 32, Z), vm(X, 32, Z), vm(X, 32, Z), vm(X, 32, Z), vm(X, 32, Z), vm(32, Z),
        vm(NJ * 8, Z), vm(NI * 16, Z), vm(NJ * 8, Z), vm(NI * 16, Z), vm(6, NJ, 16, Z), vm(6, NI, 16, Z), vm(2, NJ, 16, Z),
        vm(NJ * PACK, Z), vm(NJ * PACK, Z), vm(NJ * PACK, Z), vm(NJ * PACK, Z),
        vm(NI * STEP_X, Z), vm(NI * STEP_X, Z), vm(NI * STEP_X, Z), vm(NI * STEP_X, Z), vm(2, 16, Z),
        vm(2, X, Z), vm(2, X, Z), vm(2, X, Z), vm(2, X, Z), vm(2, Y, Z), vm(2, Y, Z),
        dma((8,)), dma((9,)), dma((9,)),
    ]
    vmem = pl.BlockSpec(memory_space=pltpu.VMEM)
    shapes = [(8 * PITCH, Z), (LINES, Z), (LINES + 2 * Y, Z), (LINES + 2 * Y, Z), (X * PAD + 8, Z), (X * PAD + 8, Z), (LINES, Z), (LINES, Z)]
    parts = pl.pallas_call(
        body,
        out_shape=[pltpu.VMEM(shape, f32) for shape in shapes],
        in_specs=[pl.BlockSpec(memory_space=pltpu.HBM)] * 5,
        out_specs=[vmem] * len(shapes),
        scratch_shapes=scratch,
        compiler_params=pltpu.CompilerParams(
            collective_id=0, has_side_effects=True, vmem_limit_bytes=40 * 1024 * 1024
        ),
    )(
        *(
            pltpu.with_memory_space_constraint(given, pltpu.HBM)
            for given in (
                cotangent.reshape(C, LINES, Z),
                diffusion.reshape(LINES, Z),
                phase.reshape(LINES, Z),
                courant.reshape(3, LINES, Z),
                upwind.reshape(3, LINES, Z),
            )
        )
    )
    out = pl.pallas_call(
        advection,
        out_shape=jax.ShapeDtypeStruct((C, LINES, Z), f32),
        in_specs=[vmem] * len(shapes),
        out_specs=pl.BlockSpec(memory_space=pl.ANY),
        scratch_shapes=[vm(C, LINES, Z), dma((4,))],
        compiler_params=pltpu.CompilerParams(vmem_limit_bytes=8 * 1024 * 1024),
    )(*(pltpu.with_memory_space_constraint(part, pltpu.VMEM) for part in parts))
    return out.reshape(C, X, Y, Z)


def solution(mesh):
    placed = (
        P(None, "gx", "gy", None),
        P("gx", "gy", None),
        P("gx", "gy", None),
        P(None, "gx", "gy", None),
        P(None, "gx", "gy", None),
    )
    return jax.shard_map(
        on_device, mesh=mesh, in_specs=placed, out_specs=P(None, "gx", "gy", None), check_vma=False
    )
```

```python
import functools

import jax
import jax.numpy as jnp
from jax import lax
from jax.experimental import pallas as pl
from jax.experimental.pallas import tpu as pltpu
from jax.sharding import PartitionSpec as P

MESH = pl.DeviceIdType.MESH
C, X, Y, Z = 6, 32, 16, 128
NI, NJ = 8, 16
LINES = X * Y
PAD = 24
PLANES = X + 2
PITCH = PLANES * PAD + 8
HALF = C * 2
PACK = 2 * HALF
HALF_X = HALF + 2
PACK_X = 2 * HALF_X
STEP_X = 32
f32 = jnp.float32
FAR = sorted(((a, b) for a in range(4) for b in range(4) if a or b), key=lambda d: -min(d[0], 4 - d[0]) - min(d[1], 4 - d[1]))
ORDER = (0, 2, 1, 3)
FAR_X = [(2, 1), (2, 0), (3, 1), (1, 1), (3, 0), (1, 0), (0, 1)]


def split(values):
    high = values.astype(jnp.bfloat16)
    low = (values - high.astype(f32)).astype(jnp.bfloat16)
    return jnp.concatenate([high, low], axis=1)


def body(
    cot_h, dif_h, pha_h, cou_h, upw_h,
    fb, c0, ax, bx, ayp, byp, azn, bzp,
    cot, dif, pha, cou, upw, ec,
    et, zt, zw, zo, zb, tri,
    yb, ya, yw, yo, yr, yf, ay, ayh, ynl, ynr, ends,
    xe, xb, xa, xw, xo, xr,
    csy, csx, rcy, rcx, ky, kx, gl,
    sty, tty, oty, rty, stx, ttx, otx, rtx, ext,
    fse, fre, fsy, fry, fsx, frx,
    in_sem,
    sent, came,
):
    i = lax.axis_index("gx")
    j = lax.axis_index("gy")
    inext, iprev = lax.rem(i + 1, NI), lax.rem(i + NI - 1, NI)
    jnext, jprev = lax.rem(j + 1, NJ), lax.rem(j + NJ - 1, NJ)

    loads = [
        pltpu.make_async_copy(dif_h, dif, in_sem.at[0]),
        pltpu.make_async_copy(pha_h, pha, in_sem.at[1]),
        pltpu.make_async_copy(cou_h, cou, in_sem.at[2]),
        pltpu.make_async_copy(upw_h, upw, in_sem.at[3]),
    ]
    quarters = [pl.ds(q * 8 * Y, 8 * Y) for q in range(4)]
    fields = [
        pltpu.make_async_copy(cot_h.at[:, rows, :], cot.at[:, rows, :], in_sem.at[4 + q])
        for q, rows in enumerate(quarters)
    ]
    loads[0].start()
    loads[1].start()
    for q in ORDER:
        fields[q].start()

    barrier = pltpu.get_barrier_semaphore()

    def greet_y(d, _):
        pl.semaphore_signal(barrier, inc=1, device_id=(i, lax.rem(j + d, NJ)), device_id_type=MESH)
        return 0

    def greet_x(d, _):
        pl.semaphore_signal(barrier, inc=1, device_id=(lax.rem(i + d, NI), j), device_id_type=MESH)
        return 0

    lax.fori_loop(1, NJ, greet_y, 0)
    lax.fori_loop(1, NI, greet_x, 0)

    loads[0].wait()
    loads[1].wait()
    ec[...] = 1.0 / (dif[...] * (1.0 + 3.0 * pha[...].astype(f32)))

    for q in range(X // 8):
        xs = pl.ds(q * 8, 8)
        cells = [ec[pl.ds(q * 8 * Y + y, 8, stride=Y), :] for y in range(Y)]
        theta = jnp.ones((8, Z), f32)
        delta = jnp.ones((8, Z), f32)
        for y in range(Y):
            yb[y, xs, :] = theta
            delta = delta + cells[y] * theta
            theta = theta + delta
        rn = 1.0 / theta
        yr[xs, :] = rn
        phi = jnp.ones((8, Z), f32)
        delta = jnp.ones((8, Z), f32)
        after = jnp.ones((8, Z), f32)
        at = (q % 2) * 8 * 8 + q // 2
        for y in range(Y - 1, -1, -1):
            a = phi * rn
            b = yb[y, xs, :] * rn
            ya[y, xs, :] = a
            yb[y, xs, :] = b
            yw[y, xs, :] = 1.0 / (b * after)
            yo[y, xs, :] = b * cells[y]
            if y == Y - 1:
                csy[pl.ds(at + 4, 8, stride=8), :] = b
            if y == 0:
                csy[pl.ds(at, 8, stride=8), :] = a
            after = b
            delta = delta + cells[y] * phi
            phi = phi + delta
        csy[pl.ds(at + 2, 8, stride=8), :] = rn

    seg = lax.broadcasted_iota(jnp.int32, (8, Z), 0)
    span = Z // 8
    tiles = LINES // Z
    for t in range(tiles):
        et[t] = ec[t * Z : (t + 1) * Z, :].T
    ones = jnp.ones((8, Z), f32)
    zeros = jnp.zeros((8, Z), f32)

    def cell(t, step):
        return et[t, pl.ds(step, 8, stride=span), :]

    starts = []
    for t in range(tiles):
        p11, p12, p21, p22 = ones, zeros, zeros, ones
        for step in range(span):
            e = cell(t, step)
            p21 = p21 + e * p11
            p22 = p22 + e * p12
            p11 = p11 + p21
            p12 = p12 + p22
        for shift in (1, 2, 4):
            keep = seg < shift
            q11 = jnp.where(keep, 1.0, pltpu.roll(p11, shift, 0))
            q12 = jnp.where(keep, 0.0, pltpu.roll(p12, shift, 0))
            q21 = jnp.where(keep, 0.0, pltpu.roll(p21, shift, 0))
            q22 = jnp.where(keep, 1.0, pltpu.roll(p22, shift, 0))
            p11, p12, p21, p22 = (
                p11 * q11 + p12 * q21,
                p11 * q12 + p12 * q22,
                p21 * q11 + p22 * q21,
                p21 * q12 + p22 * q22,
            )
        theta = jnp.where(seg < 1, 1.0, pltpu.roll(p11 + p12, 1, 0))
        delta = jnp.where(seg < 1, 1.0, pltpu.roll(p21 + p22, 1, 0))
        starts.append((theta, delta))
    for t in range(tiles):
        theta, delta = starts[t]
        for step in range(span):
            delta = delta + cell(t, step) * theta
            theta = theta + delta
            et[t, pl.ds(step, 8, stride=span), :] = theta
    lane = lax.broadcasted_iota(jnp.int32, (Z, Z), 1)
    for t in range(tiles):
        rows = pl.ds(t * Z, Z)
        theta = et[t].T
        before = jnp.where(lane < 1, 1.0, pltpu.roll(theta, 1, 1))
        zt[rows, :] = before
        zw[rows, :] = 1.0 / (theta * before)
        zo[rows, :] = before * ec[rows, :]

    row = lax.rem(lax.broadcasted_iota(jnp.int32, (2 * Z, Z), 0), Z)
    col = lax.broadcasted_iota(jnp.int32, (2 * Z, Z), 1)
    tri[0] = (row <= col).astype(f32).astype(jnp.bfloat16)
    tri[1] = (row >= col).astype(f32).astype(jnp.bfloat16)

    def exchange(src, dst, slot, pitch, rows, k, axis):
        here = j if axis == "gy" else i
        return pltpu.make_async_remote_copy(
            src_ref=src.at[pl.ds(pl.multiple_of(k * pitch, 8), rows), :],
            dst_ref=dst.at[pl.ds(pl.multiple_of(here * pitch, 8), rows), :],
            send_sem=sent.at[slot],
            recv_sem=came.at[slot],
            device_id={axis: k},
            device_id_type=MESH,
        )

    def whole_round(src, dst, slot, pitch, rows, axis):
        total = pl.ds(0, rows * ((NJ if axis == "gy" else NI) - 1))
        return pltpu.make_async_remote_copy(
            src_ref=src.at[total, :],
            dst_ref=dst.at[total, :],
            send_sem=sent.at[slot],
            recv_sem=came.at[slot],
            device_id={axis: jnext if axis == "gy" else inext},
            device_id_type=MESH,
        )

    def peers(axis):
        if axis == "gy":
            return [lax.rem(j // 4 + a, 4) * 4 + lax.rem(j + b, 4) for a, b in FAR]
        return [lax.rem(i // 2 + a, 4) * 2 + lax.rem(i + b, 2) for a, b in FAR_X]

    def send_all(src, dst, slot, pitch, rows, axis):
        here = j if axis == "gy" else i
        mine = pl.ds(pl.multiple_of(here * pitch, 8), rows)
        for k in peers(axis):
            exchange(src, dst, slot, pitch, rows, k, axis).start()
        dst[mine, :] = src[mine, :]

    def recv_all(src, dst, slot, pitch, rows, axis):
        whole_round(src, dst, slot, pitch, rows, axis).wait_recv()

    def sent_all(src, dst, slot, pitch, rows, axis):
        whole_round(src, dst, slot, pitch, rows, axis).wait_send()

    coup_y = (csy, rcy, 0, 8, 8, "gy")
    coup_x = (csx, rcx, 1, 16, 16, "gx")
    tot_y = (sty, tty, 2, PACK, PACK, "gy")
    ret_y = (oty, rty, 3, PACK, PACK, "gy")
    tot_x = (stx, ttx, 4, STEP_X, PACK_X, "gx")
    ret_x = (otx, rtx, 5, STEP_X, PACK_X, "gx")

    def face(src, dst, slot, part, axis, to):
        return pltpu.make_async_remote_copy(
            src_ref=src.at[part], dst_ref=dst.at[part], send_sem=sent.at[slot], recv_sem=came.at[slot],
            device_id={axis: to}, device_id_type=MESH,
        )

    def both(src, dst, slot):
        return pltpu.make_async_remote_copy(
            src_ref=src, dst_ref=dst, send_sem=sent.at[slot], recv_sem=came.at[slot],
            device_id={"gy": jnext}, device_id_type=MESH,
        )

    edges = [
        face(fse, fre, 6, 0, "gy", jprev),
        face(fse, fre, 6, 1, "gy", jnext),
    ]
    faces = [
        face(fsy, fry, 7, 0, "gy", jprev),
        face(fsy, fry, 7, 1, "gy", jnext),
        face(fsx, frx, 8, 0, "gx", iprev),
        face(fsx, frx, 8, 1, "gx", inext),
    ]
    pairs = [both(fse, fre, 6), both(fsy, fry, 7), both(fsx, frx, 8)]
    def z_lower(q):
        rows = quarters[q]
        scale, weight = zt[rows, :], zw[rows, :]
        for c in range(C):
            zb[c, rows, :] = weight * jnp.dot(
                split(cot[c, rows, :] * scale), tri[0], preferred_element_type=f32
            )

    def z_upper(q):
        rows = quarters[q]
        finish = zo[rows, :]
        for c in range(C):
            zb[c, rows, :] = finish * jnp.dot(split(zb[c, rows, :]), tri[1], preferred_element_type=f32)

    def y_totals(q):
        xs = pl.ds(q * 8, 8)
        heads = [jnp.zeros((8, Z), f32) for _ in range(C)]
        tails = [jnp.zeros((8, Z), f32) for _ in range(C)]
        for y in range(Y):
            a, b = ya[y, xs, :], yb[y, xs, :]
            for c in range(C):
                value = zb[c, pl.ds(q * 8 * Y + y, 8, stride=Y), :]
                heads[c] = heads[c] + a * value
                tails[c] = tails[c] + b * value
                yf[c, y, xs, :] = tails[c]
        at = (q % 2) * 8 * PACK + (q // 2) * C
        for c in range(C):
            sty[pl.ds(at + c, 8, stride=PACK), :] = heads[c]
            sty[pl.ds(at + HALF + c, 8, stride=PACK), :] = tails[c]

    for q in ORDER:
        fields[q].wait()
    loads[2].start()
    loads[3].start()
    z_lower(0)
    for q in range(4):
        if q < 3:
            z_lower(q + 1)
        z_upper(q)
        y_totals(q)

    pl.semaphore_wait(barrier, NI + NJ - 2)
    send_all(*tot_y)
    send_all(*coup_y)
    fse[0] = ec[pl.ds(0, X, stride=Y), :]
    fse[1] = ec[pl.ds(Y - 1, X, stride=Y), :]
    for e in edges:
        e.start()

    loads[2].wait()
    loads[3].wait()
    fsy[0] = upw[1, pl.ds(0, X, stride=Y), :].astype(f32) * cou[1, pl.ds(0, X, stride=Y), :]
    fsy[1] = (1.0 - upw[1, pl.ds(Y - 1, X, stride=Y), :].astype(f32)) * cou[1, pl.ds(Y - 1, X, stride=Y), :]
    fsx[0] = upw[0, 0:Y, :].astype(f32) * cou[0, 0:Y, :] * ec[0:Y, :]
    fsx[1] = (1.0 - upw[0, LINES - Y : LINES, :].astype(f32)) * cou[0, LINES - Y : LINES, :] * ec[LINES - Y : LINES, :]

    for f in faces:
        f.start()

    def reduce_factor(count, pitch, lines, half, couplings, factors):
        def spread(base, t):
            at = base + len(lines) * t
            return jnp.concatenate(
                [jnp.broadcast_to(couplings[pl.ds(at + n, 1), :], (wide, Z)) for n, wide in enumerate(lines)],
                axis=0,
            )

        edge = jnp.zeros((half, Z), f32)
        for m in range(count):
            a1, b1, bn = spread(m * pitch, 0), spread(m * pitch, 1), spread(m * pitch, 2)
            alpha = 1.0 / (1.0 - a1 * edge)
            alpha_a = a1 * alpha
            forward = b1 * alpha
            back = b1 * edge
            factors[0, m, 0:half, :] = alpha
            factors[1, m, 0:half, :] = alpha_a
            factors[2, m, 0:half, :] = forward
            factors[3, m, 0:half, :] = edge
            factors[4, m, 0:half, :] = back * alpha
            factors[5, m, 0:half, :] = b1 + back * alpha_a
            edge = bn + back * forward

    def reduce_solve(count, pitch, half, totals, factors, results):
        gain = jnp.zeros((half, Z), f32)
        for m in range(count):
            head = totals[m * pitch : m * pitch + half, :]
            tail = totals[m * pitch + half : m * pitch + 2 * half, :]
            gl[0, m, 0:half, :] = gain
            gl[1, m, 0:half, :] = factors[0, m, 0:half, :] * head + factors[1, m, 0:half, :] * gain
            gain = tail + factors[4, m, 0:half, :] * head + factors[5, m, 0:half, :] * gain
        later = jnp.zeros((half, Z), f32)
        for m in range(count - 1, -1, -1):
            results[m * pitch + half : m * pitch + 2 * half, :] = later
            later = gl[1, m, 0:half, :] + factors[2, m, 0:half, :] * later
            results[m * pitch : m * pitch + half, :] = gl[0, m, 0:half, :] + factors[3, m, 0:half, :] * later

    low_ok = jnp.where(j > 0, 1.0, 0.0).astype(f32)
    high_ok = jnp.where(j < NJ - 1, 1.0, 0.0).astype(f32)
    lane16 = lax.broadcasted_iota(jnp.int32, (Y, Z), 1)

    def coefficients(x, _):
        rows = pl.ds(pl.multiple_of(x * Y, Y), Y)
        shifted = pl.ds(pl.multiple_of(x * Y + Y, Y), Y)
        padded = pl.ds(pl.multiple_of(x * PAD + 8, 8), Y)
        flux = [cou[d, rows, :] for d in range(3)]
        ahead = [upw[d, rows, :].astype(f32) * flux[d] for d in range(3)]
        behind = [flux[d] - ahead[d] for d in range(3)]
        c0[rows, :] = 1.0 + (behind[0] - ahead[0]) + (behind[1] - ahead[1]) + (behind[2] - ahead[2])
        ax[shifted, :] = ahead[0]
        bx[shifted, :] = behind[0]
        ayp[padded, :] = ahead[1]
        byp[padded, :] = behind[1]
        azn[rows, :] = jnp.where(lane16 < Z - 1, pltpu.roll(ahead[2], Z - 1, 1), 0.0)
        bzp[rows, :] = jnp.where(lane16 > 0, pltpu.roll(behind[2], 1, 1), 0.0)
        return 0

    lax.fori_loop(0, X, coefficients, 0, unroll=8)
    ayh[...] = jnp.zeros_like(ayh)

    for q in range(4):
        xs = pl.ds(q * 8, 8)
        live = [jnp.zeros((8, Z), f32) for _ in range(C)]
        summed = jnp.zeros((8, Z), f32)
        for y in range(Y - 1, -1, -1):
            cells = pl.ds(q * 8 * Y + y, 8, stride=Y)
            weight, finish = yw[y, xs, :], yo[y, xs, :]
            summed = summed + weight
            ynl[cells, :] = finish * (summed * yr[xs, :])
            ynr[cells, :] = finish
            for c in range(C):
                live[c] = live[c] + weight * yf[c, y, xs, :]
                ay[c, cells, :] = live[c] * finish

    recv_all(*coup_y)
    reduce_factor(NJ, 8, (C, C), HALF, rcy, ky)

    recv_all(*tot_y)
    reduce_solve(NJ, PACK, HALF, tty, ky, oty)
    send_all(*ret_y)

    def x_factor():
        rows = pl.ds(0, 32)
        one = jnp.ones((32, Z), f32)

        def up(x, carry):
            theta, delta = carry
            xb[x, rows, :] = theta
            delta = delta + xe[x, rows, :] * theta
            return theta + delta, delta

        theta, _ = lax.fori_loop(0, X, up, (one, one), unroll=8)
        rn = 1.0 / theta
        xr[rows, :] = rn

        def down(step, carry):
            x = X - 1 - step
            phi, delta, after, _ = carry
            cell = xe[x, rows, :]
            a = phi * rn
            b = xb[x, rows, :] * rn
            xa[x, rows, :] = a
            xb[x, rows, :] = b
            xw[x, rows, :] = 1.0 / (b * after)
            xo[x, rows, :] = b * cell
            delta = delta + cell * phi
            return phi + delta, delta, b, a

        _, _, _, first = lax.fori_loop(0, X, down, (one, one, one, one), unroll=8)
        return first, rn

    pairs[0].wait_recv()
    for x in range(X):
        xe[x, 0:Y, :] = ec[x * Y : (x + 1) * Y, :]
        xe[x, 16:24, :] = jnp.broadcast_to(fre[1, x : x + 1, :], (8, Z))
        xe[x, 24:32, :] = jnp.broadcast_to(fre[0, x : x + 1, :], (8, Z))
    first, rn = x_factor()
    for t, part in enumerate((first, rn, xb[X - 1])):
        for r in range(2):
            csx[pl.ds(4 * t + r, 8, stride=16), :] = part[r * 8 : r * 8 + 8]
        csx[pl.ds(4 * t + 2, C, stride=16), :] = part[16 : 16 + C]
        csx[pl.ds(C * 16 + 4 * t + 2, 8 - C, stride=16), :] = part[24 : 32 - C]
        csx[pl.ds(4 * t + 3, 8, stride=16), :] = part[24:32]

    send_all(*coup_x)

    def x_totals(x, carry):
        heads, tails = carry
        rows = pl.ds(pl.multiple_of(x * Y, Y), Y)
        a, b = xa[x, 0:Y, :], xb[x, 0:Y, :]
        left, right = ynl[rows, :], ynr[rows, :]
        ends[0, rows, :] = a * left
        ends[1, rows, :] = a * right
        ends[2, rows, :] = b * left
        ends[3, rows, :] = b * right
        values = [ay[c, rows, :] for c in range(C)]
        return (
            tuple(heads[c] + a * values[c] for c in range(C)),
            tuple(tails[c] + b * values[c] for c in range(C)),
        )

    none = jnp.zeros((Y, Z), f32)
    heads, tails = lax.fori_loop(0, X, x_totals, ((none,) * C, (none,) * C), unroll=8)
    heads, tails = list(heads), list(tails)

    recv_all(*ret_y)

    def end_values(x, c):
        at = lax.rem(x, NJ) * PACK + (x // NJ) * C + c
        return (
            jnp.broadcast_to(rty[pl.ds(at, 1), :], (Y, Z)),
            jnp.broadcast_to(rty[pl.ds(at + HALF, 1), :], (Y, Z)),
        )

    for q in range(4):
        xs = pl.ds(q * 8, 8)
        at = (q % 2) * 8 * PACK + (q // 2) * C
        for c in range(C):
            left = rty[pl.ds(at + c, 8, stride=PACK), :]
            right = rty[pl.ds(at + HALF + c, 8, stride=PACK), :]
            ayh[pl.ds(q * 8 * 16 + c, 8, stride=16), :] = left * fre[1, xs, :]
            ayh[pl.ds(q * 8 * 16 + 8 + c, 8, stride=16), :] = right * fre[0, xs, :]

    def end_totals(x, carry):
        heads, tails, halo_head, halo_tail = carry
        rows = pl.ds(pl.multiple_of(x * Y, Y), Y)
        hl, hr, tl, tr = (ends[n, rows, :] for n in range(4))
        pairs_of = [end_values(x, c) for c in range(C)]
        value = ayh[rows, :]
        return (
            tuple(heads[c] + (hl * left + hr * right) for c, (left, right) in enumerate(pairs_of)),
            tuple(tails[c] + (tl * left + tr * right) for c, (left, right) in enumerate(pairs_of)),
            halo_head + xa[x, 16:32, :] * value,
            halo_tail + xb[x, 16:32, :] * value,
        )

    heads, tails, *edge_pair = lax.fori_loop(
        0, X, end_totals, (tuple(heads), tuple(tails), none, none), unroll=8
    )
    for c in range(C):
        for r in range(2):
            stx[pl.ds(r * C + c, 8, stride=STEP_X), :] = heads[c][r * 8 : r * 8 + 8]
            stx[pl.ds(HALF_X + r * C + c, 8, stride=STEP_X), :] = tails[c][r * 8 : r * 8 + 8]
    for end, part in enumerate(edge_pair):
        at = end * HALF_X + HALF
        stx[pl.ds(at, C, stride=STEP_X), :] = part[0:C]
        stx[pl.ds(C * STEP_X + at, 8 - C, stride=STEP_X), :] = part[8 : 16 - C]
        stx[pl.ds(at + 1, 2 * C - 8, stride=STEP_X), :] = part[16 - C : 8 + C]
    send_all(*tot_x)

    def x_prefix(x, carry):
        tails, halo = carry
        rows = pl.ds(pl.multiple_of(x * Y, Y), Y)
        b = xb[x, 0:Y, :]
        by_left, by_right = ynl[rows, :], ynr[rows, :]
        out = []
        for c in range(C):
            left, right = end_values(x, c)
            tail = tails[c] + b * (ay[c, rows, :] + by_left * left + by_right * right)
            ay[c, rows, :] = tail
            out.append(tail)
        halo = halo + xb[x, 16:32, :] * ayh[rows, :]
        ayh[rows, :] = halo
        return tuple(out), halo

    lax.fori_loop(0, X, x_prefix, ((none,) * C, none), unroll=8)
    recv_all(*coup_x)
    reduce_factor(NI, 16, (C, C, 1, 1), HALF_X, rcx, kx)
    sent_all(*coup_y)
    sent_all(*coup_x)
    sent_all(*tot_y)
    sent_all(*ret_y)
    for pair in pairs:
        pair.wait_send()
    recv_all(*tot_x)
    reduce_solve(NI, STEP_X, HALF_X, ttx, kx, otx)
    send_all(*ret_x)
    pairs[1].wait_recv()
    pairs[2].wait_recv()
    bx[0:Y, :] = frx[1]
    ax[(X + 1) * Y : (X + 2) * Y, :] = frx[0]
    byp[pl.ds(7, X, stride=PAD), :] = fry[1] * low_ok
    ayp[pl.ds(PAD, X, stride=PAD), :] = fry[0] * high_ok

    sent_all(*tot_x)
    recv_all(*ret_x)

    lefts, rights = [], []
    for c in range(C):
        left = jnp.concatenate([rtx[pl.ds(r * C + c, 8, stride=STEP_X), :] for r in range(2)], axis=0)
        right = jnp.concatenate([rtx[pl.ds(HALF_X + r * C + c, 8, stride=STEP_X), :] for r in range(2)], axis=0)
        fb[pl.ds(c * PITCH + 8, Y), :] = left
        fb[pl.ds(c * PITCH + (X + 1) * PAD + 8, Y), :] = right
        lefts.append(left * xr[0:Y, :])
        rights.append(right)
    for end in range(2):
        at = end * HALF_X + HALF
        ext[end, 0:C, :] = rtx[pl.ds(at, C, stride=STEP_X), :]
        ext[end, 8 : 16 - C, :] = rtx[pl.ds(C * STEP_X + at, 8 - C, stride=STEP_X), :]
        ext[end, 16 - C : 8 + C, :] = rtx[pl.ds(at + 1, 2 * C - 8, stride=STEP_X), :]
    left_halo = ext[0] * xr[16:32, :]
    right_halo = ext[1]

    def x_finish(step, carry):
        x = X - 1 - step
        live, halo = carry
        rows = pl.ds(pl.multiple_of(x * Y, Y), Y)
        weight, finish = xw[x, 0:Y, :], xo[x, 0:Y, :]
        out = []
        for c in range(C):
            value = live[c] + weight * (ay[c, rows, :] + lefts[c])
            fb[pl.ds(pl.multiple_of(c * PITCH + (x + 1) * PAD + 8, 8), Y), :] = value * finish
            out.append(value)
        halo = halo + xw[x, 16:32, :] * (ayh[rows, :] + left_halo)
        edge = halo * xo[x, 16:32, :]
        fb[pl.ds((x + 1) * PAD + 7, 8, stride=PITCH), :] = edge[0:8]
        fb[pl.ds((x + 2) * PAD, 8, stride=PITCH), :] = edge[8:16]
        return tuple(out), halo

    lax.fori_loop(0, X, x_finish, (tuple(rights), right_halo), unroll=4)

    sent_all(*ret_x)


def advection(fb, c0, ax, bx, ayp, byp, azn, bzp, out_h, out, sem):
    def advect(x, _):
        rows = pl.ds(pl.multiple_of(x * Y, Y), Y)
        middle = c0[rows, :]
        from_x, to_x = bx[rows, :], ax[pl.ds(pl.multiple_of((x + 2) * Y, Y), Y), :]
        from_y, to_y = byp[pl.ds(x * PAD + 7, Y), :], ayp[pl.ds(x * PAD + 9, Y), :]
        from_z, to_z = bzp[rows, :], azn[rows, :]
        for c in range(C):
            at = c * PITCH + (x + 1) * PAD + 8
            value = fb[pl.ds(pl.multiple_of(at, 8), Y), :]
            result = middle * value
            result += to_x * fb[pl.ds(pl.multiple_of(at + PAD, 8), Y), :]
            result -= from_x * fb[pl.ds(pl.multiple_of(at - PAD, 8), Y), :]
            result += to_y * fb[pl.ds(at + 1, Y), :]
            result -= from_y * fb[pl.ds(at - 1, Y), :]
            result += to_z * pltpu.roll(value, Z - 1, 1)
            result -= from_z * pltpu.roll(value, 1, 1)
            out[c, rows, :] = result
        return 0

    stores = []
    for part in range(4):
        lax.fori_loop(part * 8, part * 8 + 8, advect, 0, unroll=8)
        rows = pl.ds(part * 8 * Y, 8 * Y)
        store = pltpu.make_async_copy(out.at[:, rows, :], out_h.at[:, rows, :], sem.at[part])
        store.start()
        stores.append(store)
    for store in stores:
        store.wait()


def on_device(cotangent, diffusion, phase, courant, upwind):
    def vm(*shape, dtype=f32):
        return pltpu.VMEM(shape, dtype)

    dma = pltpu.SemaphoreType.DMA
    scratch = [
        vm(C, LINES, Z), vm(LINES, Z), vm(LINES, Z, dtype=jnp.int32), vm(3, LINES, Z), vm(3, LINES, Z, dtype=jnp.int32),
        vm(LINES, Z),
        vm(LINES // Z, Z, Z), vm(LINES, Z), vm(LINES, Z), vm(LINES, Z), vm(C, LINES, Z), vm(2, 2 * Z, Z, dtype=jnp.bfloat16),
        vm(Y, X, Z), vm(Y, X, Z), vm(Y, X, Z), vm(Y, X, Z), vm(X, Z), vm(C, Y, X, Z), vm(C, LINES, Z), vm(X * 16, Z), vm(LINES, Z), vm(LINES, Z), vm(4, LINES, Z),
        vm(X, 32, Z), vm(X, 32, Z), vm(X, 32, Z), vm(X, 32, Z), vm(X, 32, Z), vm(32, Z),
        vm(NJ * 8, Z), vm(NI * 16, Z), vm(NJ * 8, Z), vm(NI * 16, Z), vm(6, NJ, 16, Z), vm(6, NI, 16, Z), vm(2, NJ, 16, Z),
        vm(NJ * PACK, Z), vm(NJ * PACK, Z), vm(NJ * PACK, Z), vm(NJ * PACK, Z),
        vm(NI * STEP_X, Z), vm(NI * STEP_X, Z), vm(NI * STEP_X, Z), vm(NI * STEP_X, Z), vm(2, 16, Z),
        vm(2, X, Z), vm(2, X, Z), vm(2, X, Z), vm(2, X, Z), vm(2, Y, Z), vm(2, Y, Z),
        dma((8,)), dma((9,)), dma((9,)),
    ]
    vmem = pl.BlockSpec(memory_space=pltpu.VMEM)
    shapes = [(8 * PITCH, Z), (LINES, Z), (LINES + 2 * Y, Z), (LINES + 2 * Y, Z), (X * PAD + 8, Z), (X * PAD + 8, Z), (LINES, Z), (LINES, Z)]
    parts = pl.pallas_call(
        body,
        out_shape=[pltpu.VMEM(shape, f32) for shape in shapes],
        in_specs=[pl.BlockSpec(memory_space=pltpu.HBM)] * 5,
        out_specs=[vmem] * len(shapes),
        scratch_shapes=scratch,
        compiler_params=pltpu.CompilerParams(
            collective_id=0, has_side_effects=True, vmem_limit_bytes=40 * 1024 * 1024
        ),
    )(
        *(
            pltpu.with_memory_space_constraint(given, pltpu.HBM)
            for given in (
                cotangent.reshape(C, LINES, Z),
                diffusion.reshape(LINES, Z),
                phase.reshape(LINES, Z),
                courant.reshape(3, LINES, Z),
                upwind.reshape(3, LINES, Z),
            )
        )
    )
    out = pl.pallas_call(
        advection,
        out_shape=jax.ShapeDtypeStruct((C, LINES, Z), f32),
        in_specs=[vmem] * len(shapes),
        out_specs=pl.BlockSpec(memory_space=pl.ANY),
        scratch_shapes=[vm(C, LINES, Z), dma((4,))],
        compiler_params=pltpu.CompilerParams(vmem_limit_bytes=8 * 1024 * 1024),
    )(*(pltpu.with_memory_space_constraint(part, pltpu.VMEM) for part in parts))
    return out.reshape(C, X, Y, Z)


def solution(mesh):
    placed = (
        P(None, "gx", "gy", None),
        P("gx", "gy", None),
        P("gx", "gy", None),
        P(None, "gx", "gy", None),
        P(None, "gx", "gy", None),
    )
    return jax.shard_map(
        on_device, mesh=mesh, in_specs=placed, out_specs=P(None, "gx", "gy", None), check_vma=False
    )
```

```python
import functools

import jax
import jax.numpy as jnp
from jax import lax
from jax.experimental import pallas as pl
from jax.experimental.pallas import tpu as pltpu
from jax.sharding import PartitionSpec as P

MESH = pl.DeviceIdType.MESH
C, X, Y, Z = 6, 32, 16, 128
NI, NJ = 8, 16
LINES = X * Y
PAD = 24
PLANES = X + 2
PITCH = PLANES * PAD + 8
HALF = C * 2
PACK = 2 * HALF
HALF_X = HALF + 2
PACK_X = 2 * HALF_X
STEP_X = 32
f32 = jnp.float32
FAR = sorted(((a, b) for a in range(4) for b in range(4) if a or b), key=lambda d: -min(d[0], 4 - d[0]) - min(d[1], 4 - d[1]))
ORDER = (0, 2, 1, 3)
FAR_X = [(2, 1), (2, 0), (3, 1), (1, 1), (3, 0), (1, 0), (0, 1)]


def split(values):
    high = values.astype(jnp.bfloat16)
    low = (values - high.astype(f32)).astype(jnp.bfloat16)
    return jnp.concatenate([high, low], axis=1)


def body(
    cot_h, dif_h, pha_h, cou_h, upw_h,
    ay, ayh, xl, xo, lr, lrh, c0, ax, bx, ayp, byp, azn, bzp,
    cot, dif, pha, cou, upw, ec,
    et, zt, zw, zo, zb, tri,
    yb, ya, yw, yo, yr, yf, ynl, ynr, ends,
    xe, xb, xa, xw, xr,
    csy, csx, rcy, rcx, ky, kx, gl,
    sty, tty, oty, rty, stx, ttx, otx, rtx,
    fse, fre, fsy, fry, fsx, frx,
    in_sem,
    sent, came,
):
    i = lax.axis_index("gx")
    j = lax.axis_index("gy")
    inext, iprev = lax.rem(i + 1, NI), lax.rem(i + NI - 1, NI)
    jnext, jprev = lax.rem(j + 1, NJ), lax.rem(j + NJ - 1, NJ)

    loads = [
        pltpu.make_async_copy(dif_h, dif, in_sem.at[0]),
        pltpu.make_async_copy(pha_h, pha, in_sem.at[1]),
        pltpu.make_async_copy(cou_h, cou, in_sem.at[2]),
        pltpu.make_async_copy(upw_h, upw, in_sem.at[3]),
    ]
    quarters = [pl.ds(q * 8 * Y, 8 * Y) for q in range(4)]
    fields = [
        pltpu.make_async_copy(cot_h.at[:, rows, :], cot.at[:, rows, :], in_sem.at[4 + q])
        for q, rows in enumerate(quarters)
    ]
    loads[0].start()
    loads[1].start()
    for q in ORDER:
        fields[q].start()

    barrier = pltpu.get_barrier_semaphore()

    def greet_y(d, _):
        pl.semaphore_signal(barrier, inc=1, device_id=(i, lax.rem(j + d, NJ)), device_id_type=MESH)
        return 0

    def greet_x(d, _):
        pl.semaphore_signal(barrier, inc=1, device_id=(lax.rem(i + d, NI), j), device_id_type=MESH)
        return 0

    lax.fori_loop(1, NJ, greet_y, 0)
    lax.fori_loop(1, NI, greet_x, 0)

    loads[0].wait()
    loads[1].wait()
    ec[...] = 1.0 / (dif[...] * (1.0 + 3.0 * pha[...].astype(f32)))

    for q in range(X // 8):
        xs = pl.ds(q * 8, 8)
        cells = [ec[pl.ds(q * 8 * Y + y, 8, stride=Y), :] for y in range(Y)]
        theta = jnp.ones((8, Z), f32)
        delta = jnp.ones((8, Z), f32)
        for y in range(Y):
            yb[y, xs, :] = theta
            delta = delta + cells[y] * theta
            theta = theta + delta
        rn = 1.0 / theta
        yr[xs, :] = rn
        phi = jnp.ones((8, Z), f32)
        delta = jnp.ones((8, Z), f32)
        after = jnp.ones((8, Z), f32)
        at = (q % 2) * 8 * 8 + q // 2
        for y in range(Y - 1, -1, -1):
            a = phi * rn
            b = yb[y, xs, :] * rn
            ya[y, xs, :] = a
            yb[y, xs, :] = b
            yw[y, xs, :] = 1.0 / (b * after)
            yo[y, xs, :] = b * cells[y]
            if y == Y - 1:
                csy[pl.ds(at + 4, 8, stride=8), :] = b
            if y == 0:
                csy[pl.ds(at, 8, stride=8), :] = a
            after = b
            delta = delta + cells[y] * phi
            phi = phi + delta
        csy[pl.ds(at + 2, 8, stride=8), :] = rn

    seg = lax.broadcasted_iota(jnp.int32, (8, Z), 0)
    span = Z // 8
    tiles = LINES // Z
    for t in range(tiles):
        et[t] = ec[t * Z : (t + 1) * Z, :].T
    ones = jnp.ones((8, Z), f32)
    zeros = jnp.zeros((8, Z), f32)

    def cell(t, step):
        return et[t, pl.ds(step, 8, stride=span), :]

    starts = []
    for t in range(tiles):
        p11, p12, p21, p22 = ones, zeros, zeros, ones
        for step in range(span):
            e = cell(t, step)
            p21 = p21 + e * p11
            p22 = p22 + e * p12
            p11 = p11 + p21
            p12 = p12 + p22
        for shift in (1, 2, 4):
            keep = seg < shift
            q11 = jnp.where(keep, 1.0, pltpu.roll(p11, shift, 0))
            q12 = jnp.where(keep, 0.0, pltpu.roll(p12, shift, 0))
            q21 = jnp.where(keep, 0.0, pltpu.roll(p21, shift, 0))
            q22 = jnp.where(keep, 1.0, pltpu.roll(p22, shift, 0))
            p11, p12, p21, p22 = (
                p11 * q11 + p12 * q21,
                p11 * q12 + p12 * q22,
                p21 * q11 + p22 * q21,
                p21 * q12 + p22 * q22,
            )
        theta = jnp.where(seg < 1, 1.0, pltpu.roll(p11 + p12, 1, 0))
        delta = jnp.where(seg < 1, 1.0, pltpu.roll(p21 + p22, 1, 0))
        starts.append((theta, delta))
    for t in range(tiles):
        theta, delta = starts[t]
        for step in range(span):
            delta = delta + cell(t, step) * theta
            theta = theta + delta
            et[t, pl.ds(step, 8, stride=span), :] = theta
    lane = lax.broadcasted_iota(jnp.int32, (Z, Z), 1)
    for t in range(tiles):
        rows = pl.ds(t * Z, Z)
        theta = et[t].T
        before = jnp.where(lane < 1, 1.0, pltpu.roll(theta, 1, 1))
        zt[rows, :] = before
        zw[rows, :] = 1.0 / (theta * before)
        zo[rows, :] = before * ec[rows, :]

    row = lax.rem(lax.broadcasted_iota(jnp.int32, (2 * Z, Z), 0), Z)
    col = lax.broadcasted_iota(jnp.int32, (2 * Z, Z), 1)
    tri[0] = (row <= col).astype(f32).astype(jnp.bfloat16)
    tri[1] = (row >= col).astype(f32).astype(jnp.bfloat16)

    def exchange(src, dst, slot, pitch, rows, k, axis):
        here = j if axis == "gy" else i
        return pltpu.make_async_remote_copy(
            src_ref=src.at[pl.ds(pl.multiple_of(k * pitch, 8), rows), :],
            dst_ref=dst.at[pl.ds(pl.multiple_of(here * pitch, 8), rows), :],
            send_sem=sent.at[slot],
            recv_sem=came.at[slot],
            device_id={axis: k},
            device_id_type=MESH,
        )

    def whole_round(src, dst, slot, pitch, rows, axis):
        total = pl.ds(0, rows * ((NJ if axis == "gy" else NI) - 1))
        return pltpu.make_async_remote_copy(
            src_ref=src.at[total, :],
            dst_ref=dst.at[total, :],
            send_sem=sent.at[slot],
            recv_sem=came.at[slot],
            device_id={axis: jnext if axis == "gy" else inext},
            device_id_type=MESH,
        )

    def peers(axis):
        if axis == "gy":
            return [lax.rem(j // 4 + a, 4) * 4 + lax.rem(j + b, 4) for a, b in FAR]
        return [lax.rem(i // 2 + a, 4) * 2 + lax.rem(i + b, 2) for a, b in FAR_X]

    def send_all(src, dst, slot, pitch, rows, axis):
        here = j if axis == "gy" else i
        mine = pl.ds(pl.multiple_of(here * pitch, 8), rows)
        for k in peers(axis):
            exchange(src, dst, slot, pitch, rows, k, axis).start()
        dst[mine, :] = src[mine, :]

    def recv_all(src, dst, slot, pitch, rows, axis):
        whole_round(src, dst, slot, pitch, rows, axis).wait_recv()

    def sent_all(src, dst, slot, pitch, rows, axis):
        whole_round(src, dst, slot, pitch, rows, axis).wait_send()

    coup_y = (csy, rcy, 0, 8, 8, "gy")
    coup_x = (csx, rcx, 1, 16, 16, "gx")
    tot_y = (sty, tty, 2, PACK, PACK, "gy")
    ret_y = (oty, rty, 3, PACK, PACK, "gy")
    tot_x = (stx, ttx, 4, STEP_X, PACK_X, "gx")
    ret_x = (otx, rtx, 5, STEP_X, PACK_X, "gx")

    def face(src, dst, slot, part, axis, to):
        return pltpu.make_async_remote_copy(
            src_ref=src.at[part], dst_ref=dst.at[part], send_sem=sent.at[slot], recv_sem=came.at[slot],
            device_id={axis: to}, device_id_type=MESH,
        )

    def both(src, dst, slot):
        return pltpu.make_async_remote_copy(
            src_ref=src, dst_ref=dst, send_sem=sent.at[slot], recv_sem=came.at[slot],
            device_id={"gy": jnext}, device_id_type=MESH,
        )

    edges = [
        face(fse, fre, 6, 0, "gy", jprev),
        face(fse, fre, 6, 1, "gy", jnext),
    ]
    faces = [
        face(fsy, fry, 7, 0, "gy", jprev),
        face(fsy, fry, 7, 1, "gy", jnext),
        face(fsx, frx, 8, 0, "gx", iprev),
        face(fsx, frx, 8, 1, "gx", inext),
    ]
    pairs = [both(fse, fre, 6), both(fsy, fry, 7), both(fsx, frx, 8)]
    def z_lower(q):
        rows = quarters[q]
        scale, weight = zt[rows, :], zw[rows, :]
        for c in range(C):
            zb[c, rows, :] = weight * jnp.dot(
                split(cot[c, rows, :] * scale), tri[0], preferred_element_type=f32
            )

    def z_upper(q):
        rows = quarters[q]
        finish = zo[rows, :]
        for c in range(C):
            zb[c, rows, :] = finish * jnp.dot(split(zb[c, rows, :]), tri[1], preferred_element_type=f32)

    def y_totals(q):
        xs = pl.ds(q * 8, 8)
        heads = [jnp.zeros((8, Z), f32) for _ in range(C)]
        tails = [jnp.zeros((8, Z), f32) for _ in range(C)]
        for y in range(Y):
            a, b = ya[y, xs, :], yb[y, xs, :]
            for c in range(C):
                value = zb[c, pl.ds(q * 8 * Y + y, 8, stride=Y), :]
                heads[c] = heads[c] + a * value
                tails[c] = tails[c] + b * value
                yf[c, y, xs, :] = tails[c]
        at = (q % 2) * 8 * PACK + (q // 2) * C
        for c in range(C):
            sty[pl.ds(at + c, 8, stride=PACK), :] = heads[c]
            sty[pl.ds(at + HALF + c, 8, stride=PACK), :] = tails[c]

    for q in ORDER:
        fields[q].wait()
    loads[2].start()
    loads[3].start()
    z_lower(0)
    for q in range(4):
        if q < 3:
            z_lower(q + 1)
        z_upper(q)
        y_totals(q)

    pl.semaphore_wait(barrier, NI + NJ - 2)
    send_all(*tot_y)
    send_all(*coup_y)
    fse[0] = ec[pl.ds(0, X, stride=Y), :]
    fse[1] = ec[pl.ds(Y - 1, X, stride=Y), :]
    for e in edges:
        e.start()

    loads[2].wait()
    loads[3].wait()
    fsy[0] = upw[1, pl.ds(0, X, stride=Y), :].astype(f32) * cou[1, pl.ds(0, X, stride=Y), :]
    fsy[1] = (1.0 - upw[1, pl.ds(Y - 1, X, stride=Y), :].astype(f32)) * cou[1, pl.ds(Y - 1, X, stride=Y), :]
    fsx[0] = upw[0, 0:Y, :].astype(f32) * cou[0, 0:Y, :] * ec[0:Y, :]
    fsx[1] = (1.0 - upw[0, LINES - Y : LINES, :].astype(f32)) * cou[0, LINES - Y : LINES, :] * ec[LINES - Y : LINES, :]

    for f in faces:
        f.start()

    def reduce_factor(count, pitch, lines, half, couplings, factors):
        def spread(base, t):
            at = base + len(lines) * t
            return jnp.concatenate(
                [jnp.broadcast_to(couplings[pl.ds(at + n, 1), :], (wide, Z)) for n, wide in enumerate(lines)],
                axis=0,
            )

        edge = jnp.zeros((half, Z), f32)
        for m in range(count):
            a1, b1, bn = spread(m * pitch, 0), spread(m * pitch, 1), spread(m * pitch, 2)
            alpha = 1.0 / (1.0 - a1 * edge)
            alpha_a = a1 * alpha
            forward = b1 * alpha
            back = b1 * edge
            factors[0, m, 0:half, :] = alpha
            factors[1, m, 0:half, :] = alpha_a
            factors[2, m, 0:half, :] = forward
            factors[3, m, 0:half, :] = edge
            factors[4, m, 0:half, :] = back * alpha
            factors[5, m, 0:half, :] = b1 + back * alpha_a
            edge = bn + back * forward

    def reduce_solve(count, pitch, half, totals, factors, results):
        gain = jnp.zeros((half, Z), f32)
        for m in range(count):
            head = totals[m * pitch : m * pitch + half, :]
            tail = totals[m * pitch + half : m * pitch + 2 * half, :]
            gl[0, m, 0:half, :] = gain
            gl[1, m, 0:half, :] = factors[0, m, 0:half, :] * head + factors[1, m, 0:half, :] * gain
            gain = tail + factors[4, m, 0:half, :] * head + factors[5, m, 0:half, :] * gain
        later = jnp.zeros((half, Z), f32)
        for m in range(count - 1, -1, -1):
            results[m * pitch + half : m * pitch + 2 * half, :] = later
            later = gl[1, m, 0:half, :] + factors[2, m, 0:half, :] * later
            results[m * pitch : m * pitch + half, :] = gl[0, m, 0:half, :] + factors[3, m, 0:half, :] * later

    low_ok = jnp.where(j > 0, 1.0, 0.0).astype(f32)
    high_ok = jnp.where(j < NJ - 1, 1.0, 0.0).astype(f32)
    lane16 = lax.broadcasted_iota(jnp.int32, (Y, Z), 1)

    def coefficients(x, _):
        rows = pl.ds(pl.multiple_of(x * Y, Y), Y)
        shifted = pl.ds(pl.multiple_of(x * Y + Y, Y), Y)
        padded = pl.ds(pl.multiple_of(x * PAD + 8, 8), Y)
        flux = [cou[d, rows, :] for d in range(3)]
        ahead = [upw[d, rows, :].astype(f32) * flux[d] for d in range(3)]
        behind = [flux[d] - ahead[d] for d in range(3)]
        c0[rows, :] = 1.0 + (behind[0] - ahead[0]) + (behind[1] - ahead[1]) + (behind[2] - ahead[2])
        ax[shifted, :] = ahead[0]
        bx[shifted, :] = behind[0]
        ayp[padded, :] = ahead[1]
        byp[padded, :] = behind[1]
        azn[rows, :] = jnp.where(lane16 < Z - 1, pltpu.roll(ahead[2], Z - 1, 1), 0.0)
        bzp[rows, :] = jnp.where(lane16 > 0, pltpu.roll(behind[2], 1, 1), 0.0)
        return 0

    lax.fori_loop(0, X, coefficients, 0, unroll=8)
    ayh[...] = jnp.zeros_like(ayh)

    for q in range(4):
        xs = pl.ds(q * 8, 8)
        live = [jnp.zeros((8, Z), f32) for _ in range(C)]
        summed = jnp.zeros((8, Z), f32)
        for y in range(Y - 1, -1, -1):
            cells = pl.ds(q * 8 * Y + y, 8, stride=Y)
            weight, finish = yw[y, xs, :], yo[y, xs, :]
            summed = summed + weight
            ynl[cells, :] = finish * (summed * yr[xs, :])
            ynr[cells, :] = finish
            for c in range(C):
                live[c] = live[c] + weight * yf[c, y, xs, :]
                ay[c, cells, :] = live[c] * finish

    recv_all(*coup_y)
    reduce_factor(NJ, 8, (C, C), HALF, rcy, ky)

    recv_all(*tot_y)
    reduce_solve(NJ, PACK, HALF, tty, ky, oty)
    send_all(*ret_y)

    def x_factor():
        rows = pl.ds(0, 32)
        one = jnp.ones((32, Z), f32)

        def up(x, carry):
            theta, delta = carry
            xb[x, rows, :] = theta
            delta = delta + xe[x, rows, :] * theta
            return theta + delta, delta

        theta, _ = lax.fori_loop(0, X, up, (one, one), unroll=8)
        rn = 1.0 / theta
        xr[rows, :] = rn

        def down(step, carry):
            x = X - 1 - step
            phi, delta, after, _ = carry
            cell = xe[x, rows, :]
            a = phi * rn
            b = xb[x, rows, :] * rn
            xa[x, rows, :] = a
            xb[x, rows, :] = b
            xw[x, rows, :] = 1.0 / (b * after)
            xo[x, rows, :] = b * cell
            delta = delta + cell * phi
            return phi + delta, delta, b, a

        _, _, _, first = lax.fori_loop(0, X, down, (one, one, one, one), unroll=8)
        return first, rn

    pairs[0].wait_recv()
    for x in range(X):
        xe[x, 0:Y, :] = ec[x * Y : (x + 1) * Y, :]
        xe[x, 16:24, :] = jnp.broadcast_to(fre[1, x : x + 1, :], (8, Z))
        xe[x, 24:32, :] = jnp.broadcast_to(fre[0, x : x + 1, :], (8, Z))
    first, rn = x_factor()
    for t, part in enumerate((first, rn, xb[X - 1])):
        for r in range(2):
            csx[pl.ds(4 * t + r, 8, stride=16), :] = part[r * 8 : r * 8 + 8]
        csx[pl.ds(4 * t + 2, C, stride=16), :] = part[16 : 16 + C]
        csx[pl.ds(C * 16 + 4 * t + 2, 8 - C, stride=16), :] = part[24 : 32 - C]
        csx[pl.ds(4 * t + 3, 8, stride=16), :] = part[24:32]

    send_all(*coup_x)

    def x_totals(x, carry):
        heads, tails = carry
        rows = pl.ds(pl.multiple_of(x * Y, Y), Y)
        a, b = xa[x, 0:Y, :], xb[x, 0:Y, :]
        left, right = ynl[rows, :], ynr[rows, :]
        ends[0, rows, :] = a * left
        ends[1, rows, :] = a * right
        ends[2, rows, :] = b * left
        ends[3, rows, :] = b * right
        values = [ay[c, rows, :] for c in range(C)]
        return (
            tuple(heads[c] + a * values[c] for c in range(C)),
            tuple(tails[c] + b * values[c] for c in range(C)),
        )

    none = jnp.zeros((Y, Z), f32)
    heads, tails = lax.fori_loop(0, X, x_totals, ((none,) * C, (none,) * C), unroll=8)
    heads, tails = list(heads), list(tails)

    recv_all(*ret_y)

    def end_values(x, c):
        at = lax.rem(x, NJ) * PACK + (x // NJ) * C + c
        return (
            jnp.broadcast_to(rty[pl.ds(at, 1), :], (Y, Z)),
            jnp.broadcast_to(rty[pl.ds(at + HALF, 1), :], (Y, Z)),
        )

    for q in range(4):
        xs = pl.ds(q * 8, 8)
        at = (q % 2) * 8 * PACK + (q // 2) * C
        for c in range(C):
            left = rty[pl.ds(at + c, 8, stride=PACK), :]
            right = rty[pl.ds(at + HALF + c, 8, stride=PACK), :]
            ayh[pl.ds(q * 8 * 16 + c, 8, stride=16), :] = left * fre[1, xs, :]
            ayh[pl.ds(q * 8 * 16 + 8 + c, 8, stride=16), :] = right * fre[0, xs, :]

    def end_totals(x, carry):
        heads, tails, halo_head, halo_tail = carry
        rows = pl.ds(pl.multiple_of(x * Y, Y), Y)
        hl, hr, tl, tr = (ends[n, rows, :] for n in range(4))
        pairs_of = [end_values(x, c) for c in range(C)]
        value = ayh[rows, :]
        return (
            tuple(heads[c] + (hl * left + hr * right) for c, (left, right) in enumerate(pairs_of)),
            tuple(tails[c] + (tl * left + tr * right) for c, (left, right) in enumerate(pairs_of)),
            halo_head + xa[x, 16:32, :] * value,
            halo_tail + xb[x, 16:32, :] * value,
        )

    heads, tails, *edge_pair = lax.fori_loop(
        0, X, end_totals, (tuple(heads), tuple(tails), none, none), unroll=8
    )
    for c in range(C):
        for r in range(2):
            stx[pl.ds(r * C + c, 8, stride=STEP_X), :] = heads[c][r * 8 : r * 8 + 8]
            stx[pl.ds(HALF_X + r * C + c, 8, stride=STEP_X), :] = tails[c][r * 8 : r * 8 + 8]
    for end, part in enumerate(edge_pair):
        at = end * HALF_X + HALF
        stx[pl.ds(at, C, stride=STEP_X), :] = part[0:C]
        stx[pl.ds(C * STEP_X + at, 8 - C, stride=STEP_X), :] = part[8 : 16 - C]
        stx[pl.ds(at + 1, 2 * C - 8, stride=STEP_X), :] = part[16 - C : 8 + C]
    send_all(*tot_x)

    def x_prefix(x, carry):
        tails, halo = carry
        rows = pl.ds(pl.multiple_of(x * Y, Y), Y)
        b = xb[x, 0:Y, :]
        by_left, by_right = ynl[rows, :], ynr[rows, :]
        out = []
        for c in range(C):
            left, right = end_values(x, c)
            tail = tails[c] + b * (ay[c, rows, :] + by_left * left + by_right * right)
            ay[c, rows, :] = tail
            out.append(tail)
        halo = halo + xb[x, 16:32, :] * ayh[rows, :]
        ayh[rows, :] = halo
        return tuple(out), halo

    lax.fori_loop(0, X, x_prefix, ((none,) * C, none), unroll=8)
    recv_all(*coup_x)
    reduce_factor(NI, 16, (C, C, 1, 1), HALF_X, rcx, kx)
    sent_all(*coup_y)
    sent_all(*coup_x)
    sent_all(*tot_y)
    sent_all(*ret_y)
    for pair in pairs:
        pair.wait_send()
    recv_all(*tot_x)
    reduce_solve(NI, STEP_X, HALF_X, ttx, kx, otx)
    send_all(*ret_x)
    pairs[1].wait_recv()
    pairs[2].wait_recv()
    bx[0:Y, :] = frx[1]
    ax[(X + 1) * Y : (X + 2) * Y, :] = frx[0]
    byp[pl.ds(7, X, stride=PAD), :] = fry[1] * low_ok
    ayp[pl.ds(PAD, X, stride=PAD), :] = fry[0] * high_ok

    def x_local(step, carry):
        x = X - 1 - step
        live, halo, summed = carry
        rows = pl.ds(pl.multiple_of(x * Y, Y), Y)
        weight, finish = xw[x], xo[x]
        summed = summed + weight
        xl[x] = finish * (summed * xr[...])
        out = []
        for c in range(C):
            value = live[c] + weight[0:Y] * ay[c, rows, :]
            ay[c, rows, :] = value * finish[0:Y]
            out.append(value)
        halo = halo + weight[16:32] * ayh[rows, :]
        ayh[rows, :] = halo * finish[16:32]
        return tuple(out), halo, summed

    lax.fori_loop(0, X, x_local, ((none,) * C, none, jnp.zeros((32, Z), f32)), unroll=4)
    sent_all(*tot_x)
    recv_all(*ret_x)

    for end in range(2):
        for c in range(C):
            for r in range(2):
                lr[end, c, r * 8 : r * 8 + 8, :] = rtx[pl.ds(end * HALF_X + r * C + c, 8, stride=STEP_X), :]
        at = end * HALF_X + HALF
        lrh[end] = jnp.zeros((16, Z), f32)
        lrh[end, 0:C, :] = rtx[pl.ds(at, C, stride=STEP_X), :]
        lrh[end, 8 : 16 - C, :] = rtx[pl.ds(C * STEP_X + at, 8 - C, stride=STEP_X), :]
        lrh[end, 16 - C : 8 + C, :] = rtx[pl.ds(at + 1, 2 * C - 8, stride=STEP_X), :]
    sent_all(*ret_x)


def advection(ay, ayh, xl, xo, lr, lrh, c0, ax, bx, ayp, byp, azn, bzp, out_h, fb, out, sem):
    for c in range(C):
        fb[pl.ds(c * PITCH + 8, Y), :] = lr[0, c]
        fb[pl.ds(c * PITCH + (X + 1) * PAD + 8, Y), :] = lr[1, c]

    def fill(x, _):
        rows = pl.ds(pl.multiple_of(x * Y, Y), Y)
        left, right = xl[x], xo[x]
        for c in range(C):
            fb[pl.ds(pl.multiple_of(c * PITCH + (x + 1) * PAD + 8, 8), Y), :] = (
                ay[c, rows, :] + left[0:Y] * lr[0, c] + right[0:Y] * lr[1, c]
            )
        edge = ayh[rows, :] + left[16:32] * lrh[0] + right[16:32] * lrh[1]
        fb[pl.ds((x + 1) * PAD + 7, 8, stride=PITCH), :] = edge[0:8]
        fb[pl.ds((x + 2) * PAD, 8, stride=PITCH), :] = edge[8:16]
        return 0

    def advect(x, _):
        rows = pl.ds(pl.multiple_of(x * Y, Y), Y)
        middle = c0[rows, :]
        from_x, to_x = bx[rows, :], ax[pl.ds(pl.multiple_of((x + 2) * Y, Y), Y), :]
        from_y, to_y = byp[pl.ds(x * PAD + 7, Y), :], ayp[pl.ds(x * PAD + 9, Y), :]
        from_z, to_z = bzp[rows, :], azn[rows, :]
        for c in range(C):
            at = c * PITCH + (x + 1) * PAD + 8
            value = fb[pl.ds(pl.multiple_of(at, 8), Y), :]
            result = middle * value
            result += to_x * fb[pl.ds(pl.multiple_of(at + PAD, 8), Y), :]
            result -= from_x * fb[pl.ds(pl.multiple_of(at - PAD, 8), Y), :]
            result += to_y * fb[pl.ds(at + 1, Y), :]
            result -= from_y * fb[pl.ds(at - 1, Y), :]
            result += to_z * pltpu.roll(value, Z - 1, 1)
            result -= from_z * pltpu.roll(value, 1, 1)
            out[c, rows, :] = result
        return 0

    stores = []
    for part in range(4):
        lax.fori_loop(part * 8 + min(part, 1), min(part * 8 + 9, X), fill, 0, unroll=True)
        lax.fori_loop(part * 8, part * 8 + 8, advect, 0, unroll=8)
        rows = pl.ds(part * 8 * Y, 8 * Y)
        store = pltpu.make_async_copy(out.at[:, rows, :], out_h.at[:, rows, :], sem.at[part])
        store.start()
        stores.append(store)
    for store in stores:
        store.wait()


def on_device(cotangent, diffusion, phase, courant, upwind):
    def vm(*shape, dtype=f32):
        return pltpu.VMEM(shape, dtype)

    dma = pltpu.SemaphoreType.DMA
    scratch = [
        vm(C, LINES, Z), vm(LINES, Z), vm(LINES, Z, dtype=jnp.int32), vm(3, LINES, Z), vm(3, LINES, Z, dtype=jnp.int32),
        vm(LINES, Z),
        vm(LINES // Z, Z, Z), vm(LINES, Z), vm(LINES, Z), vm(LINES, Z), vm(C, LINES, Z), vm(2, 2 * Z, Z, dtype=jnp.bfloat16),
        vm(Y, X, Z), vm(Y, X, Z), vm(Y, X, Z), vm(Y, X, Z), vm(X, Z), vm(C, Y, X, Z), vm(LINES, Z), vm(LINES, Z), vm(4, LINES, Z),
        vm(X, 32, Z), vm(X, 32, Z), vm(X, 32, Z), vm(X, 32, Z), vm(32, Z),
        vm(NJ * 8, Z), vm(NI * 16, Z), vm(NJ * 8, Z), vm(NI * 16, Z), vm(6, NJ, 16, Z), vm(6, NI, 16, Z), vm(2, NJ, 16, Z),
        vm(NJ * PACK, Z), vm(NJ * PACK, Z), vm(NJ * PACK, Z), vm(NJ * PACK, Z),
        vm(NI * STEP_X, Z), vm(NI * STEP_X, Z), vm(NI * STEP_X, Z), vm(NI * STEP_X, Z),
        vm(2, X, Z), vm(2, X, Z), vm(2, X, Z), vm(2, X, Z), vm(2, Y, Z), vm(2, Y, Z),
        dma((8,)), dma((9,)), dma((9,)),
    ]
    vmem = pl.BlockSpec(memory_space=pltpu.VMEM)
    shapes = [(C, LINES, Z), (X * 16, Z), (X, 32, Z), (X, 32, Z), (2, C, Y, Z), (2, 16, Z)]
    shapes += [(LINES, Z), (LINES + 2 * Y, Z), (LINES + 2 * Y, Z), (X * PAD + 8, Z), (X * PAD + 8, Z), (LINES, Z), (LINES, Z)]
    parts = pl.pallas_call(
        body,
        out_shape=[pltpu.VMEM(shape, f32) for shape in shapes],
        in_specs=[pl.BlockSpec(memory_space=pltpu.HBM)] * 5,
        out_specs=[vmem] * len(shapes),
        scratch_shapes=scratch,
        compiler_params=pltpu.CompilerParams(
            collective_id=0, has_side_effects=True, vmem_limit_bytes=40 * 1024 * 1024
        ),
    )(
        *(
            pltpu.with_memory_space_constraint(given, pltpu.HBM)
            for given in (
                cotangent.reshape(C, LINES, Z),
                diffusion.reshape(LINES, Z),
                phase.reshape(LINES, Z),
                courant.reshape(3, LINES, Z),
                upwind.reshape(3, LINES, Z),
            )
        )
    )
    out = pl.pallas_call(
        advection,
        out_shape=jax.ShapeDtypeStruct((C, LINES, Z), f32),
        in_specs=[vmem] * len(shapes),
        out_specs=pl.BlockSpec(memory_space=pl.ANY),
        scratch_shapes=[vm(8 * PITCH, Z), vm(C, LINES, Z), dma((4,))],
        compiler_params=pltpu.CompilerParams(vmem_limit_bytes=12 * 1024 * 1024),
    )(*(pltpu.with_memory_space_constraint(part, pltpu.VMEM) for part in parts))
    return out.reshape(C, X, Y, Z)


def solution(mesh):
    placed = (
        P(None, "gx", "gy", None),
        P("gx", "gy", None),
        P("gx", "gy", None),
        P(None, "gx", "gy", None),
        P(None, "gx", "gy", None),
    )
    return jax.shard_map(
        on_device, mesh=mesh, in_specs=placed, out_specs=P(None, "gx", "gy", None), check_vma=False
    )
```

```python
import functools

import jax
import jax.numpy as jnp
from jax import lax
from jax.experimental import pallas as pl
from jax.experimental.pallas import tpu as pltpu
from jax.sharding import PartitionSpec as P

MESH = pl.DeviceIdType.MESH
C, X, Y, Z = 6, 32, 16, 128
NI, NJ = 8, 16
LINES = X * Y
PAD = 24
PLANES = X + 2
PITCH = PLANES * PAD + 8
HALF = C * 2
PACK = 2 * HALF
HALF_X = HALF + 2
PACK_X = 2 * HALF_X
STEP_X = 32
f32 = jnp.float32
FAR = sorted(((a, b) for a in range(4) for b in range(4) if a or b), key=lambda d: -min(d[0], 4 - d[0]) - min(d[1], 4 - d[1]))
FAR_X = [(2, 1), (2, 0), (3, 1), (1, 1), (3, 0), (1, 0), (0, 1)]


def split(values):
    high = values.astype(jnp.bfloat16)
    low = (values - high.astype(f32)).astype(jnp.bfloat16)
    return jnp.concatenate([high, low], axis=1)


def body(
    cot_h, dif_h, pha_h, cou_h, upw_h,
    fb, c0, ax, bx, ayp, byp, azn, bzp,
    cot, dif, pha, cou, upw, ec,
    et, zt, zw, zo, zb, tri,
    yb, ya, yw, yo, yr, yf, ay, ayh, ynl, ynr, ends,
    xe, xb, xa, xw, xo, xr,
    csy, csx, rcy, rcx, ky, kx, gl,
    sty, tty, oty, rty, stx, ttx, otx, rtx, ext,
    fse, fre, fsy, fry, fsx, frx,
    in_sem,
    sent, came,
):
    i = lax.axis_index("gx")
    j = lax.axis_index("gy")
    inext, iprev = lax.rem(i + 1, NI), lax.rem(i + NI - 1, NI)
    jnext, jprev = lax.rem(j + 1, NJ), lax.rem(j + NJ - 1, NJ)

    loads = [
        pltpu.make_async_copy(dif_h, dif, in_sem.at[0]),
        pltpu.make_async_copy(pha_h, pha, in_sem.at[1]),
        pltpu.make_async_copy(cou_h, cou, in_sem.at[2]),
        pltpu.make_async_copy(upw_h, upw, in_sem.at[3]),
    ]
    quarters = [pl.ds(q * 8 * Y, 8 * Y) for q in range(4)]
    field = pltpu.make_async_copy(cot_h, cot, in_sem.at[4])
    loads[0].start()
    loads[1].start()
    field.start()

    barrier = pltpu.get_barrier_semaphore()

    for a, b in FAR:
        to = lax.rem(j // 4 + a, 4) * 4 + lax.rem(j + b, 4)
        pl.semaphore_signal(barrier, inc=1, device_id={"gy": to}, device_id_type=MESH)
    for a, b in FAR_X:
        to = lax.rem(i // 2 + a, 4) * 2 + lax.rem(i + b, 2)
        pl.semaphore_signal(barrier, inc=1, device_id={"gx": to}, device_id_type=MESH)

    loads[0].wait()
    loads[1].wait()
    ec[...] = 1.0 / (dif[...] * (1.0 + 3.0 * pha[...].astype(f32)))

    for q in range(X // 8):
        xs = pl.ds(q * 8, 8)
        cells = [ec[pl.ds(q * 8 * Y + y, 8, stride=Y), :] for y in range(Y)]
        theta = jnp.ones((8, Z), f32)
        delta = jnp.ones((8, Z), f32)
        for y in range(Y):
            yb[y, xs, :] = theta
            delta = delta + cells[y] * theta
            theta = theta + delta
        rn = 1.0 / theta
        yr[xs, :] = rn
        phi = jnp.ones((8, Z), f32)
        delta = jnp.ones((8, Z), f32)
        after = jnp.ones((8, Z), f32)
        at = (q % 2) * 8 * 8 + q // 2
        for y in range(Y - 1, -1, -1):
            a = phi * rn
            b = yb[y, xs, :] * rn
            ya[y, xs, :] = a
            yb[y, xs, :] = b
            yw[y, xs, :] = 1.0 / (b * after)
            yo[y, xs, :] = b * cells[y]
            if y == Y - 1:
                csy[pl.ds(at + 4, 8, stride=8), :] = b
            if y == 0:
                csy[pl.ds(at, 8, stride=8), :] = a
            after = b
            delta = delta + cells[y] * phi
            phi = phi + delta
        csy[pl.ds(at + 2, 8, stride=8), :] = rn

    seg = lax.broadcasted_iota(jnp.int32, (8, Z), 0)
    span = Z // 8
    tiles = LINES // Z
    for t in range(tiles):
        et[t] = ec[t * Z : (t + 1) * Z, :].T
    ones = jnp.ones((8, Z), f32)
    zeros = jnp.zeros((8, Z), f32)

    def cell(t, step):
        return et[t, pl.ds(step, 8, stride=span), :]

    starts = []
    for t in range(tiles):
        p11, p12, p21, p22 = ones, zeros, zeros, ones
        for step in range(span):
            e = cell(t, step)
            p21 = p21 + e * p11
            p22 = p22 + e * p12
            p11 = p11 + p21
            p12 = p12 + p22
        for shift in (1, 2, 4):
            keep = seg < shift
            q11 = jnp.where(keep, 1.0, pltpu.roll(p11, shift, 0))
            q12 = jnp.where(keep, 0.0, pltpu.roll(p12, shift, 0))
            q21 = jnp.where(keep, 0.0, pltpu.roll(p21, shift, 0))
            q22 = jnp.where(keep, 1.0, pltpu.roll(p22, shift, 0))
            p11, p12, p21, p22 = (
                p11 * q11 + p12 * q21,
                p11 * q12 + p12 * q22,
                p21 * q11 + p22 * q21,
                p21 * q12 + p22 * q22,
            )
        theta = jnp.where(seg < 1, 1.0, pltpu.roll(p11 + p12, 1, 0))
        delta = jnp.where(seg < 1, 1.0, pltpu.roll(p21 + p22, 1, 0))
        starts.append((theta, delta))
    for t in range(tiles):
        theta, delta = starts[t]
        for step in range(span):
            delta = delta + cell(t, step) * theta
            theta = theta + delta
            et[t, pl.ds(step, 8, stride=span), :] = theta
    lane = lax.broadcasted_iota(jnp.int32, (Z, Z), 1)
    for t in range(tiles):
        rows = pl.ds(t * Z, Z)
        theta = et[t].T
        before = jnp.where(lane < 1, 1.0, pltpu.roll(theta, 1, 1))
        zt[rows, :] = before
        zw[rows, :] = 1.0 / (theta * before)
        zo[rows, :] = before * ec[rows, :]

    row = lax.rem(lax.broadcasted_iota(jnp.int32, (2 * Z, Z), 0), Z)
    col = lax.broadcasted_iota(jnp.int32, (2 * Z, Z), 1)
    tri[0] = (row <= col).astype(f32).astype(jnp.bfloat16)
    tri[1] = (row >= col).astype(f32).astype(jnp.bfloat16)

    def exchange(src, dst, slot, pitch, rows, k, axis):
        here = j if axis == "gy" else i
        return pltpu.make_async_remote_copy(
            src_ref=src.at[pl.ds(pl.multiple_of(k * pitch, 8), rows), :],
            dst_ref=dst.at[pl.ds(pl.multiple_of(here * pitch, 8), rows), :],
            send_sem=sent.at[slot],
            recv_sem=came.at[slot],
            device_id={axis: k},
            device_id_type=MESH,
        )

    def whole_round(src, dst, slot, pitch, rows, axis):
        total = pl.ds(0, rows * ((NJ if axis == "gy" else NI) - 1))
        return pltpu.make_async_remote_copy(
            src_ref=src.at[total, :],
            dst_ref=dst.at[total, :],
            send_sem=sent.at[slot],
            recv_sem=came.at[slot],
            device_id={axis: jnext if axis == "gy" else inext},
            device_id_type=MESH,
        )

    def peers(axis):
        if axis == "gy":
            return [lax.rem(j // 4 + a, 4) * 4 + lax.rem(j + b, 4) for a, b in FAR]
        return [lax.rem(i // 2 + a, 4) * 2 + lax.rem(i + b, 2) for a, b in FAR_X]

    def send_all(src, dst, slot, pitch, rows, axis):
        here = j if axis == "gy" else i
        mine = pl.ds(pl.multiple_of(here * pitch, 8), rows)
        for k in peers(axis):
            exchange(src, dst, slot, pitch, rows, k, axis).start()
        dst[mine, :] = src[mine, :]

    def recv_all(src, dst, slot, pitch, rows, axis):
        whole_round(src, dst, slot, pitch, rows, axis).wait_recv()

    def sent_all(src, dst, slot, pitch, rows, axis):
        whole_round(src, dst, slot, pitch, rows, axis).wait_send()

    coup_y = (csy, rcy, 0, 8, 8, "gy")
    coup_x = (csx, rcx, 1, 16, 16, "gx")
    tot_y = (sty, tty, 2, PACK, PACK, "gy")
    ret_y = (oty, rty, 3, PACK, PACK, "gy")
    tot_x = (stx, ttx, 4, STEP_X, PACK_X, "gx")
    ret_x = (otx, rtx, 5, STEP_X, PACK_X, "gx")

    def face(src, dst, slot, part, axis, to):
        return pltpu.make_async_remote_copy(
            src_ref=src.at[part], dst_ref=dst.at[part], send_sem=sent.at[slot], recv_sem=came.at[slot],
            device_id={axis: to}, device_id_type=MESH,
        )

    def both(src, dst, slot):
        return pltpu.make_async_remote_copy(
            src_ref=src, dst_ref=dst, send_sem=sent.at[slot], recv_sem=came.at[slot],
            device_id={"gy": jnext}, device_id_type=MESH,
        )

    edges = [
        face(fse, fre, 6, 0, "gy", jprev),
        face(fse, fre, 6, 1, "gy", jnext),
    ]
    faces = [
        face(fsy, fry, 7, 0, "gy", jprev),
        face(fsy, fry, 7, 1, "gy", jnext),
        face(fsx, frx, 8, 0, "gx", iprev),
        face(fsx, frx, 8, 1, "gx", inext),
    ]
    pairs = [both(fse, fre, 6), both(fsy, fry, 7), both(fsx, frx, 8)]
    def z_lower(q):
        rows = quarters[q]
        scale, weight = zt[rows, :], zw[rows, :]
        for c in range(C):
            zb[c, rows, :] = weight * jnp.dot(
                split(cot[c, rows, :] * scale), tri[0], preferred_element_type=f32
            )

    def z_upper(q):
        rows = quarters[q]
        finish = zo[rows, :]
        for c in range(C):
            zb[c, rows, :] = finish * jnp.dot(split(zb[c, rows, :]), tri[1], preferred_element_type=f32)

    def y_totals(q):
        xs = pl.ds(q * 8, 8)
        heads = [jnp.zeros((8, Z), f32) for _ in range(C)]
        tails = [jnp.zeros((8, Z), f32) for _ in range(C)]
        for y in range(Y):
            a, b = ya[y, xs, :], yb[y, xs, :]
            for c in range(C):
                value = zb[c, pl.ds(q * 8 * Y + y, 8, stride=Y), :]
                heads[c] = heads[c] + a * value
                tails[c] = tails[c] + b * value
                yf[c, y, xs, :] = tails[c]
        at = (q % 2) * 8 * PACK + (q // 2) * C
        for c in range(C):
            sty[pl.ds(at + c, 8, stride=PACK), :] = heads[c]
            sty[pl.ds(at + HALF + c, 8, stride=PACK), :] = tails[c]

    field.wait()
    loads[2].start()
    loads[3].start()
    z_lower(0)
    for q in range(4):
        if q < 3:
            z_lower(q + 1)
        z_upper(q)
        y_totals(q)

    pl.semaphore_wait(barrier, NI + NJ - 2)
    send_all(*tot_y)
    send_all(*coup_y)
    fse[0] = ec[pl.ds(0, X, stride=Y), :]
    fse[1] = ec[pl.ds(Y - 1, X, stride=Y), :]
    for e in edges:
        e.start()

    loads[2].wait()
    loads[3].wait()
    fsy[0] = upw[1, pl.ds(0, X, stride=Y), :].astype(f32) * cou[1, pl.ds(0, X, stride=Y), :]
    fsy[1] = (1.0 - upw[1, pl.ds(Y - 1, X, stride=Y), :].astype(f32)) * cou[1, pl.ds(Y - 1, X, stride=Y), :]
    fsx[0] = upw[0, 0:Y, :].astype(f32) * cou[0, 0:Y, :] * ec[0:Y, :]
    fsx[1] = (1.0 - upw[0, LINES - Y : LINES, :].astype(f32)) * cou[0, LINES - Y : LINES, :] * ec[LINES - Y : LINES, :]

    for f in faces:
        f.start()

    def reduce_factor(count, pitch, lines, half, couplings, factors):
        def spread(base, t):
            at = base + len(lines) * t
            return jnp.concatenate(
                [jnp.broadcast_to(couplings[pl.ds(at + n, 1), :], (wide, Z)) for n, wide in enumerate(lines)],
                axis=0,
            )

        edge = jnp.zeros((half, Z), f32)
        for m in range(count):
            a1, b1, bn = spread(m * pitch, 0), spread(m * pitch, 1), spread(m * pitch, 2)
            alpha = 1.0 / (1.0 - a1 * edge)
            alpha_a = a1 * alpha
            forward = b1 * alpha
            back = b1 * edge
            factors[0, m, 0:half, :] = alpha
            factors[1, m, 0:half, :] = alpha_a
            factors[2, m, 0:half, :] = forward
            factors[3, m, 0:half, :] = edge
            factors[4, m, 0:half, :] = back * alpha
            factors[5, m, 0:half, :] = b1 + back * alpha_a
            edge = bn + back * forward

    def reduce_solve(count, pitch, half, totals, factors, results):
        gain = jnp.zeros((half, Z), f32)
        for m in range(count):
            head = totals[m * pitch : m * pitch + half, :]
            tail = totals[m * pitch + half : m * pitch + 2 * half, :]
            gl[0, m, 0:half, :] = gain
            gl[1, m, 0:half, :] = factors[0, m, 0:half, :] * head + factors[1, m, 0:half, :] * gain
            gain = tail + factors[4, m, 0:half, :] * head + factors[5, m, 0:half, :] * gain
        later = jnp.zeros((half, Z), f32)
        for m in range(count - 1, -1, -1):
            results[m * pitch + half : m * pitch + 2 * half, :] = later
            later = gl[1, m, 0:half, :] + factors[2, m, 0:half, :] * later
            results[m * pitch : m * pitch + half, :] = gl[0, m, 0:half, :] + factors[3, m, 0:half, :] * later

    low_ok = jnp.where(j > 0, 1.0, 0.0).astype(f32)
    high_ok = jnp.where(j < NJ - 1, 1.0, 0.0).astype(f32)
    lane16 = lax.broadcasted_iota(jnp.int32, (Y, Z), 1)

    def coefficients(x, _):
        rows = pl.ds(pl.multiple_of(x * Y, Y), Y)
        shifted = pl.ds(pl.multiple_of(x * Y + Y, Y), Y)
        padded = pl.ds(pl.multiple_of(x * PAD + 8, 8), Y)
        flux = [cou[d, rows, :] for d in range(3)]
        ahead = [upw[d, rows, :].astype(f32) * flux[d] for d in range(3)]
        behind = [flux[d] - ahead[d] for d in range(3)]
        c0[rows, :] = 1.0 + (behind[0] - ahead[0]) + (behind[1] - ahead[1]) + (behind[2] - ahead[2])
        ax[shifted, :] = ahead[0]
        bx[shifted, :] = behind[0]
        ayp[padded, :] = ahead[1]
        byp[padded, :] = behind[1]
        azn[rows, :] = jnp.where(lane16 < Z - 1, pltpu.roll(ahead[2], Z - 1, 1), 0.0)
        bzp[rows, :] = jnp.where(lane16 > 0, pltpu.roll(behind[2], 1, 1), 0.0)
        return 0

    lax.fori_loop(0, X, coefficients, 0, unroll=8)
    ayh[...] = jnp.zeros_like(ayh)

    for q in range(4):
        xs = pl.ds(q * 8, 8)
        live = [jnp.zeros((8, Z), f32) for _ in range(C)]
        summed = jnp.zeros((8, Z), f32)
        for y in range(Y - 1, -1, -1):
            cells = pl.ds(q * 8 * Y + y, 8, stride=Y)
            weight, finish = yw[y, xs, :], yo[y, xs, :]
            summed = summed + weight
            ynl[cells, :] = finish * (summed * yr[xs, :])
            ynr[cells, :] = finish
            for c in range(C):
                live[c] = live[c] + weight * yf[c, y, xs, :]
                ay[c, cells, :] = live[c] * finish

    recv_all(*coup_y)
    reduce_factor(NJ, 8, (C, C), HALF, rcy, ky)

    recv_all(*tot_y)
    reduce_solve(NJ, PACK, HALF, tty, ky, oty)
    send_all(*ret_y)

    def x_factor():
        rows = pl.ds(0, 32)
        one = jnp.ones((32, Z), f32)

        def up(x, carry):
            theta, delta = carry
            xb[x, rows, :] = theta
            delta = delta + xe[x, rows, :] * theta
            return theta + delta, delta

        theta, _ = lax.fori_loop(0, X, up, (one, one), unroll=8)
        rn = 1.0 / theta
        xr[rows, :] = rn

        def down(step, carry):
            x = X - 1 - step
            phi, delta, after, _ = carry
            cell = xe[x, rows, :]
            a = phi * rn
            b = xb[x, rows, :] * rn
            xa[x, rows, :] = a
            xb[x, rows, :] = b
            xw[x, rows, :] = 1.0 / (b * after)
            xo[x, rows, :] = b * cell
            delta = delta + cell * phi
            return phi + delta, delta, b, a

        _, _, _, first = lax.fori_loop(0, X, down, (one, one, one, one), unroll=8)
        return first, rn

    pairs[0].wait_recv()
    for x in range(X):
        xe[x, 0:Y, :] = ec[x * Y : (x + 1) * Y, :]
        xe[x, 16:24, :] = jnp.broadcast_to(fre[1, x : x + 1, :], (8, Z))
        xe[x, 24:32, :] = jnp.broadcast_to(fre[0, x : x + 1, :], (8, Z))
    first, rn = x_factor()
    for t, part in enumerate((first, rn, xb[X - 1])):
        for r in range(2):
            csx[pl.ds(4 * t + r, 8, stride=16), :] = part[r * 8 : r * 8 + 8]
        csx[pl.ds(4 * t + 2, C, stride=16), :] = part[16 : 16 + C]
        csx[pl.ds(C * 16 + 4 * t + 2, 8 - C, stride=16), :] = part[24 : 32 - C]
        csx[pl.ds(4 * t + 3, 8, stride=16), :] = part[24:32]

    send_all(*coup_x)

    def x_totals(x, carry):
        heads, tails = carry
        rows = pl.ds(pl.multiple_of(x * Y, Y), Y)
        a, b = xa[x, 0:Y, :], xb[x, 0:Y, :]
        left, right = ynl[rows, :], ynr[rows, :]
        ends[0, rows, :] = a * left
        ends[1, rows, :] = a * right
        ends[2, rows, :] = b * left
        ends[3, rows, :] = b * right
        values = [ay[c, rows, :] for c in range(C)]
        return (
            tuple(heads[c] + a * values[c] for c in range(C)),
            tuple(tails[c] + b * values[c] for c in range(C)),
        )

    none = jnp.zeros((Y, Z), f32)
    heads, tails = lax.fori_loop(0, X, x_totals, ((none,) * C, (none,) * C), unroll=8)
    heads, tails = list(heads), list(tails)

    recv_all(*ret_y)

    def end_values(x, c):
        at = lax.rem(x, NJ) * PACK + (x // NJ) * C + c
        return (
            jnp.broadcast_to(rty[pl.ds(at, 1), :], (Y, Z)),
            jnp.broadcast_to(rty[pl.ds(at + HALF, 1), :], (Y, Z)),
        )

    for q in range(4):
        xs = pl.ds(q * 8, 8)
        at = (q % 2) * 8 * PACK + (q // 2) * C
        for c in range(C):
            left = rty[pl.ds(at + c, 8, stride=PACK), :]
            right = rty[pl.ds(at + HALF + c, 8, stride=PACK), :]
            ayh[pl.ds(q * 8 * 16 + c, 8, stride=16), :] = left * fre[1, xs, :]
            ayh[pl.ds(q * 8 * 16 + 8 + c, 8, stride=16), :] = right * fre[0, xs, :]

    def end_totals(x, carry):
        heads, tails, halo_head, halo_tail = carry
        rows = pl.ds(pl.multiple_of(x * Y, Y), Y)
        hl, hr, tl, tr = (ends[n, rows, :] for n in range(4))
        pairs_of = [end_values(x, c) for c in range(C)]
        value = ayh[rows, :]
        return (
            tuple(heads[c] + (hl * left + hr * right) for c, (left, right) in enumerate(pairs_of)),
            tuple(tails[c] + (tl * left + tr * right) for c, (left, right) in enumerate(pairs_of)),
            halo_head + xa[x, 16:32, :] * value,
            halo_tail + xb[x, 16:32, :] * value,
        )

    heads, tails, *edge_pair = lax.fori_loop(
        0, X, end_totals, (tuple(heads), tuple(tails), none, none), unroll=8
    )
    for c in range(C):
        for r in range(2):
            stx[pl.ds(r * C + c, 8, stride=STEP_X), :] = heads[c][r * 8 : r * 8 + 8]
            stx[pl.ds(HALF_X + r * C + c, 8, stride=STEP_X), :] = tails[c][r * 8 : r * 8 + 8]
    for end, part in enumerate(edge_pair):
        at = end * HALF_X + HALF
        stx[pl.ds(at, C, stride=STEP_X), :] = part[0:C]
        stx[pl.ds(C * STEP_X + at, 8 - C, stride=STEP_X), :] = part[8 : 16 - C]
        stx[pl.ds(at + 1, 2 * C - 8, stride=STEP_X), :] = part[16 - C : 8 + C]
    send_all(*tot_x)

    def x_prefix(x, carry):
        tails, halo = carry
        rows = pl.ds(pl.multiple_of(x * Y, Y), Y)
        b = xb[x, 0:Y, :]
        by_left, by_right = ynl[rows, :], ynr[rows, :]
        out = []
        for c in range(C):
            left, right = end_values(x, c)
            tail = tails[c] + b * (ay[c, rows, :] + by_left * left + by_right * right)
            ay[c, rows, :] = tail
            out.append(tail)
        halo = halo + xb[x, 16:32, :] * ayh[rows, :]
        ayh[rows, :] = halo
        return tuple(out), halo

    lax.fori_loop(0, X, x_prefix, ((none,) * C, none), unroll=8)
    recv_all(*coup_x)
    reduce_factor(NI, 16, (C, C, 1, 1), HALF_X, rcx, kx)
    sent_all(*coup_y)
    sent_all(*coup_x)
    sent_all(*tot_y)
    sent_all(*ret_y)
    for pair in pairs:
        pair.wait_send()
    recv_all(*tot_x)
    reduce_solve(NI, STEP_X, HALF_X, ttx, kx, otx)
    send_all(*ret_x)
    pairs[1].wait_recv()
    pairs[2].wait_recv()
    bx[0:Y, :] = frx[1]
    ax[(X + 1) * Y : (X + 2) * Y, :] = frx[0]
    byp[pl.ds(7, X, stride=PAD), :] = fry[1] * low_ok
    ayp[pl.ds(PAD, X, stride=PAD), :] = fry[0] * high_ok

    sent_all(*tot_x)
    recv_all(*ret_x)

    lefts, rights = [], []
    for c in range(C):
        left = jnp.concatenate([rtx[pl.ds(r * C + c, 8, stride=STEP_X), :] for r in range(2)], axis=0)
        right = jnp.concatenate([rtx[pl.ds(HALF_X + r * C + c, 8, stride=STEP_X), :] for r in range(2)], axis=0)
        fb[pl.ds(c * PITCH + 8, Y), :] = left
        fb[pl.ds(c * PITCH + (X + 1) * PAD + 8, Y), :] = right
        lefts.append(left * xr[0:Y, :])
        rights.append(right)
    for end in range(2):
        at = end * HALF_X + HALF
        ext[end, 0:C, :] = rtx[pl.ds(at, C, stride=STEP_X), :]
        ext[end, 8 : 16 - C, :] = rtx[pl.ds(C * STEP_X + at, 8 - C, stride=STEP_X), :]
        ext[end, 16 - C : 8 + C, :] = rtx[pl.ds(at + 1, 2 * C - 8, stride=STEP_X), :]
    left_halo = ext[0] * xr[16:32, :]
    right_halo = ext[1]

    def x_finish(step, carry):
        x = X - 1 - step
        live, halo = carry
        rows = pl.ds(pl.multiple_of(x * Y, Y), Y)
        weight, finish = xw[x, 0:Y, :], xo[x, 0:Y, :]
        out = []
        for c in range(C):
            value = live[c] + weight * (ay[c, rows, :] + lefts[c])
            fb[pl.ds(pl.multiple_of(c * PITCH + (x + 1) * PAD + 8, 8), Y), :] = value * finish
            out.append(value)
        halo = halo + xw[x, 16:32, :] * (ayh[rows, :] + left_halo)
        edge = halo * xo[x, 16:32, :]
        fb[pl.ds((x + 1) * PAD + 7, 8, stride=PITCH), :] = edge[0:8]
        fb[pl.ds((x + 2) * PAD, 8, stride=PITCH), :] = edge[8:16]
        return tuple(out), halo

    lax.fori_loop(0, X, x_finish, (tuple(rights), right_halo), unroll=4)

    sent_all(*ret_x)


def advection(fb, c0, ax, bx, ayp, byp, azn, bzp, out_h, out, sem):
    def advect(x, _):
        rows = pl.ds(pl.multiple_of(x * Y, Y), Y)
        middle = c0[rows, :]
        from_x, to_x = bx[rows, :], ax[pl.ds(pl.multiple_of((x + 2) * Y, Y), Y), :]
        from_y, to_y = byp[pl.ds(x * PAD + 7, Y), :], ayp[pl.ds(x * PAD + 9, Y), :]
        from_z, to_z = bzp[rows, :], azn[rows, :]
        for c in range(C):
            at = c * PITCH + (x + 1) * PAD + 8
            value = fb[pl.ds(pl.multiple_of(at, 8), Y), :]
            result = middle * value
            result += to_x * fb[pl.ds(pl.multiple_of(at + PAD, 8), Y), :]
            result -= from_x * fb[pl.ds(pl.multiple_of(at - PAD, 8), Y), :]
            result += to_y * fb[pl.ds(at + 1, Y), :]
            result -= from_y * fb[pl.ds(at - 1, Y), :]
            result += to_z * pltpu.roll(value, Z - 1, 1)
            result -= from_z * pltpu.roll(value, 1, 1)
            out[c, rows, :] = result
        return 0

    stores = []
    for part in range(4):
        lax.fori_loop(part * 8, part * 8 + 8, advect, 0, unroll=8)
        rows = pl.ds(part * 8 * Y, 8 * Y)
        store = pltpu.make_async_copy(out.at[:, rows, :], out_h.at[:, rows, :], sem.at[part])
        store.start()
        stores.append(store)
    for store in stores:
        store.wait()


def on_device(cotangent, diffusion, phase, courant, upwind):
    def vm(*shape, dtype=f32):
        return pltpu.VMEM(shape, dtype)

    dma = pltpu.SemaphoreType.DMA
    scratch = [
        vm(C, LINES, Z), vm(LINES, Z), vm(LINES, Z, dtype=jnp.int32), vm(3, LINES, Z), vm(3, LINES, Z, dtype=jnp.int32),
        vm(LINES, Z),
        vm(LINES // Z, Z, Z), vm(LINES, Z), vm(LINES, Z), vm(LINES, Z), vm(C, LINES, Z), vm(2, 2 * Z, Z, dtype=jnp.bfloat16),
        vm(Y, X, Z), vm(Y, X, Z), vm(Y, X, Z), vm(Y, X, Z), vm(X, Z), vm(C, Y, X, Z), vm(C, LINES, Z), vm(X * 16, Z), vm(LINES, Z), vm(LINES, Z), vm(4, LINES, Z),
        vm(X, 32, Z), vm(X, 32, Z), vm(X, 32, Z), vm(X, 32, Z), vm(X, 32, Z), vm(32, Z),
        vm(NJ * 8, Z), vm(NI * 16, Z), vm(NJ * 8, Z), vm(NI * 16, Z), vm(6, NJ, 16, Z), vm(6, NI, 16, Z), vm(2, NJ, 16, Z),
        vm(NJ * PACK, Z), vm(NJ * PACK, Z), vm(NJ * PACK, Z), vm(NJ * PACK, Z),
        vm(NI * STEP_X, Z), vm(NI * STEP_X, Z), vm(NI * STEP_X, Z), vm(NI * STEP_X, Z), vm(2, 16, Z),
        vm(2, X, Z), vm(2, X, Z), vm(2, X, Z), vm(2, X, Z), vm(2, Y, Z), vm(2, Y, Z),
        dma((5,)), dma((9,)), dma((9,)),
    ]
    vmem = pl.BlockSpec(memory_space=pltpu.VMEM)
    shapes = [(8 * PITCH, Z), (LINES, Z), (LINES + 2 * Y, Z), (LINES + 2 * Y, Z), (X * PAD + 8, Z), (X * PAD + 8, Z), (LINES, Z), (LINES, Z)]
    parts = pl.pallas_call(
        body,
        out_shape=[pltpu.VMEM(shape, f32) for shape in shapes],
        in_specs=[pl.BlockSpec(memory_space=pltpu.HBM)] * 5,
        out_specs=[vmem] * len(shapes),
        scratch_shapes=scratch,
        compiler_params=pltpu.CompilerParams(
            collective_id=0, has_side_effects=True, vmem_limit_bytes=40 * 1024 * 1024
        ),
    )(
        *(
            pltpu.with_memory_space_constraint(given, pltpu.HBM)
            for given in (
                cotangent.reshape(C, LINES, Z),
                diffusion.reshape(LINES, Z),
                phase.reshape(LINES, Z),
                courant.reshape(3, LINES, Z),
                upwind.reshape(3, LINES, Z),
            )
        )
    )
    out = pl.pallas_call(
        advection,
        out_shape=jax.ShapeDtypeStruct((C, LINES, Z), f32),
        in_specs=[vmem] * len(shapes),
        out_specs=pl.BlockSpec(memory_space=pl.ANY),
        scratch_shapes=[vm(C, LINES, Z), dma((4,))],
        compiler_params=pltpu.CompilerParams(vmem_limit_bytes=8 * 1024 * 1024),
    )(*(pltpu.with_memory_space_constraint(part, pltpu.VMEM) for part in parts))
    return out.reshape(C, X, Y, Z)


def solution(mesh):
    placed = (
        P(None, "gx", "gy", None),
        P("gx", "gy", None),
        P("gx", "gy", None),
        P(None, "gx", "gy", None),
        P(None, "gx", "gy", None),
    )
    return jax.shard_map(
        on_device, mesh=mesh, in_specs=placed, out_specs=P(None, "gx", "gy", None), check_vma=False
    )
```

```python
import functools

import jax
import jax.numpy as jnp
from jax import lax
from jax.experimental import pallas as pl
from jax.experimental.pallas import tpu as pltpu
from jax.sharding import PartitionSpec as P

MESH = pl.DeviceIdType.MESH
C, X, Y, Z = 6, 32, 16, 128
NI, NJ = 8, 16
LINES = X * Y
PAD = 24
PLANES = X + 2
PITCH = PLANES * PAD + 8
HALF = C * 2
PACK = 2 * HALF
HALF_X = HALF + 2
PACK_X = 2 * HALF_X
STEP_X = 32
f32 = jnp.float32
FAR = sorted(((a, b) for a in range(4) for b in range(4) if a or b), key=lambda d: -min(d[0], 4 - d[0]) - min(d[1], 4 - d[1]))
ORDER = (0, 2, 1, 3)
FAR_X = [(2, 1), (2, 0), (3, 1), (1, 1), (3, 0), (1, 0), (0, 1)]


def split(values):
    high = values.astype(jnp.bfloat16)
    low = (values - high.astype(f32)).astype(jnp.bfloat16)
    return jnp.concatenate([high, low], axis=1)


def body(
    cot_h, dif_h, pha_h, cou_h, upw_h,
    fb, c0, ax, bx, ayp, byp, azn, bzp,
    cot, dif, pha, cou, upw, ec,
    et, zt, zw, zo, zb, tri,
    yb, ya, yw, yo, yr, yf, ay, ayh, ynl, ynr, ends,
    xe, xb, xa, xw, xo, xr,
    csy, csx, rcy, rcx, ky, kx, gl,
    sty, tty, oty, rty, stx, ttx, otx, rtx, ext,
    fse, fre, fsy, fry, fsx, frx,
    in_sem,
    sent, came,
):
    i = lax.axis_index("gx")
    j = lax.axis_index("gy")
    inext, iprev = lax.rem(i + 1, NI), lax.rem(i + NI - 1, NI)
    jnext, jprev = lax.rem(j + 1, NJ), lax.rem(j + NJ - 1, NJ)

    loads = [
        pltpu.make_async_copy(dif_h, dif, in_sem.at[0]),
        pltpu.make_async_copy(pha_h, pha, in_sem.at[1]),
        pltpu.make_async_copy(cou_h, cou, in_sem.at[2]),
        pltpu.make_async_copy(upw_h, upw, in_sem.at[3]),
    ]
    quarters = [pl.ds(q * 8 * Y, 8 * Y) for q in range(4)]
    fields = [
        pltpu.make_async_copy(cot_h.at[:, rows, :], cot.at[:, rows, :], in_sem.at[4 + q])
        for q, rows in enumerate(quarters)
    ]
    loads[0].start()
    loads[1].start()
    for q in ORDER:
        fields[q].start()

    barrier = pltpu.get_barrier_semaphore()

    def greet_y(d, _):
        pl.semaphore_signal(barrier, inc=1, device_id=(i, lax.rem(j + d, NJ)), device_id_type=MESH)
        return 0

    def greet_x(d, _):
        pl.semaphore_signal(barrier, inc=1, device_id=(lax.rem(i + d, NI), j), device_id_type=MESH)
        return 0

    lax.fori_loop(1, NJ, greet_y, 0)
    lax.fori_loop(1, NI, greet_x, 0)

    loads[0].wait()
    loads[1].wait()
    ec[...] = 1.0 / (dif[...] * (1.0 + 3.0 * pha[...].astype(f32)))

    for q in range(X // 8):
        xs = pl.ds(q * 8, 8)
        cells = [ec[pl.ds(q * 8 * Y + y, 8, stride=Y), :] for y in range(Y)]
        theta = jnp.ones((8, Z), f32)
        delta = jnp.ones((8, Z), f32)
        for y in range(Y):
            yb[y, xs, :] = theta
            delta = delta + cells[y] * theta
            theta = theta + delta
        rn = 1.0 / theta
        yr[xs, :] = rn
        phi = jnp.ones((8, Z), f32)
        delta = jnp.ones((8, Z), f32)
        after = jnp.ones((8, Z), f32)
        at = (q % 2) * 8 * 8 + q // 2
        for y in range(Y - 1, -1, -1):
            a = phi * rn
            b = yb[y, xs, :] * rn
            ya[y, xs, :] = a
            yb[y, xs, :] = b
            yw[y, xs, :] = 1.0 / (b * after)
            yo[y, xs, :] = b * cells[y]
            if y == Y - 1:
                csy[pl.ds(at + 4, 8, stride=8), :] = b
            if y == 0:
                csy[pl.ds(at, 8, stride=8), :] = a
            after = b
            delta = delta + cells[y] * phi
            phi = phi + delta
        csy[pl.ds(at + 2, 8, stride=8), :] = rn

    seg = lax.broadcasted_iota(jnp.int32, (8, Z), 0)
    span = Z // 8
    tiles = LINES // Z
    for t in range(tiles):
        et[t] = ec[t * Z : (t + 1) * Z, :].T
    ones = jnp.ones((8, Z), f32)
    zeros = jnp.zeros((8, Z), f32)

    def cell(t, step):
        return et[t, pl.ds(step, 8, stride=span), :]

    starts = []
    for t in range(tiles):
        p11, p12, p21, p22 = ones, zeros, zeros, ones
        for step in range(span):
            e = cell(t, step)
            p21 = p21 + e * p11
            p22 = p22 + e * p12
            p11 = p11 + p21
            p12 = p12 + p22
        for shift in (1, 2, 4):
            keep = seg < shift
            q11 = jnp.where(keep, 1.0, pltpu.roll(p11, shift, 0))
            q12 = jnp.where(keep, 0.0, pltpu.roll(p12, shift, 0))
            q21 = jnp.where(keep, 0.0, pltpu.roll(p21, shift, 0))
            q22 = jnp.where(keep, 1.0, pltpu.roll(p22, shift, 0))
            p11, p12, p21, p22 = (
                p11 * q11 + p12 * q21,
                p11 * q12 + p12 * q22,
                p21 * q11 + p22 * q21,
                p21 * q12 + p22 * q22,
            )
        theta = jnp.where(seg < 1, 1.0, pltpu.roll(p11 + p12, 1, 0))
        delta = jnp.where(seg < 1, 1.0, pltpu.roll(p21 + p22, 1, 0))
        starts.append((theta, delta))
    for t in range(tiles):
        theta, delta = starts[t]
        for step in range(span):
            delta = delta + cell(t, step) * theta
            theta = theta + delta
            et[t, pl.ds(step, 8, stride=span), :] = theta
    lane = lax.broadcasted_iota(jnp.int32, (Z, Z), 1)
    for t in range(tiles):
        rows = pl.ds(t * Z, Z)
        theta = et[t].T
        before = jnp.where(lane < 1, 1.0, pltpu.roll(theta, 1, 1))
        zt[rows, :] = before
        zw[rows, :] = 1.0 / (theta * before)
        zo[rows, :] = before * ec[rows, :]

    row = lax.rem(lax.broadcasted_iota(jnp.int32, (2 * Z, Z), 0), Z)
    col = lax.broadcasted_iota(jnp.int32, (2 * Z, Z), 1)
    tri[0] = (row <= col).astype(f32).astype(jnp.bfloat16)
    tri[1] = (row >= col).astype(f32).astype(jnp.bfloat16)

    def exchange(src, dst, slot, pitch, rows, k, axis):
        here = j if axis == "gy" else i
        return pltpu.make_async_remote_copy(
            src_ref=src.at[pl.ds(pl.multiple_of(k * pitch, 8), rows), :],
            dst_ref=dst.at[pl.ds(pl.multiple_of(here * pitch, 8), rows), :],
            send_sem=sent.at[slot],
            recv_sem=came.at[slot],
            device_id={axis: k},
            device_id_type=MESH,
        )

    def whole_round(src, dst, slot, pitch, rows, axis):
        total = pl.ds(0, rows * ((NJ if axis == "gy" else NI) - 1))
        return pltpu.make_async_remote_copy(
            src_ref=src.at[total, :],
            dst_ref=dst.at[total, :],
            send_sem=sent.at[slot],
            recv_sem=came.at[slot],
            device_id={axis: jnext if axis == "gy" else inext},
            device_id_type=MESH,
        )

    def peers(axis):
        if axis == "gy":
            return [lax.rem(j // 4 + a, 4) * 4 + lax.rem(j + b, 4) for a, b in FAR]
        return [lax.rem(i // 2 + a, 4) * 2 + lax.rem(i + b, 2) for a, b in FAR_X]

    def send_all(src, dst, slot, pitch, rows, axis):
        here = j if axis == "gy" else i
        mine = pl.ds(pl.multiple_of(here * pitch, 8), rows)
        for k in peers(axis):
            exchange(src, dst, slot, pitch, rows, k, axis).start()
        dst[mine, :] = src[mine, :]

    def recv_all(src, dst, slot, pitch, rows, axis):
        whole_round(src, dst, slot, pitch, rows, axis).wait_recv()

    def sent_all(src, dst, slot, pitch, rows, axis):
        whole_round(src, dst, slot, pitch, rows, axis).wait_send()

    coup_y = (csy, rcy, 0, 8, 8, "gy")
    coup_x = (csx, rcx, 1, 16, 16, "gx")
    tot_y = (sty, tty, 2, PACK, PACK, "gy")
    ret_y = (oty, rty, 3, PACK, PACK, "gy")
    tot_x = (stx, ttx, 4, STEP_X, PACK_X, "gx")
    ret_x = (otx, rtx, 5, STEP_X, PACK_X, "gx")

    def face(src, dst, slot, part, axis, to):
        return pltpu.make_async_remote_copy(
            src_ref=src.at[part], dst_ref=dst.at[part], send_sem=sent.at[slot], recv_sem=came.at[slot],
            device_id={axis: to}, device_id_type=MESH,
        )

    def both(src, dst, slot):
        return pltpu.make_async_remote_copy(
            src_ref=src, dst_ref=dst, send_sem=sent.at[slot], recv_sem=came.at[slot],
            device_id={"gy": jnext}, device_id_type=MESH,
        )

    edges = [
        face(fse, fre, 6, 0, "gy", jprev),
        face(fse, fre, 6, 1, "gy", jnext),
    ]
    faces = [
        face(fsy, fry, 7, 0, "gy", jprev),
        face(fsy, fry, 7, 1, "gy", jnext),
        face(fsx, frx, 8, 0, "gx", iprev),
        face(fsx, frx, 8, 1, "gx", inext),
    ]
    pairs = [both(fse, fre, 6), both(fsy, fry, 7), both(fsx, frx, 8)]
    def z_lower(q):
        rows = quarters[q]
        scale, weight = zt[rows, :], zw[rows, :]
        for c in range(C):
            zb[c, rows, :] = weight * jnp.dot(
                split(cot[c, rows, :] * scale), tri[0], preferred_element_type=f32
            )

    def z_upper(q):
        rows = quarters[q]
        finish = zo[rows, :]
        for c in range(C):
            zb[c, rows, :] = finish * jnp.dot(split(zb[c, rows, :]), tri[1], preferred_element_type=f32)

    def y_totals(q):
        xs = pl.ds(q * 8, 8)
        heads = [jnp.zeros((8, Z), f32) for _ in range(C)]
        tails = [jnp.zeros((8, Z), f32) for _ in range(C)]
        for y in range(Y):
            a, b = ya[y, xs, :], yb[y, xs, :]
            for c in range(C):
                value = zb[c, pl.ds(q * 8 * Y + y, 8, stride=Y), :]
                heads[c] = heads[c] + a * value
                tails[c] = tails[c] + b * value
                yf[c, y, xs, :] = tails[c]
        at = (q % 2) * 8 * PACK + (q // 2) * C
        for c in range(C):
            sty[pl.ds(at + c, 8, stride=PACK), :] = heads[c]
            sty[pl.ds(at + HALF + c, 8, stride=PACK), :] = tails[c]

    for q in ORDER:
        fields[q].wait()
    loads[2].start()
    loads[3].start()
    z_lower(0)
    for q in range(4):
        if q < 3:
            z_lower(q + 1)
        z_upper(q)
        y_totals(q)

    pl.semaphore_wait(barrier, NI + NJ - 2)
    send_all(*coup_y)
    send_all(*tot_y)
    fse[0] = ec[pl.ds(0, X, stride=Y), :]
    fse[1] = ec[pl.ds(Y - 1, X, stride=Y), :]
    for e in edges:
        e.start()

    loads[2].wait()
    loads[3].wait()
    fsy[0] = upw[1, pl.ds(0, X, stride=Y), :].astype(f32) * cou[1, pl.ds(0, X, stride=Y), :]
    fsy[1] = (1.0 - upw[1, pl.ds(Y - 1, X, stride=Y), :].astype(f32)) * cou[1, pl.ds(Y - 1, X, stride=Y), :]
    fsx[0] = upw[0, 0:Y, :].astype(f32) * cou[0, 0:Y, :] * ec[0:Y, :]
    fsx[1] = (1.0 - upw[0, LINES - Y : LINES, :].astype(f32)) * cou[0, LINES - Y : LINES, :] * ec[LINES - Y : LINES, :]

    for f in faces:
        f.start()

    def reduce_factor(count, pitch, lines, half, couplings, factors):
        def spread(base, t):
            at = base + len(lines) * t
            return jnp.concatenate(
                [jnp.broadcast_to(couplings[pl.ds(at + n, 1), :], (wide, Z)) for n, wide in enumerate(lines)],
                axis=0,
            )

        edge = jnp.zeros((half, Z), f32)
        for m in range(count):
            a1, b1, bn = spread(m * pitch, 0), spread(m * pitch, 1), spread(m * pitch, 2)
            alpha = 1.0 / (1.0 - a1 * edge)
            alpha_a = a1 * alpha
            forward = b1 * alpha
            back = b1 * edge
            factors[0, m, 0:half, :] = alpha
            factors[1, m, 0:half, :] = alpha_a
            factors[2, m, 0:half, :] = forward
            factors[3, m, 0:half, :] = edge
            factors[4, m, 0:half, :] = back * alpha
            factors[5, m, 0:half, :] = b1 + back * alpha_a
            edge = bn + back * forward

    def reduce_solve(count, pitch, half, totals, factors, results):
        gain = jnp.zeros((half, Z), f32)
        for m in range(count):
            head = totals[m * pitch : m * pitch + half, :]
            tail = totals[m * pitch + half : m * pitch + 2 * half, :]
            gl[0, m, 0:half, :] = gain
            gl[1, m, 0:half, :] = factors[0, m, 0:half, :] * head + factors[1, m, 0:half, :] * gain
            gain = tail + factors[4, m, 0:half, :] * head + factors[5, m, 0:half, :] * gain
        later = jnp.zeros((half, Z), f32)
        for m in range(count - 1, -1, -1):
            results[m * pitch + half : m * pitch + 2 * half, :] = later
            later = gl[1, m, 0:half, :] + factors[2, m, 0:half, :] * later
            results[m * pitch : m * pitch + half, :] = gl[0, m, 0:half, :] + factors[3, m, 0:half, :] * later

    low_ok = jnp.where(j > 0, 1.0, 0.0).astype(f32)
    high_ok = jnp.where(j < NJ - 1, 1.0, 0.0).astype(f32)
    lane16 = lax.broadcasted_iota(jnp.int32, (Y, Z), 1)

    def coefficients(x, _):
        rows = pl.ds(pl.multiple_of(x * Y, Y), Y)
        shifted = pl.ds(pl.multiple_of(x * Y + Y, Y), Y)
        padded = pl.ds(pl.multiple_of(x * PAD + 8, 8), Y)
        flux = [cou[d, rows, :] for d in range(3)]
        ahead = [upw[d, rows, :].astype(f32) * flux[d] for d in range(3)]
        behind = [flux[d] - ahead[d] for d in range(3)]
        c0[rows, :] = 1.0 + (behind[0] - ahead[0]) + (behind[1] - ahead[1]) + (behind[2] - ahead[2])
        ax[shifted, :] = ahead[0]
        bx[shifted, :] = behind[0]
        ayp[padded, :] = ahead[1]
        byp[padded, :] = behind[1]
        azn[rows, :] = jnp.where(lane16 < Z - 1, pltpu.roll(ahead[2], Z - 1, 1), 0.0)
        bzp[rows, :] = jnp.where(lane16 > 0, pltpu.roll(behind[2], 1, 1), 0.0)
        return 0

    lax.fori_loop(0, X, coefficients, 0, unroll=8)
    ayh[...] = jnp.zeros_like(ayh)

    for q in range(4):
        xs = pl.ds(q * 8, 8)
        live = [jnp.zeros((8, Z), f32) for _ in range(C)]
        summed = jnp.zeros((8, Z), f32)
        for y in range(Y - 1, -1, -1):
            cells = pl.ds(q * 8 * Y + y, 8, stride=Y)
            weight, finish = yw[y, xs, :], yo[y, xs, :]
            summed = summed + weight
            ynl[cells, :] = finish * (summed * yr[xs, :])
            ynr[cells, :] = finish
            for c in range(C):
                live[c] = live[c] + weight * yf[c, y, xs, :]
                ay[c, cells, :] = live[c] * finish

    recv_all(*coup_y)
    reduce_factor(NJ, 8, (C, C), HALF, rcy, ky)

    recv_all(*tot_y)
    reduce_solve(NJ, PACK, HALF, tty, ky, oty)
    send_all(*ret_y)

    def x_factor():
        rows = pl.ds(0, 32)
        one = jnp.ones((32, Z), f32)

        def up(x, carry):
            theta, delta = carry
            xb[x, rows, :] = theta
            delta = delta + xe[x, rows, :] * theta
            return theta + delta, delta

        theta, _ = lax.fori_loop(0, X, up, (one, one), unroll=8)
        rn = 1.0 / theta
        xr[rows, :] = rn

        def down(step, carry):
            x = X - 1 - step
            phi, delta, after, _ = carry
            cell = xe[x, rows, :]
            a = phi * rn
            b = xb[x, rows, :] * rn
            xa[x, rows, :] = a
            xb[x, rows, :] = b
            xw[x, rows, :] = 1.0 / (b * after)
            xo[x, rows, :] = b * cell
            delta = delta + cell * phi
            return phi + delta, delta, b, a

        _, _, _, first = lax.fori_loop(0, X, down, (one, one, one, one), unroll=8)
        return first, rn

    pairs[0].wait_recv()
    for x in range(X):
        xe[x, 0:Y, :] = ec[x * Y : (x + 1) * Y, :]
        xe[x, 16:24, :] = jnp.broadcast_to(fre[1, x : x + 1, :], (8, Z))
        xe[x, 24:32, :] = jnp.broadcast_to(fre[0, x : x + 1, :], (8, Z))
    first, rn = x_factor()
    for t, part in enumerate((first, rn, xb[X - 1])):
        for r in range(2):
            csx[pl.ds(4 * t + r, 8, stride=16), :] = part[r * 8 : r * 8 + 8]
        csx[pl.ds(4 * t + 2, C, stride=16), :] = part[16 : 16 + C]
        csx[pl.ds(C * 16 + 4 * t + 2, 8 - C, stride=16), :] = part[24 : 32 - C]
        csx[pl.ds(4 * t + 3, 8, stride=16), :] = part[24:32]

    send_all(*coup_x)

    def x_totals(x, carry):
        heads, tails = carry
        rows = pl.ds(pl.multiple_of(x * Y, Y), Y)
        a, b = xa[x, 0:Y, :], xb[x, 0:Y, :]
        left, right = ynl[rows, :], ynr[rows, :]
        ends[0, rows, :] = a * left
        ends[1, rows, :] = a * right
        ends[2, rows, :] = b * left
        ends[3, rows, :] = b * right
        values = [ay[c, rows, :] for c in range(C)]
        return (
            tuple(heads[c] + a * values[c] for c in range(C)),
            tuple(tails[c] + b * values[c] for c in range(C)),
        )

    none = jnp.zeros((Y, Z), f32)
    heads, tails = lax.fori_loop(0, X, x_totals, ((none,) * C, (none,) * C), unroll=8)
    heads, tails = list(heads), list(tails)

    recv_all(*ret_y)

    def end_values(x, c):
        at = lax.rem(x, NJ) * PACK + (x // NJ) * C + c
        return (
            jnp.broadcast_to(rty[pl.ds(at, 1), :], (Y, Z)),
            jnp.broadcast_to(rty[pl.ds(at + HALF, 1), :], (Y, Z)),
        )

    for q in range(4):
        xs = pl.ds(q * 8, 8)
        at = (q % 2) * 8 * PACK + (q // 2) * C
        for c in range(C):
            left = rty[pl.ds(at + c, 8, stride=PACK), :]
            right = rty[pl.ds(at + HALF + c, 8, stride=PACK), :]
            ayh[pl.ds(q * 8 * 16 + c, 8, stride=16), :] = left * fre[1, xs, :]
            ayh[pl.ds(q * 8 * 16 + 8 + c, 8, stride=16), :] = right * fre[0, xs, :]

    def end_totals(x, carry):
        heads, tails, halo_head, halo_tail = carry
        rows = pl.ds(pl.multiple_of(x * Y, Y), Y)
        hl, hr, tl, tr = (ends[n, rows, :] for n in range(4))
        pairs_of = [end_values(x, c) for c in range(C)]
        value = ayh[rows, :]
        return (
            tuple(heads[c] + (hl * left + hr * right) for c, (left, right) in enumerate(pairs_of)),
            tuple(tails[c] + (tl * left + tr * right) for c, (left, right) in enumerate(pairs_of)),
            halo_head + xa[x, 16:32, :] * value,
            halo_tail + xb[x, 16:32, :] * value,
        )

    heads, tails, *edge_pair = lax.fori_loop(
        0, X, end_totals, (tuple(heads), tuple(tails), none, none), unroll=8
    )
    for c in range(C):
        for r in range(2):
            stx[pl.ds(r * C + c, 8, stride=STEP_X), :] = heads[c][r * 8 : r * 8 + 8]
            stx[pl.ds(HALF_X + r * C + c, 8, stride=STEP_X), :] = tails[c][r * 8 : r * 8 + 8]
    for end, part in enumerate(edge_pair):
        at = end * HALF_X + HALF
        stx[pl.ds(at, C, stride=STEP_X), :] = part[0:C]
        stx[pl.ds(C * STEP_X + at, 8 - C, stride=STEP_X), :] = part[8 : 16 - C]
        stx[pl.ds(at + 1, 2 * C - 8, stride=STEP_X), :] = part[16 - C : 8 + C]
    send_all(*tot_x)

    def x_prefix(x, carry):
        tails, halo = carry
        rows = pl.ds(pl.multiple_of(x * Y, Y), Y)
        b = xb[x, 0:Y, :]
        by_left, by_right = ynl[rows, :], ynr[rows, :]
        out = []
        for c in range(C):
            left, right = end_values(x, c)
            tail = tails[c] + b * (ay[c, rows, :] + by_left * left + by_right * right)
            ay[c, rows, :] = tail
            out.append(tail)
        halo = halo + xb[x, 16:32, :] * ayh[rows, :]
        ayh[rows, :] = halo
        return tuple(out), halo

    lax.fori_loop(0, X, x_prefix, ((none,) * C, none), unroll=8)
    recv_all(*coup_x)
    reduce_factor(NI, 16, (C, C, 1, 1), HALF_X, rcx, kx)
    sent_all(*coup_y)
    sent_all(*coup_x)
    sent_all(*tot_y)
    sent_all(*ret_y)
    for pair in pairs:
        pair.wait_send()
    recv_all(*tot_x)
    reduce_solve(NI, STEP_X, HALF_X, ttx, kx, otx)
    send_all(*ret_x)
    pairs[1].wait_recv()
    pairs[2].wait_recv()
    bx[0:Y, :] = frx[1]
    ax[(X + 1) * Y : (X + 2) * Y, :] = frx[0]
    byp[pl.ds(7, X, stride=PAD), :] = fry[1] * low_ok
    ayp[pl.ds(PAD, X, stride=PAD), :] = fry[0] * high_ok

    sent_all(*tot_x)
    recv_all(*ret_x)

    lefts, rights = [], []
    for c in range(C):
        left = jnp.concatenate([rtx[pl.ds(r * C + c, 8, stride=STEP_X), :] for r in range(2)], axis=0)
        right = jnp.concatenate([rtx[pl.ds(HALF_X + r * C + c, 8, stride=STEP_X), :] for r in range(2)], axis=0)
        fb[pl.ds(c * PITCH + 8, Y), :] = left
        fb[pl.ds(c * PITCH + (X + 1) * PAD + 8, Y), :] = right
        lefts.append(left * xr[0:Y, :])
        rights.append(right)
    for end in range(2):
        at = end * HALF_X + HALF
        ext[end, 0:C, :] = rtx[pl.ds(at, C, stride=STEP_X), :]
        ext[end, 8 : 16 - C, :] = rtx[pl.ds(C * STEP_X + at, 8 - C, stride=STEP_X), :]
        ext[end, 16 - C : 8 + C, :] = rtx[pl.ds(at + 1, 2 * C - 8, stride=STEP_X), :]
    left_halo = ext[0] * xr[16:32, :]
    right_halo = ext[1]

    def x_finish(step, carry):
        x = X - 1 - step
        live, halo = carry
        rows = pl.ds(pl.multiple_of(x * Y, Y), Y)
        weight, finish = xw[x, 0:Y, :], xo[x, 0:Y, :]
        out = []
        for c in range(C):
            value = live[c] + weight * (ay[c, rows, :] + lefts[c])
            fb[pl.ds(pl.multiple_of(c * PITCH + (x + 1) * PAD + 8, 8), Y), :] = value * finish
            out.append(value)
        halo = halo + xw[x, 16:32, :] * (ayh[rows, :] + left_halo)
        edge = halo * xo[x, 16:32, :]
        fb[pl.ds((x + 1) * PAD + 7, 8, stride=PITCH), :] = edge[0:8]
        fb[pl.ds((x + 2) * PAD, 8, stride=PITCH), :] = edge[8:16]
        return tuple(out), halo

    lax.fori_loop(0, X, x_finish, (tuple(rights), right_halo), unroll=4)

    sent_all(*ret_x)


def advection(fb, c0, ax, bx, ayp, byp, azn, bzp, out_h, out, sem):
    def advect(x, _):
        rows = pl.ds(pl.multiple_of(x * Y, Y), Y)
        middle = c0[rows, :]
        from_x, to_x = bx[rows, :], ax[pl.ds(pl.multiple_of((x + 2) * Y, Y), Y), :]
        from_y, to_y = byp[pl.ds(x * PAD + 7, Y), :], ayp[pl.ds(x * PAD + 9, Y), :]
        from_z, to_z = bzp[rows, :], azn[rows, :]
        for c in range(C):
            at = c * PITCH + (x + 1) * PAD + 8
            value = fb[pl.ds(pl.multiple_of(at, 8), Y), :]
            result = middle * value
            result += to_x * fb[pl.ds(pl.multiple_of(at + PAD, 8), Y), :]
            result -= from_x * fb[pl.ds(pl.multiple_of(at - PAD, 8), Y), :]
            result += to_y * fb[pl.ds(at + 1, Y), :]
            result -= from_y * fb[pl.ds(at - 1, Y), :]
            result += to_z * pltpu.roll(value, Z - 1, 1)
            result -= from_z * pltpu.roll(value, 1, 1)
            out[c, rows, :] = result
        return 0

    stores = []
    for part in range(4):
        lax.fori_loop(part * 8, part * 8 + 8, advect, 0, unroll=8)
        rows = pl.ds(part * 8 * Y, 8 * Y)
        store = pltpu.make_async_copy(out.at[:, rows, :], out_h.at[:, rows, :], sem.at[part])
        store.start()
        stores.append(store)
    for store in stores:
        store.wait()


def on_device(cotangent, diffusion, phase, courant, upwind):
    def vm(*shape, dtype=f32):
        return pltpu.VMEM(shape, dtype)

    dma = pltpu.SemaphoreType.DMA
    scratch = [
        vm(C, LINES, Z), vm(LINES, Z), vm(LINES, Z, dtype=jnp.int32), vm(3, LINES, Z), vm(3, LINES, Z, dtype=jnp.int32),
        vm(LINES, Z),
        vm(LINES // Z, Z, Z), vm(LINES, Z), vm(LINES, Z), vm(LINES, Z), vm(C, LINES, Z), vm(2, 2 * Z, Z, dtype=jnp.bfloat16),
        vm(Y, X, Z), vm(Y, X, Z), vm(Y, X, Z), vm(Y, X, Z), vm(X, Z), vm(C, Y, X, Z), vm(C, LINES, Z), vm(X * 16, Z), vm(LINES, Z), vm(LINES, Z), vm(4, LINES, Z),
        vm(X, 32, Z), vm(X, 32, Z), vm(X, 32, Z), vm(X, 32, Z), vm(X, 32, Z), vm(32, Z),
        vm(NJ * 8, Z), vm(NI * 16, Z), vm(NJ * 8, Z), vm(NI * 16, Z), vm(6, NJ, 16, Z), vm(6, NI, 16, Z), vm(2, NJ, 16, Z),
        vm(NJ * PACK, Z), vm(NJ * PACK, Z), vm(NJ * PACK, Z), vm(NJ * PACK, Z),
        vm(NI * STEP_X, Z), vm(NI * STEP_X, Z), vm(NI * STEP_X, Z), vm(NI * STEP_X, Z), vm(2, 16, Z),
        vm(2, X, Z), vm(2, X, Z), vm(2, X, Z), vm(2, X, Z), vm(2, Y, Z), vm(2, Y, Z),
        dma((8,)), dma((9,)), dma((9,)),
    ]
    vmem = pl.BlockSpec(memory_space=pltpu.VMEM)
    shapes = [(8 * PITCH, Z), (LINES, Z), (LINES + 2 * Y, Z), (LINES + 2 * Y, Z), (X * PAD + 8, Z), (X * PAD + 8, Z), (LINES, Z), (LINES, Z)]
    parts = pl.pallas_call(
        body,
        out_shape=[pltpu.VMEM(shape, f32) for shape in shapes],
        in_specs=[pl.BlockSpec(memory_space=pltpu.HBM)] * 5,
        out_specs=[vmem] * len(shapes),
        scratch_shapes=scratch,
        compiler_params=pltpu.CompilerParams(
            collective_id=0, has_side_effects=True, vmem_limit_bytes=40 * 1024 * 1024
        ),
    )(
        *(
            pltpu.with_memory_space_constraint(given, pltpu.HBM)
            for given in (
                cotangent.reshape(C, LINES, Z),
                diffusion.reshape(LINES, Z),
                phase.reshape(LINES, Z),
                courant.reshape(3, LINES, Z),
                upwind.reshape(3, LINES, Z),
            )
        )
    )
    out = pl.pallas_call(
        advection,
        out_shape=jax.ShapeDtypeStruct((C, LINES, Z), f32),
        in_specs=[vmem] * len(shapes),
        out_specs=pl.BlockSpec(memory_space=pl.ANY),
        scratch_shapes=[vm(C, LINES, Z), dma((4,))],
        compiler_params=pltpu.CompilerParams(vmem_limit_bytes=8 * 1024 * 1024),
    )(*(pltpu.with_memory_space_constraint(part, pltpu.VMEM) for part in parts))
    return out.reshape(C, X, Y, Z)


def solution(mesh):
    placed = (
        P(None, "gx", "gy", None),
        P("gx", "gy", None),
        P("gx", "gy", None),
        P(None, "gx", "gy", None),
        P(None, "gx", "gy", None),
    )
    return jax.shard_map(
        on_device, mesh=mesh, in_specs=placed, out_specs=P(None, "gx", "gy", None), check_vma=False
    )
```

```python
import functools

import jax
import jax.numpy as jnp
from jax import lax
from jax.experimental import pallas as pl
from jax.experimental.pallas import tpu as pltpu
from jax.sharding import PartitionSpec as P

MESH = pl.DeviceIdType.MESH
C, X, Y, Z = 6, 32, 16, 128
NI, NJ = 8, 16
LINES = X * Y
PAD = 24
PLANES = X + 2
PITCH = PLANES * PAD + 8
HALF = C * 2
PACK = 2 * HALF
HALF_X = HALF + 2
PACK_X = 2 * HALF_X
STEP_X = 32
f32 = jnp.float32
FAR = sorted(((a, b) for a in range(4) for b in range(4) if a or b), key=lambda d: -min(d[0], 4 - d[0]) - min(d[1], 4 - d[1]))
ORDER = (0, 2, 1, 3)
FAR_X = [(2, 1), (2, 0), (3, 1), (1, 1), (3, 0), (1, 0), (0, 1)]


def split(values):
    high = values.astype(jnp.bfloat16)
    low = (values - high.astype(f32)).astype(jnp.bfloat16)
    return jnp.concatenate([high, low], axis=1)


def body(
    cot_h, dif_h, pha_h, cou_h, upw_h,
    fb, c0, ax, bx, ayp, byp, azn, bzp,
    cot, dif, pha, cou, upw, ec,
    et, zt, zw, zo, zb, tri,
    yb, ya, yw, yo, yr, yf, ay, ayh, ynl, ynr, ends,
    xe, xb, xa, xw, xo, xr,
    csy, csx, rcy, rcx, ky, kx, gl,
    sty, tty, oty, rty, stx, ttx, otx, rtx, ext,
    fse, fre, fsy, fry, fsx, frx,
    in_sem,
    sent, came,
):
    i = lax.axis_index("gx")
    j = lax.axis_index("gy")
    inext, iprev = lax.rem(i + 1, NI), lax.rem(i + NI - 1, NI)
    jnext, jprev = lax.rem(j + 1, NJ), lax.rem(j + NJ - 1, NJ)

    loads = [
        pltpu.make_async_copy(dif_h, dif, in_sem.at[0]),
        pltpu.make_async_copy(pha_h, pha, in_sem.at[1]),
        pltpu.make_async_copy(cou_h, cou, in_sem.at[2]),
        pltpu.make_async_copy(upw_h, upw, in_sem.at[3]),
    ]
    quarters = [pl.ds(q * 8 * Y, 8 * Y) for q in range(4)]
    fields = [
        pltpu.make_async_copy(cot_h.at[:, rows, :], cot.at[:, rows, :], in_sem.at[4 + q])
        for q, rows in enumerate(quarters)
    ]
    loads[0].start()
    loads[1].start()
    for q in ORDER:
        fields[q].start()

    barrier = pltpu.get_barrier_semaphore()

    def greet_y(d, _):
        pl.semaphore_signal(barrier, inc=1, device_id=(i, lax.rem(j + d, NJ)), device_id_type=MESH)
        return 0

    def greet_x(d, _):
        pl.semaphore_signal(barrier, inc=1, device_id=(lax.rem(i + d, NI), j), device_id_type=MESH)
        return 0

    lax.fori_loop(1, NJ, greet_y, 0)
    lax.fori_loop(1, NI, greet_x, 0)

    loads[0].wait()
    loads[1].wait()
    ec[...] = 1.0 / (dif[...] * (1.0 + 3.0 * pha[...].astype(f32)))

    for q in range(X // 8):
        xs = pl.ds(q * 8, 8)
        cells = [ec[pl.ds(q * 8 * Y + y, 8, stride=Y), :] for y in range(Y)]
        theta = jnp.ones((8, Z), f32)
        delta = jnp.ones((8, Z), f32)
        for y in range(Y):
            yb[y, xs, :] = theta
            delta = delta + cells[y] * theta
            theta = theta + delta
        rn = 1.0 / theta
        yr[xs, :] = rn
        phi = jnp.ones((8, Z), f32)
        delta = jnp.ones((8, Z), f32)
        after = jnp.ones((8, Z), f32)
        at = (q % 2) * 8 * 8 + q // 2
        for y in range(Y - 1, -1, -1):
            a = phi * rn
            b = yb[y, xs, :] * rn
            ya[y, xs, :] = a
            yb[y, xs, :] = b
            yw[y, xs, :] = 1.0 / (b * after)
            yo[y, xs, :] = b * cells[y]
            if y == Y - 1:
                csy[pl.ds(at + 4, 8, stride=8), :] = b
            if y == 0:
                csy[pl.ds(at, 8, stride=8), :] = a
            after = b
            delta = delta + cells[y] * phi
            phi = phi + delta
        csy[pl.ds(at + 2, 8, stride=8), :] = rn

    seg = lax.broadcasted_iota(jnp.int32, (8, Z), 0)
    span = Z // 8
    tiles = LINES // Z
    for t in range(tiles):
        et[t] = ec[t * Z : (t + 1) * Z, :].T
    ones = jnp.ones((8, Z), f32)
    zeros = jnp.zeros((8, Z), f32)

    def cell(t, step):
        return et[t, pl.ds(step, 8, stride=span), :]

    starts = []
    for t in range(tiles):
        p11, p12, p21, p22 = ones, zeros, zeros, ones
        for step in range(span):
            e = cell(t, step)
            p21 = p21 + e * p11
            p22 = p22 + e * p12
            p11 = p11 + p21
            p12 = p12 + p22
        for shift in (1, 2, 4):
            keep = seg < shift
            q11 = jnp.where(keep, 1.0, pltpu.roll(p11, shift, 0))
            q12 = jnp.where(keep, 0.0, pltpu.roll(p12, shift, 0))
            q21 = jnp.where(keep, 0.0, pltpu.roll(p21, shift, 0))
            q22 = jnp.where(keep, 1.0, pltpu.roll(p22, shift, 0))
            p11, p12, p21, p22 = (
                p11 * q11 + p12 * q21,
                p11 * q12 + p12 * q22,
                p21 * q11 + p22 * q21,
                p21 * q12 + p22 * q22,
            )
        theta = jnp.where(seg < 1, 1.0, pltpu.roll(p11 + p12, 1, 0))
        delta = jnp.where(seg < 1, 1.0, pltpu.roll(p21 + p22, 1, 0))
        starts.append((theta, delta))
    for t in range(tiles):
        theta, delta = starts[t]
        for step in range(span):
            delta = delta + cell(t, step) * theta
            theta = theta + delta
            et[t, pl.ds(step, 8, stride=span), :] = theta
    lane = lax.broadcasted_iota(jnp.int32, (Z, Z), 1)
    for t in range(tiles):
        rows = pl.ds(t * Z, Z)
        theta = et[t].T
        before = jnp.where(lane < 1, 1.0, pltpu.roll(theta, 1, 1))
        zt[rows, :] = before
        zw[rows, :] = 1.0 / (theta * before)
        zo[rows, :] = before * ec[rows, :]

    row = lax.rem(lax.broadcasted_iota(jnp.int32, (2 * Z, Z), 0), Z)
    col = lax.broadcasted_iota(jnp.int32, (2 * Z, Z), 1)
    tri[0] = (row <= col).astype(f32).astype(jnp.bfloat16)
    tri[1] = (row >= col).astype(f32).astype(jnp.bfloat16)

    def exchange(src, dst, slot, pitch, rows, k, axis):
        here = j if axis == "gy" else i
        return pltpu.make_async_remote_copy(
            src_ref=src.at[pl.ds(pl.multiple_of(k * pitch, 8), rows), :],
            dst_ref=dst.at[pl.ds(pl.multiple_of(here * pitch, 8), rows), :],
            send_sem=sent.at[slot],
            recv_sem=came.at[slot],
            device_id={axis: k},
            device_id_type=MESH,
        )

    def whole_round(src, dst, slot, pitch, rows, axis):
        total = pl.ds(0, rows * ((NJ if axis == "gy" else NI) - 1))
        return pltpu.make_async_remote_copy(
            src_ref=src.at[total, :],
            dst_ref=dst.at[total, :],
            send_sem=sent.at[slot],
            recv_sem=came.at[slot],
            device_id={axis: jnext if axis == "gy" else inext},
            device_id_type=MESH,
        )

    def peers(axis):
        if axis == "gy":
            return [lax.rem(j // 4 + a, 4) * 4 + lax.rem(j + b, 4) for a, b in FAR]
        return [lax.rem(i // 2 + a, 4) * 2 + lax.rem(i + b, 2) for a, b in FAR_X]

    def send_all(src, dst, slot, pitch, rows, axis):
        here = j if axis == "gy" else i
        mine = pl.ds(pl.multiple_of(here * pitch, 8), rows)
        for k in peers(axis):
            exchange(src, dst, slot, pitch, rows, k, axis).start()
        dst[mine, :] = src[mine, :]

    def recv_all(src, dst, slot, pitch, rows, axis):
        whole_round(src, dst, slot, pitch, rows, axis).wait_recv()

    def sent_all(src, dst, slot, pitch, rows, axis):
        whole_round(src, dst, slot, pitch, rows, axis).wait_send()

    coup_y = (csy, rcy, 0, 8, 8, "gy")
    coup_x = (csx, rcx, 1, 16, 16, "gx")
    tot_y = (sty, tty, 2, PACK, PACK, "gy")
    ret_y = (oty, rty, 3, PACK, PACK, "gy")
    tot_x = (stx, ttx, 4, STEP_X, PACK_X, "gx")
    ret_x = (otx, rtx, 5, STEP_X, PACK_X, "gx")

    def face(src, dst, slot, part, axis, to):
        return pltpu.make_async_remote_copy(
            src_ref=src.at[part], dst_ref=dst.at[part], send_sem=sent.at[slot], recv_sem=came.at[slot],
            device_id={axis: to}, device_id_type=MESH,
        )

    def both(src, dst, slot):
        return pltpu.make_async_remote_copy(
            src_ref=src, dst_ref=dst, send_sem=sent.at[slot], recv_sem=came.at[slot],
            device_id={"gy": jnext}, device_id_type=MESH,
        )

    edges = [
        face(fse, fre, 6, 0, "gy", jprev),
        face(fse, fre, 6, 1, "gy", jnext),
    ]
    faces = [
        face(fsy, fry, 7, 0, "gy", jprev),
        face(fsy, fry, 7, 1, "gy", jnext),
        face(fsx, frx, 8, 0, "gx", iprev),
        face(fsx, frx, 8, 1, "gx", inext),
    ]
    pairs = [both(fse, fre, 6), both(fsy, fry, 7), both(fsx, frx, 8)]
    def z_lower(q):
        rows = quarters[q]
        scale, weight = zt[rows, :], zw[rows, :]
        for c in range(C):
            zb[c, rows, :] = weight * jnp.dot(
                split(cot[c, rows, :] * scale), tri[0], preferred_element_type=f32
            )

    def z_upper(q):
        rows = quarters[q]
        finish = zo[rows, :]
        for c in range(C):
            zb[c, rows, :] = finish * jnp.dot(split(zb[c, rows, :]), tri[1], preferred_element_type=f32)

    def y_totals(q):
        xs = pl.ds(q * 8, 8)
        heads = [jnp.zeros((8, Z), f32) for _ in range(C)]
        tails = [jnp.zeros((8, Z), f32) for _ in range(C)]
        for y in range(Y):
            a, b = ya[y, xs, :], yb[y, xs, :]
            for c in range(C):
                value = zb[c, pl.ds(q * 8 * Y + y, 8, stride=Y), :]
                heads[c] = heads[c] + a * value
                tails[c] = tails[c] + b * value
                yf[c, y, xs, :] = tails[c]
        at = (q % 2) * 8 * PACK + (q // 2) * C
        for c in range(C):
            sty[pl.ds(at + c, 8, stride=PACK), :] = heads[c]
            sty[pl.ds(at + HALF + c, 8, stride=PACK), :] = tails[c]

    for q in ORDER:
        fields[q].wait()
    loads[2].start()
    loads[3].start()
    z_lower(0)
    for q in range(4):
        if q < 3:
            z_lower(q + 1)
        z_upper(q)
        y_totals(q)

    pl.semaphore_wait(barrier, NI + NJ - 2)
    send_all(*tot_y)
    send_all(*coup_y)
    fse[0] = ec[pl.ds(0, X, stride=Y), :]
    fse[1] = ec[pl.ds(Y - 1, X, stride=Y), :]
    for e in edges:
        e.start()

    loads[2].wait()
    loads[3].wait()
    fsy[0] = upw[1, pl.ds(0, X, stride=Y), :].astype(f32) * cou[1, pl.ds(0, X, stride=Y), :]
    fsy[1] = (1.0 - upw[1, pl.ds(Y - 1, X, stride=Y), :].astype(f32)) * cou[1, pl.ds(Y - 1, X, stride=Y), :]
    fsx[0] = upw[0, 0:Y, :].astype(f32) * cou[0, 0:Y, :] * ec[0:Y, :]
    fsx[1] = (1.0 - upw[0, LINES - Y : LINES, :].astype(f32)) * cou[0, LINES - Y : LINES, :] * ec[LINES - Y : LINES, :]

    for f in faces:
        f.start()

    def reduce_factor(count, pitch, lines, half, couplings, factors):
        def spread(base, t):
            at = base + len(lines) * t
            return jnp.concatenate(
                [jnp.broadcast_to(couplings[pl.ds(at + n, 1), :], (wide, Z)) for n, wide in enumerate(lines)],
                axis=0,
            )

        edge = jnp.zeros((half, Z), f32)
        for m in range(count):
            a1, b1, bn = spread(m * pitch, 0), spread(m * pitch, 1), spread(m * pitch, 2)
            alpha = 1.0 / (1.0 - a1 * edge)
            alpha_a = a1 * alpha
            forward = b1 * alpha
            back = b1 * edge
            factors[0, m, 0:half, :] = alpha
            factors[1, m, 0:half, :] = alpha_a
            factors[2, m, 0:half, :] = forward
            factors[3, m, 0:half, :] = edge
            factors[4, m, 0:half, :] = back * alpha
            factors[5, m, 0:half, :] = b1 + back * alpha_a
            edge = bn + back * forward

    def reduce_solve(count, pitch, half, totals, factors, results):
        gain = jnp.zeros((half, Z), f32)
        for m in range(count):
            head = totals[m * pitch : m * pitch + half, :]
            tail = totals[m * pitch + half : m * pitch + 2 * half, :]
            gl[0, m, 0:half, :] = gain
            gl[1, m, 0:half, :] = factors[0, m, 0:half, :] * head + factors[1, m, 0:half, :] * gain
            gain = tail + factors[4, m, 0:half, :] * head + factors[5, m, 0:half, :] * gain
        later = jnp.zeros((half, Z), f32)
        for m in range(count - 1, -1, -1):
            results[m * pitch + half : m * pitch + 2 * half, :] = later
            later = gl[1, m, 0:half, :] + factors[2, m, 0:half, :] * later
            results[m * pitch : m * pitch + half, :] = gl[0, m, 0:half, :] + factors[3, m, 0:half, :] * later

    low_ok = jnp.where(j > 0, 1.0, 0.0).astype(f32)
    high_ok = jnp.where(j < NJ - 1, 1.0, 0.0).astype(f32)
    lane16 = lax.broadcasted_iota(jnp.int32, (Y, Z), 1)

    def coefficients(x, _):
        rows = pl.ds(pl.multiple_of(x * Y, Y), Y)
        shifted = pl.ds(pl.multiple_of(x * Y + Y, Y), Y)
        padded = pl.ds(pl.multiple_of(x * PAD + 8, 8), Y)
        flux = [cou[d, rows, :] for d in range(3)]
        ahead = [upw[d, rows, :].astype(f32) * flux[d] for d in range(3)]
        behind = [flux[d] - ahead[d] for d in range(3)]
        c0[rows, :] = 1.0 + (behind[0] - ahead[0]) + (behind[1] - ahead[1]) + (behind[2] - ahead[2])
        ax[shifted, :] = ahead[0]
        bx[shifted, :] = behind[0]
        ayp[padded, :] = ahead[1]
        byp[padded, :] = behind[1]
        azn[rows, :] = jnp.where(lane16 < Z - 1, pltpu.roll(ahead[2], Z - 1, 1), 0.0)
        bzp[rows, :] = jnp.where(lane16 > 0, pltpu.roll(behind[2], 1, 1), 0.0)
        return 0

    lax.fori_loop(0, X, coefficients, 0, unroll=8)
    ayh[...] = jnp.zeros_like(ayh)

    for q in range(4):
        xs = pl.ds(q * 8, 8)
        live = [jnp.zeros((8, Z), f32) for _ in range(C)]
        summed = jnp.zeros((8, Z), f32)
        for y in range(Y - 1, -1, -1):
            cells = pl.ds(q * 8 * Y + y, 8, stride=Y)
            weight, finish = yw[y, xs, :], yo[y, xs, :]
            summed = summed + weight
            ynl[cells, :] = finish * (summed * yr[xs, :])
            ynr[cells, :] = finish
            for c in range(C):
                live[c] = live[c] + weight * yf[c, y, xs, :]
                ay[c, cells, :] = live[c] * finish

    recv_all(*coup_y)
    reduce_factor(NJ, 8, (C, C), HALF, rcy, ky)

    recv_all(*tot_y)
    reduce_solve(NJ, PACK, HALF, tty, ky, oty)
    send_all(*ret_y)

    def x_factor():
        rows = pl.ds(0, 32)
        one = jnp.ones((32, Z), f32)

        def up(x, carry):
            theta, delta = carry
            xb[x, rows, :] = theta
            delta = delta + xe[x, rows, :] * theta
            return theta + delta, delta

        theta, _ = lax.fori_loop(0, X, up, (one, one), unroll=8)
        rn = 1.0 / theta
        xr[rows, :] = rn

        def down(step, carry):
            x = X - 1 - step
            phi, delta, after, _ = carry
            cell = xe[x, rows, :]
            a = phi * rn
            b = xb[x, rows, :] * rn
            xa[x, rows, :] = a
            xb[x, rows, :] = b
            xw[x, rows, :] = 1.0 / (b * after)
            xo[x, rows, :] = b * cell
            delta = delta + cell * phi
            return phi + delta, delta, b, a

        _, _, _, first = lax.fori_loop(0, X, down, (one, one, one, one), unroll=8)
        return first, rn

    pairs[0].wait_recv()
    for x in range(X):
        xe[x, 0:Y, :] = ec[x * Y : (x + 1) * Y, :]
        xe[x, 16:24, :] = jnp.broadcast_to(fre[1, x : x + 1, :], (8, Z))
        xe[x, 24:32, :] = jnp.broadcast_to(fre[0, x : x + 1, :], (8, Z))
    first, rn = x_factor()
    for t, part in enumerate((first, rn, xb[X - 1])):
        for r in range(2):
            csx[pl.ds(4 * t + r, 8, stride=16), :] = part[r * 8 : r * 8 + 8]
        csx[pl.ds(4 * t + 2, C, stride=16), :] = part[16 : 16 + C]
        csx[pl.ds(C * 16 + 4 * t + 2, 8 - C, stride=16), :] = part[24 : 32 - C]
        csx[pl.ds(4 * t + 3, 8, stride=16), :] = part[24:32]

    send_all(*coup_x)

    def x_totals(x, carry):
        heads, tails = carry
        rows = pl.ds(pl.multiple_of(x * Y, Y), Y)
        a, b = xa[x, 0:Y, :], xb[x, 0:Y, :]
        left, right = ynl[rows, :], ynr[rows, :]
        ends[0, rows, :] = a * left
        ends[1, rows, :] = a * right
        ends[2, rows, :] = b * left
        ends[3, rows, :] = b * right
        values = [ay[c, rows, :] for c in range(C)]
        return (
            tuple(heads[c] + a * values[c] for c in range(C)),
            tuple(tails[c] + b * values[c] for c in range(C)),
        )

    none = jnp.zeros((Y, Z), f32)
    heads, tails = lax.fori_loop(0, X, x_totals, ((none,) * C, (none,) * C), unroll=8)
    heads, tails = list(heads), list(tails)

    recv_all(*ret_y)

    def end_values(x, c):
        at = lax.rem(x, NJ) * PACK + (x // NJ) * C + c
        return (
            jnp.broadcast_to(rty[pl.ds(at, 1), :], (Y, Z)),
            jnp.broadcast_to(rty[pl.ds(at + HALF, 1), :], (Y, Z)),
        )

    for q in range(4):
        xs = pl.ds(q * 8, 8)
        at = (q % 2) * 8 * PACK + (q // 2) * C
        for c in range(C):
            left = rty[pl.ds(at + c, 8, stride=PACK), :]
            right = rty[pl.ds(at + HALF + c, 8, stride=PACK), :]
            ayh[pl.ds(q * 8 * 16 + c, 8, stride=16), :] = left * fre[1, xs, :]
            ayh[pl.ds(q * 8 * 16 + 8 + c, 8, stride=16), :] = right * fre[0, xs, :]

    def end_totals(x, carry):
        heads, tails, halo_head, halo_tail = carry
        rows = pl.ds(pl.multiple_of(x * Y, Y), Y)
        hl, hr, tl, tr = (ends[n, rows, :] for n in range(4))
        pairs_of = [end_values(x, c) for c in range(C)]
        value = ayh[rows, :]
        return (
            tuple(heads[c] + (hl * left + hr * right) for c, (left, right) in enumerate(pairs_of)),
            tuple(tails[c] + (tl * left + tr * right) for c, (left, right) in enumerate(pairs_of)),
            halo_head + xa[x, 16:32, :] * value,
            halo_tail + xb[x, 16:32, :] * value,
        )

    heads, tails, *edge_pair = lax.fori_loop(
        0, X, end_totals, (tuple(heads), tuple(tails), none, none), unroll=32
    )
    for c in range(C):
        for r in range(2):
            stx[pl.ds(r * C + c, 8, stride=STEP_X), :] = heads[c][r * 8 : r * 8 + 8]
            stx[pl.ds(HALF_X + r * C + c, 8, stride=STEP_X), :] = tails[c][r * 8 : r * 8 + 8]
    for end, part in enumerate(edge_pair):
        at = end * HALF_X + HALF
        stx[pl.ds(at, C, stride=STEP_X), :] = part[0:C]
        stx[pl.ds(C * STEP_X + at, 8 - C, stride=STEP_X), :] = part[8 : 16 - C]
        stx[pl.ds(at + 1, 2 * C - 8, stride=STEP_X), :] = part[16 - C : 8 + C]
    send_all(*tot_x)

    def x_prefix(x, carry):
        tails, halo = carry
        rows = pl.ds(pl.multiple_of(x * Y, Y), Y)
        b = xb[x, 0:Y, :]
        by_left, by_right = ynl[rows, :], ynr[rows, :]
        out = []
        for c in range(C):
            left, right = end_values(x, c)
            tail = tails[c] + b * (ay[c, rows, :] + by_left * left + by_right * right)
            ay[c, rows, :] = tail
            out.append(tail)
        halo = halo + xb[x, 16:32, :] * ayh[rows, :]
        ayh[rows, :] = halo
        return tuple(out), halo

    lax.fori_loop(0, X, x_prefix, ((none,) * C, none), unroll=8)
    recv_all(*coup_x)
    reduce_factor(NI, 16, (C, C, 1, 1), HALF_X, rcx, kx)
    sent_all(*coup_y)
    sent_all(*coup_x)
    sent_all(*tot_y)
    sent_all(*ret_y)
    for pair in pairs:
        pair.wait_send()
    recv_all(*tot_x)
    reduce_solve(NI, STEP_X, HALF_X, ttx, kx, otx)
    send_all(*ret_x)
    pairs[1].wait_recv()
    pairs[2].wait_recv()
    bx[0:Y, :] = frx[1]
    ax[(X + 1) * Y : (X + 2) * Y, :] = frx[0]
    byp[pl.ds(7, X, stride=PAD), :] = fry[1] * low_ok
    ayp[pl.ds(PAD, X, stride=PAD), :] = fry[0] * high_ok

    sent_all(*tot_x)
    recv_all(*ret_x)

    lefts, rights = [], []
    for c in range(C):
        left = jnp.concatenate([rtx[pl.ds(r * C + c, 8, stride=STEP_X), :] for r in range(2)], axis=0)
        right = jnp.concatenate([rtx[pl.ds(HALF_X + r * C + c, 8, stride=STEP_X), :] for r in range(2)], axis=0)
        fb[pl.ds(c * PITCH + 8, Y), :] = left
        fb[pl.ds(c * PITCH + (X + 1) * PAD + 8, Y), :] = right
        lefts.append(left * xr[0:Y, :])
        rights.append(right)
    for end in range(2):
        at = end * HALF_X + HALF
        ext[end, 0:C, :] = rtx[pl.ds(at, C, stride=STEP_X), :]
        ext[end, 8 : 16 - C, :] = rtx[pl.ds(C * STEP_X + at, 8 - C, stride=STEP_X), :]
        ext[end, 16 - C : 8 + C, :] = rtx[pl.ds(at + 1, 2 * C - 8, stride=STEP_X), :]
    left_halo = ext[0] * xr[16:32, :]
    right_halo = ext[1]

    def x_finish(step, carry):
        x = X - 1 - step
        live, halo = carry
        rows = pl.ds(pl.multiple_of(x * Y, Y), Y)
        weight, finish = xw[x, 0:Y, :], xo[x, 0:Y, :]
        out = []
        for c in range(C):
            value = live[c] + weight * (ay[c, rows, :] + lefts[c])
            fb[pl.ds(pl.multiple_of(c * PITCH + (x + 1) * PAD + 8, 8), Y), :] = value * finish
            out.append(value)
        halo = halo + xw[x, 16:32, :] * (ayh[rows, :] + left_halo)
        edge = halo * xo[x, 16:32, :]
        fb[pl.ds((x + 1) * PAD + 7, 8, stride=PITCH), :] = edge[0:8]
        fb[pl.ds((x + 2) * PAD, 8, stride=PITCH), :] = edge[8:16]
        return tuple(out), halo

    lax.fori_loop(0, X, x_finish, (tuple(rights), right_halo), unroll=8)

    sent_all(*ret_x)


def advection(fb, c0, ax, bx, ayp, byp, azn, bzp, out_h, out, sem):
    def advect(x, _):
        rows = pl.ds(pl.multiple_of(x * Y, Y), Y)
        middle = c0[rows, :]
        from_x, to_x = bx[rows, :], ax[pl.ds(pl.multiple_of((x + 2) * Y, Y), Y), :]
        from_y, to_y = byp[pl.ds(x * PAD + 7, Y), :], ayp[pl.ds(x * PAD + 9, Y), :]
        from_z, to_z = bzp[rows, :], azn[rows, :]
        for c in range(C):
            at = c * PITCH + (x + 1) * PAD + 8
            value = fb[pl.ds(pl.multiple_of(at, 8), Y), :]
            result = middle * value
            result += to_x * fb[pl.ds(pl.multiple_of(at + PAD, 8), Y), :]
            result -= from_x * fb[pl.ds(pl.multiple_of(at - PAD, 8), Y), :]
            result += to_y * fb[pl.ds(at + 1, Y), :]
            result -= from_y * fb[pl.ds(at - 1, Y), :]
            result += to_z * pltpu.roll(value, Z - 1, 1)
            result -= from_z * pltpu.roll(value, 1, 1)
            out[c, rows, :] = result
        return 0

    stores = []
    for part in range(4):
        lax.fori_loop(part * 8, part * 8 + 8, advect, 0, unroll=8)
        rows = pl.ds(part * 8 * Y, 8 * Y)
        store = pltpu.make_async_copy(out.at[:, rows, :], out_h.at[:, rows, :], sem.at[part])
        store.start()
        stores.append(store)
    for store in stores:
        store.wait()


def on_device(cotangent, diffusion, phase, courant, upwind):
    def vm(*shape, dtype=f32):
        return pltpu.VMEM(shape, dtype)

    dma = pltpu.SemaphoreType.DMA
    scratch = [
        vm(C, LINES, Z), vm(LINES, Z), vm(LINES, Z, dtype=jnp.int32), vm(3, LINES, Z), vm(3, LINES, Z, dtype=jnp.int32),
        vm(LINES, Z),
        vm(LINES // Z, Z, Z), vm(LINES, Z), vm(LINES, Z), vm(LINES, Z), vm(C, LINES, Z), vm(2, 2 * Z, Z, dtype=jnp.bfloat16),
        vm(Y, X, Z), vm(Y, X, Z), vm(Y, X, Z), vm(Y, X, Z), vm(X, Z), vm(C, Y, X, Z), vm(C, LINES, Z), vm(X * 16, Z), vm(LINES, Z), vm(LINES, Z), vm(4, LINES, Z),
        vm(X, 32, Z), vm(X, 32, Z), vm(X, 32, Z), vm(X, 32, Z), vm(X, 32, Z), vm(32, Z),
        vm(NJ * 8, Z), vm(NI * 16, Z), vm(NJ * 8, Z), vm(NI * 16, Z), vm(6, NJ, 16, Z), vm(6, NI, 16, Z), vm(2, NJ, 16, Z),
        vm(NJ * PACK, Z), vm(NJ * PACK, Z), vm(NJ * PACK, Z), vm(NJ * PACK, Z),
        vm(NI * STEP_X, Z), vm(NI * STEP_X, Z), vm(NI * STEP_X, Z), vm(NI * STEP_X, Z), vm(2, 16, Z),
        vm(2, X, Z), vm(2, X, Z), vm(2, X, Z), vm(2, X, Z), vm(2, Y, Z), vm(2, Y, Z),
        dma((8,)), dma((9,)), dma((9,)),
    ]
    vmem = pl.BlockSpec(memory_space=pltpu.VMEM)
    shapes = [(8 * PITCH, Z), (LINES, Z), (LINES + 2 * Y, Z), (LINES + 2 * Y, Z), (X * PAD + 8, Z), (X * PAD + 8, Z), (LINES, Z), (LINES, Z)]
    parts = pl.pallas_call(
        body,
        out_shape=[pltpu.VMEM(shape, f32) for shape in shapes],
        in_specs=[pl.BlockSpec(memory_space=pltpu.HBM)] * 5,
        out_specs=[vmem] * len(shapes),
        scratch_shapes=scratch,
        compiler_params=pltpu.CompilerParams(
            collective_id=0, has_side_effects=True, vmem_limit_bytes=40 * 1024 * 1024
        ),
    )(
        *(
            pltpu.with_memory_space_constraint(given, pltpu.HBM)
            for given in (
                cotangent.reshape(C, LINES, Z),
                diffusion.reshape(LINES, Z),
                phase.reshape(LINES, Z),
                courant.reshape(3, LINES, Z),
                upwind.reshape(3, LINES, Z),
            )
        )
    )
    out = pl.pallas_call(
        advection,
        out_shape=jax.ShapeDtypeStruct((C, LINES, Z), f32),
        in_specs=[vmem] * len(shapes),
        out_specs=pl.BlockSpec(memory_space=pl.ANY),
        scratch_shapes=[vm(C, LINES, Z), dma((4,))],
        compiler_params=pltpu.CompilerParams(vmem_limit_bytes=8 * 1024 * 1024),
    )(*(pltpu.with_memory_space_constraint(part, pltpu.VMEM) for part in parts))
    return out.reshape(C, X, Y, Z)


def solution(mesh):
    placed = (
        P(None, "gx", "gy", None),
        P("gx", "gy", None),
        P("gx", "gy", None),
        P(None, "gx", "gy", None),
        P(None, "gx", "gy", None),
    )
    return jax.shard_map(
        on_device, mesh=mesh, in_specs=placed, out_specs=P(None, "gx", "gy", None), check_vma=False
    )
```
